32 devices in a mesh: grp: 2 (over y), row: 2 (over x), col: 4 (over z), dep: 2 (over core).
Axes of the slice: x: 2, y: 2, z: 4, core: 2. Of those that a mesh axis runs over, the one named last changes fastest.
Arguments:
- left_blocks: bfloat16 [4, 4, 2, 64, 128, 128], P(('grp', 'row'), 'col', 'dep'), parts along dimension 0
- right_blocks: bfloat16 [4, 4, 2, 56, 128, 128], P(('grp', 'row'), 'col', 'dep'), parts along dimension 0
- triples: int32 [4, 4, 2, 7, 3, 64], P(('grp', 'row'), 'col', 'dep'), parts along dimension 0, may hold values from 0 to 224, as said below
Outputs:
- squared: bfloat16 [4, 4, 2, 112, 128, 128], P(('grp', 'row'), 'col', 'dep'), parts along dimension 0
The draws below stay inside these ranges and needn't reach their ends.
There are 2 independent parts, one for each index of `grp`. The reference program is written for one: setup_inputs(seed, part) draws one part's arguments, and reference() takes and returns one part's arrays. A program takes and returns all parts, laid end to end along the dimension named above; each array names one. Nothing has to cross between parts.
Inputs may be any that keep to these rules, and one draw needn't show every extreme that they name: `triples`: index 0 names a slot of the left panel, index 1 a slot of the right panels laid end to end, index 2 a slot of the cell's result blocks over all layers, or 224 for an unused entry (then indices 0 and 1 are 0). The lists are exactly the products X(i, k) X(k, j) of one matrix X with 7 blocks in every block row, each counted once over all layers and steps; left and right slots that name the same block hold equal values.
All inputs are finite; a program needn't handle non-finite values.
Results may differ from the reference program's by a relative error of at most 0.001.
Values may be sent and summed in bfloat16 or wider, within the bound.
No kernel may reach another device: no remote copies, remote signals or barrier semaphores. Data moves between devices by JAX's collectives and lax.ppermute only.
A program may use at most 128 MiB of HBM per device.

```python
import jax
import jax.numpy as jnp
from jax import lax

BS = 128
BAND = 7
HALF = 3
NBQ = 32
NB = 128
KQ = 16
KR = 8
SLOT_A = 64
SLOT_B = 56
SLOT_OUT = 224
SLOT_C = 112
N_ROW = 2
N_COL = 4
N_DEP = 2


def slot_ranks(key):
    left_key, right_key, out_key = jax.random.split(key, 3)

    def ranks(sub_key, count, width):
        scores = jax.random.randint(sub_key, (count, width), 0, 1 << 20) * width + jnp.arange(width, dtype=jnp.int32)[None, :]
        order = jnp.argsort(scores, axis=1).astype(jnp.int32)
        return jnp.argsort(order, axis=1).astype(jnp.int32)
    rank_left = ranks(left_key, N_COL * N_DEP, KQ).reshape(N_COL, N_DEP, KQ)
    rank_right = ranks(right_key, N_COL * N_DEP, KQ).reshape(N_COL, N_DEP, KQ)
    rank_out = ranks(out_key, N_COL, NBQ)
    return (rank_left, rank_right, rank_out)


def block_values(key, idents, spread):
    scale = (1.0 * BAND * BS) ** (-0.25)

    def one_block(ident):
        block_key = jax.random.fold_in(key, ident)
        normal_key = jax.random.fold_in(block_key, 0)
        size_key = jax.random.fold_in(block_key, 2)
        normal_part = jax.random.normal(normal_key, (BS, BS), jnp.float32)
        factor = jnp.exp(spread * jax.random.uniform(size_key, (), jnp.float32, -1.0, 1.0))
        return scale * factor * normal_part
    return jax.vmap(one_block)(idents)


def left_layout(order_left, row_index, middle_res, layer_index, slot_index):
    hit_index = slot_index // KQ
    position = slot_index % KQ
    coarse_local = order_left[middle_res, layer_index, position]
    middle = N_COL * (layer_index * KQ + coarse_local) + middle_res
    first_offset = -HALF + (row_index - middle_res + HALF) % N_ROW
    row_offset = first_offset + hit_index * N_ROW
    live = row_offset <= HALF
    return (coarse_local, middle, row_offset, live)


def draw_left_blocks(key, part):
    rank_left, rank_right, rank_out = slot_ranks(key)
    order_left = jnp.argsort(rank_left, axis=2).astype(jnp.int32)
    spread = 0.0
    value_key = jax.random.fold_in(key, 11)
    row_index = jnp.arange(N_ROW, dtype=jnp.int32)[:, None, None, None]
    middle_res = jnp.arange(N_COL, dtype=jnp.int32)[None, :, None, None]
    layer_index = jnp.arange(N_DEP, dtype=jnp.int32)[None, None, :, None]
    slot_index = jnp.arange(SLOT_A, dtype=jnp.int32)[None, None, None, :]
    coarse_local, middle, row_offset, live = left_layout(order_left, row_index, middle_res, layer_index, slot_index)
    block_row = (middle + row_offset) % NB
    idents = block_row * BAND + jnp.clip(HALF - row_offset, 0, BAND - 1)
    idents = jnp.broadcast_to(idents, (N_ROW, N_COL, N_DEP, SLOT_A)).reshape(-1)
    keep = jnp.broadcast_to(live, (N_ROW, N_COL, N_DEP, SLOT_A)).reshape(-1)
    values = block_values(value_key, idents, spread)
    values = jnp.where(keep[:, None, None], values, 0.0)
    return values.reshape(N_ROW, N_COL, N_DEP, SLOT_A, BS, BS).astype(jnp.bfloat16)


def draw_right_blocks(key, part):
    rank_left, rank_right, rank_out = slot_ranks(key)
    order_right = jnp.argsort(rank_right, axis=2).astype(jnp.int32)
    spread = 0.0
    value_key = jax.random.fold_in(key, 11)
    row_index = jnp.arange(N_ROW, dtype=jnp.int32)[:, None, None, None]
    col_index = jnp.arange(N_COL, dtype=jnp.int32)[None, :, None, None]
    layer_index = jnp.arange(N_DEP, dtype=jnp.int32)[None, None, :, None]
    slot_index = jnp.arange(SLOT_B, dtype=jnp.int32)[None, None, None, :]
    step_index = slot_index // KR
    position = row_index * KR + slot_index % KR
    coarse_local = order_right[col_index, layer_index, position]
    step_offset = step_index - HALF
    middle = N_COL * (layer_index * KQ + coarse_local) + (col_index + step_offset + N_COL) % N_COL
    idents = middle * BAND + (HALF - step_offset)
    idents = jnp.broadcast_to(idents, (N_ROW, N_COL, N_DEP, SLOT_B)).reshape(-1)
    values = block_values(value_key, idents, spread)
    return values.reshape(N_ROW, N_COL, N_DEP, SLOT_B, BS, BS).astype(jnp.bfloat16)


def draw_triples(key, part):
    rank_left, rank_right, rank_out = slot_ranks(key)
    order_left = jnp.argsort(rank_left, axis=2).astype(jnp.int32)
    row_index = jnp.arange(N_ROW, dtype=jnp.int32)[:, None, None, None, None]
    col_index = jnp.arange(N_COL, dtype=jnp.int32)[None, :, None, None, None]
    layer_index = jnp.arange(N_DEP, dtype=jnp.int32)[None, None, :, None, None]
    step_index = jnp.arange(BAND, dtype=jnp.int32)[None, None, None, :, None]
    slot_index = jnp.arange(SLOT_A, dtype=jnp.int32)[None, None, None, None, :]
    step_offset = step_index - HALF
    middle_res = (col_index + step_offset + N_COL) % N_COL
    coarse_local, middle, row_offset, live = left_layout(order_left, row_index, middle_res, layer_index, slot_index)
    position = rank_right[col_index, layer_index, coarse_local]
    second = position // KR * SLOT_B + step_index * KR + position % KR
    block_col = (middle - step_offset + NB) % NB
    coarse_col = block_col // N_COL
    result_offset = row_offset + step_offset
    first_result = -2 * HALF + (row_index - col_index + 2 * HALF) % N_ROW
    result_hit = (result_offset - first_result) // N_ROW
    third = result_hit * NBQ + rank_out[col_index, coarse_col]
    shape = (N_ROW, N_COL, N_DEP, BAND, SLOT_A)
    live_all = jnp.broadcast_to(live, shape)
    first_index = jnp.where(live_all, jnp.broadcast_to(slot_index, shape), 0)
    second_index = jnp.where(live_all, jnp.broadcast_to(second, shape), 0)
    third_index = jnp.where(live_all, jnp.broadcast_to(third, shape), SLOT_OUT)
    lists = jnp.stack([first_index, second_index, third_index], axis=4)
    return lists.astype(jnp.int32)


def setup_inputs(seed: int = 0, part: int = 0) -> dict:
    key_list = jax.random.split(jax.random.key(seed), 4)
    own_keys = jax.random.split(jax.random.fold_in(key_list[3], part), 4)
    left_blocks = draw_left_blocks(jax.random.fold_in(jax.random.fold_in(key_list[3], part), 71), part)
    right_blocks = draw_right_blocks(jax.random.fold_in(jax.random.fold_in(key_list[3], part), 71), part)
    triples = draw_triples(jax.random.fold_in(jax.random.fold_in(key_list[3], part), 71), part)
    return dict(left_blocks=left_blocks, right_blocks=right_blocks, triples=triples)


def reference(left_blocks, right_blocks, triples):
    def one_cell(cell_index):
        row_index = (cell_index // N_COL).astype(jnp.int32)
        col_index = (cell_index % N_COL).astype(jnp.int32)
        accumulated = jnp.zeros((SLOT_OUT + 1, BS, BS), jnp.float32)
        for layer_index in range(N_DEP):
            gathered = right_blocks[:, col_index, layer_index].reshape(N_ROW * SLOT_B, BS, BS)
            for step_index in range(BAND):
                source = ((col_index + step_index - HALF + N_COL) % N_COL).astype(jnp.int32)
                left_panel = left_blocks[row_index, source, layer_index]
                step_list = triples[row_index, col_index, layer_index, step_index]
                left_rows = jnp.take(left_panel, step_list[0], axis=0).astype(jnp.float32)
                right_rows = jnp.take(gathered, step_list[1], axis=0).astype(jnp.float32)
                products = jnp.einsum("tij,tjk->tik", left_rows, right_rows)
                accumulated = accumulated + jax.ops.segment_sum(products, step_list[2], num_segments=SLOT_OUT + 1)
        rounded = accumulated[:SLOT_OUT].astype(jnp.bfloat16)
        return rounded.reshape(N_DEP, SLOT_C, BS, BS)

    cells = lax.map(one_cell, jnp.arange(N_ROW * N_COL, dtype=jnp.int32))
    return cells.reshape(N_ROW, N_COL, N_DEP, SLOT_C, BS, BS)
```

```python
import functools

import jax
import jax.numpy as jnp
from jax import lax
from jax.experimental import pallas as pl
from jax.experimental.pallas import tpu as pltpu
from jax.sharding import PartitionSpec as P

NBQ = 32
UNROLL = 4


def stage_kernel(panels, first, last, *refs):
    lists, todo = refs[0], refs[-1]
    lefts = refs[1 : 1 + 2 * panels]
    rights = refs[1 + 2 * panels : 3 + 2 * panels]
    work = refs[-2]
    half = work.shape[0] - 1
    if first:
        work[...] = jnp.zeros_like(work)
    else:
        work[...] = refs[3 + 2 * panels][...]
    for panel in range(panels):
        for layer in range(2):
            row = 2 * panel + layer
            left, right = lefts[row], rights[layer]

            def keep(index, count):
                entry = lists[row, index]
                todo[count] = entry
                return count + (entry >= 0).astype(jnp.int32)

            count = lax.fori_loop(0, lists.shape[1], keep, jnp.int32(0))
            for extra in range(UNROLL - 1):
                todo[count + extra] = jnp.int32(half << 20)

            def several(group, carry):
                for lane in range(UNROLL):
                    entry = todo[group * UNROLL + lane]
                    product = jnp.dot(
                        left[entry & 1023], right[(entry >> 10) & 1023], preferred_element_type=jnp.float32
                    )
                    work[entry >> 20] += product
                return carry

            lax.fori_loop(0, (count + UNROLL - 1) // UNROLL, several, jnp.int32(0))
    if last:
        out = refs[-3]
        out[...] = work[:half].astype(out.dtype)


def stage(lists, lefts, rights, given, half, last):
    width = rights[0].shape[1]
    first = given is None
    operands = [lists, *lefts, *rights] + ([] if first else [given])
    vmem = pl.BlockSpec(memory_space=pltpu.VMEM)
    if last:
        out_shape = jax.ShapeDtypeStruct((half, width, width), jnp.bfloat16)
        scratch = [pltpu.VMEM((half + 1, width, width), jnp.float32)]
    else:
        out_shape = jax.ShapeDtypeStruct((half + 1, width, width), jnp.float32)
        scratch = []
    return pl.pallas_call(
        functools.partial(stage_kernel, len(lefts) // 2, first, last),
        out_shape=out_shape,
        in_specs=[pl.BlockSpec(memory_space=pltpu.SMEM)] + [vmem] * (len(operands) - 1),
        out_specs=vmem,
        scratch_shapes=scratch + [pltpu.SMEM((lists.shape[1] + UNROLL,), jnp.int32)],
        compiler_params=pltpu.CompilerParams(vmem_limit_bytes=56 << 20),
        cost_estimate=pl.CostEstimate(
            flops=lists.size * width**3, bytes_accessed=32 << 20, transcendentals=0
        ),
    )(*operands)


def local(left_blocks, right_blocks, triples):
    own = left_blocks[0, 0, 0]
    right_own = right_blocks[0, 0, 0]
    step_lists = triples[0, 0, 0]
    slots = own.shape[0]
    step_count = step_lists.shape[0]
    centre = step_count // 2
    columns = lax.axis_size("col")
    place = lax.axis_index("col")
    layer = lax.axis_index("dep")
    cyclic = columns >= step_count
    reach = centre if cyclic else columns - 1

    swap = [(0, 1), (1, 0)]
    row_count = lax.axis_size("row")
    half = (2 * step_count - 2 + row_count) // row_count * NBQ // 2
    other_lists = lax.ppermute(step_lists, "dep", swap)
    both = jnp.stack([step_lists, other_lists])
    result = both[:, :, 2] - layer * half
    wanted = (result >= 0) & (result < half)
    packed = jnp.where(wanted, both[:, :, 0] | (both[:, :, 1] << 10) | (result << 20), -1)

    right_here = lax.all_gather(right_own, "row", axis=0, tiled=True)
    right_there = lax.ppermute(right_here, "dep", swap)
    rights = [right_here, right_there]

    steps_of = [[s for s in range(step_count) if (s - centre - q) % columns == 0] for q in range(columns)]
    most = max(len(steps) for steps in steps_of)
    nothing = jnp.full((2, slots), -1, jnp.int32)

    def lists_of(offset):
        steps = steps_of[offset % columns]
        rows = [packed[:, s] for s in steps] + [nothing] * (most - len(steps))
        return jnp.concatenate(rows, axis=1)

    def doubled(panel):
        return [panel, lax.ppermute(panel, "dep", swap)]

    def forward(panel, round_index):
        if cyclic:
            return lax.ppermute(panel, "col", [(i, (i + 1) % columns) for i in range(columns)])
        return lax.ppermute(panel, "col", [(i, i + 1) for i in range(round_index - 1, columns - 1)])

    def backward(panel, round_index):
        if cyclic:
            return lax.ppermute(panel, "col", [(i, (i - 1) % columns) for i in range(columns)])
        return lax.ppermute(panel, "col", [(i + 1, i) for i in range(columns - round_index)])

    rising, falling = own, own
    total = None
    lefts, lists = doubled(own), [lists_of(0)]
    for distance in range(1, reach + 1):
        rising = forward(rising, distance)
        falling = backward(falling, distance)
        from_left, from_right = lists_of(-distance), lists_of(distance)
        if not cyclic:
            from_left = jnp.where(place >= distance, from_left, -1)
            from_right = jnp.where(place + distance < columns, from_right, -1)
        if not cyclic and 2 * distance >= columns:
            lefts += doubled(jnp.where(place >= distance, rising, falling))
            lists += [jnp.where(place >= distance, from_left, from_right)]
        else:
            lefts += doubled(rising) + doubled(falling)
            lists += [from_left, from_right]
        last = distance == reach
        total = stage(jnp.concatenate(lists), lefts, rights, total, half, last)
        lefts, lists = [], []
    return total[None, None, None]


def solution(mesh):
    return jax.shard_map(
        local,
        mesh=mesh,
        in_specs=(
            P(("grp", "row"), "col", "dep", None, None, None),
            P(("grp", "row"), "col", "dep", None, None, None),
            P(("grp", "row"), "col", "dep", None, None, None),
        ),
        out_specs=P(("grp", "row"), "col", "dep", None, None, None),
        check_vma=False,
    )
```

```python
import functools

import jax
import jax.numpy as jnp
from jax import lax
from jax.experimental import pallas as pl
from jax.experimental.pallas import tpu as pltpu
from jax.sharding import PartitionSpec as P

NBQ = 32
UNROLL = 4


def adding_kernel(left_count, right_count, given_count, rows, *refs):
    lists, refs = refs[0], refs[1:]
    lefts, refs = refs[:left_count], refs[left_count:]
    rights, refs = refs[:right_count], refs[right_count:]
    givens, refs = refs[:given_count], refs[given_count:]
    out, work, left_all, right_all, todo, sems, out_sem = refs
    half = work.shape[0] - 1
    copies = []
    for group, target in ((rights, right_all), (lefts, left_all)):
        start = 0
        for source in group:
            count = source.shape[0]
            copies.append(pltpu.make_async_copy(source, target.at[pl.ds(start, count)], sems.at[len(copies)]))
            start += count
    if givens:
        copies.append(pltpu.make_async_copy(givens[0], work, sems.at[len(copies)]))
    for copy in copies:
        copy.start()

    def keep(index, count):
        entry = lists[index]
        todo[count] = entry
        return count + (entry >= 0).astype(jnp.int32)

    count = lax.fori_loop(0, lists.shape[0], keep, jnp.int32(0), unroll=8)
    for extra in range(UNROLL - 1):
        todo[count + extra] = jnp.int32(half)
    if not givens:
        work[...] = jnp.zeros_like(work)
    for copy in copies:
        copy.wait()

    def several(group, carry):
        entries = [todo[group * UNROLL + lane] for lane in range(UNROLL)]
        products = [
            jnp.dot(
                left_all[(entry >> 10) & 1023], right_all[entry >> 20], preferred_element_type=jnp.float32
            )
            for entry in entries
        ]
        for entry, product in zip(entries, products):
            work[entry & 1023] += product
        return carry

    lax.fori_loop(0, (count + UNROLL - 1) // UNROLL, several, jnp.int32(0))
    if out.dtype == work.dtype:
        copy = pltpu.make_async_copy(work, out, out_sem)
        copy.start()
        copy.wait()
    else:
        out[...] = work[:half].astype(out.dtype)


def add_products(lists, lefts, rights, givens, half, last):
    width = rights[0].shape[2]
    rows = lefts[0].shape[1]
    left_slots = sum(panel.shape[0] for panel in lefts)
    right_slots = sum(panel.shape[0] for panel in rights)
    assert left_slots <= 1024 and right_slots <= 1024 and half < 1024
    anywhere = pl.BlockSpec(memory_space=pl.ANY)
    out_shape = (
        jax.ShapeDtypeStruct((half, rows, width), jnp.bfloat16)
        if last
        else jax.ShapeDtypeStruct((half + 1, rows, width), jnp.float32)
    )
    operands = [*lefts, *rights, *givens]
    return pl.pallas_call(
        functools.partial(adding_kernel, len(lefts), len(rights), len(givens), rows),
        out_shape=out_shape,
        in_specs=[pl.BlockSpec(memory_space=pltpu.SMEM)] + [anywhere] * len(operands),
        out_specs=pl.BlockSpec(memory_space=pltpu.VMEM) if last else anywhere,
        scratch_shapes=[
            pltpu.VMEM((half + 1, rows, width), jnp.float32),
            pltpu.VMEM((left_slots, rows, width), jnp.bfloat16),
            pltpu.VMEM((right_slots, width, width), jnp.bfloat16),
            pltpu.SMEM((lists.shape[0] + UNROLL,), jnp.int32),
            pltpu.SemaphoreType.DMA((len(operands),)),
            pltpu.SemaphoreType.DMA,
        ],
        compiler_params=pltpu.CompilerParams(vmem_limit_bytes=56 << 20),
        cost_estimate=pl.CostEstimate(
            flops=lists.size * rows * width**2, bytes_accessed=32 << 20, transcendentals=0
        ),
    )(lists, *operands)


def swapped(value):
    return lax.ppermute(value, "dep", [(0, 1), (1, 0)])


def local(left_blocks, right_blocks, triples):
    own = left_blocks[0, 0, 0]
    right_own = right_blocks[0, 0, 0]
    step_lists = triples[0, 0, 0]
    slots = own.shape[0]
    part = right_own.shape[0]
    step_count = step_lists.shape[0]
    centre = step_count // 2
    columns, row_count = lax.axis_size("col"), lax.axis_size("row")
    place, layer = lax.axis_index("col"), lax.axis_index("dep")
    cyclic = columns >= step_count
    reach = centre if cyclic else columns - 1
    half = (2 * step_count - 2 + row_count) // row_count * NBQ // 2

    right_slots = row_count * part
    if row_count == 2:
        met = lax.ppermute(right_own, "row", [(0, 1), (1, 0)])
        rights = [right_own, met, swapped(right_own), swapped(met)]
        turn = lax.axis_index("row") * part
    else:
        gathered = lax.all_gather(right_own, "row", axis=0, tiled=True)
        rights = [gathered, swapped(gathered)]
        turn = 0

    both = jnp.stack([step_lists, swapped(step_lists)])
    result = both[:, :, 2] - layer * half
    wanted = (result >= 0) & (result < half)
    order = jnp.arange(2, dtype=jnp.int32)[:, None, None]
    second = (both[:, :, 1] - turn) % right_slots + order * right_slots
    first = both[:, :, 0] + (order ^ layer) * slots
    packed = jnp.where(wanted, second << 20 | first << 10 | result, -1)

    def listed(offset, panel, valid=True):
        rows = [packed[:, s] for s in range(step_count) if (s - centre - offset) % columns == 0]
        entries = jnp.concatenate(rows, axis=1).reshape(-1)
        return jnp.where(valid & (entries >= 0), entries + (panel * 2 * slots << 10), -1)

    def paired(panel):
        return lax.all_gather(panel, "dep", axis=0, tiled=True)

    if cyclic:
        rising, falling, total = own, own, None
        lefts, lists = [paired(own)], [listed(0, 0)]
        for distance in range(1, reach + 1):
            rising = lax.ppermute(rising, "col", [(i, (i + 1) % columns) for i in range(columns)])
            falling = lax.ppermute(falling, "col", [(i, (i - 1) % columns) for i in range(columns)])
            lists += [listed(-distance, len(lefts)), listed(distance, len(lefts) + 1)]
            lefts += [paired(rising), paired(falling)]
            givens = [] if total is None else [total]
            total = add_products(jnp.concatenate(lists), lefts, rights, givens, half, distance == reach)
            lefts, lists = [], []
        return total[None, None, None]

    assert columns == 4
    rising = lax.ppermute(own, "col", [(0, 1), (1, 2), (2, 3)])
    falling = lax.ppermute(own, "col", [(1, 0), (2, 1), (3, 2)])
    own_pair = paired(own)
    rising, falling, rights, own_pair = lax.optimization_barrier((rising, falling, rights, own_pair))
    rising_two = lax.ppermute(rising, "col", [(1, 2), (2, 3)])
    falling_two = lax.ppermute(falling, "col", [(1, 0), (2, 1)])
    near = [listed(0, 0), listed(-1, 1, place > 0), listed(1, 2, place < 3)]
    total = add_products(
        jnp.concatenate(near), [own_pair, paired(rising), paired(falling)], rights, [], half, False
    )
    rising_two, falling_two, total = lax.optimization_barrier((rising_two, falling_two, total))
    rising_three = lax.ppermute(rising_two, "col", [(2, 3)])
    falling_three = lax.ppermute(falling_two, "col", [(1, 0)])
    two = jnp.where(place > 1, rising_two, falling_two)
    three = jnp.where(place > 1, rising_three, falling_three)
    far = [listed(2, 0), jnp.where(place == 3, listed(1, 1), listed(-1, 1, place == 0))]
    total = add_products(jnp.concatenate(far), [paired(two), paired(three)], rights, [total], half, True)
    return total[None, None, None]


def solution(mesh):
    return jax.shard_map(
        local,
        mesh=mesh,
        in_specs=(
            P(("grp", "row"), "col", "dep", None, None, None),
            P(("grp", "row"), "col", "dep", None, None, None),
            P(("grp", "row"), "col", "dep", None, None, None),
        ),
        out_specs=P(("grp", "row"), "col", "dep", None, None, None),
        check_vma=False,
    )
```

```python
import functools

import jax
import jax.numpy as jnp
from jax import lax
from jax.experimental import pallas as pl
from jax.experimental.pallas import tpu as pltpu
from jax.sharding import PartitionSpec as P

NBQ = 32
UNROLL = 4


def adding_kernel(shape, left_counts, right_count, given_count, *refs):
    step_count, columns, slots, rounds = shape
    packed, classes, refs = refs[0], refs[1], refs[2:]
    lefts, refs = refs[: sum(left_counts)], refs[sum(left_counts) :]
    rights, refs = refs[:right_count], refs[right_count:]
    givens, refs = refs[:given_count], refs[given_count:]
    out, work, left_all, right_all, todo, sems, out_sem = refs
    half = work.shape[0] - 1
    copies, needed = [], []
    owners = [panel for panel, pieces in enumerate(left_counts) for _ in range(pieces)]
    for group, target, panels in ((rights, right_all, [None] * right_count), (lefts, left_all, owners)):
        start = 0
        for source, panel in zip(group, panels):
            count = source.shape[0]
            copies.append(pltpu.make_async_copy(source, target.at[pl.ds(start, count)], sems.at[len(copies)]))
            needed.append(None if panel is None else classes[panel] >= 0)
            start += count
    if givens:
        copies.append(pltpu.make_async_copy(givens[0], work, sems.at[len(copies)]))
        needed.append(None)

    def each_copy(method):
        for copy, when in zip(copies, needed):
            if when is None:
                getattr(copy, method)()
            else:
                pl.when(when)(getattr(copy, method))

    each_copy("start")

    count = jnp.int32(0)
    for panel in range(len(left_counts)):
        kind = classes[panel]
        for extra in range(rounds):
            step = lax.rem(kind + step_count // 2, columns) + extra * columns
            groups = jnp.where((kind >= 0) & (step < step_count), slots // 8, 0)
            for layer in range(2):
                base = (layer * step_count + step) * slots

                def keep(group, count):
                    for lane in range(8):
                        entry = packed[base + group * 8 + lane]
                        todo[count] = entry + (panel * 2 * slots << 10)
                        count += (entry >= 0).astype(jnp.int32)
                    return count

                count = lax.fori_loop(0, groups, keep, count)
    for extra in range(UNROLL - 1):
        todo[count + extra] = jnp.int32(half)
    if not givens:
        work[...] = jnp.zeros_like(work)
    each_copy("wait")

    def several(group, carry):
        entries = [todo[group * UNROLL + lane] for lane in range(UNROLL)]
        products = [
            jnp.dot(left_all[(entry >> 10) & 1023], right_all[entry >> 20], preferred_element_type=jnp.float32)
            for entry in entries
        ]
        for entry, product in zip(entries, products):
            work[entry & 1023] += product
        return carry

    lax.fori_loop(0, (count + UNROLL - 1) // UNROLL, several, jnp.int32(0))
    if out.dtype == work.dtype:
        copy = pltpu.make_async_copy(work, out, out_sem)
        copy.start()
        copy.wait()
    else:
        out[...] = work[:half].astype(out.dtype)


def add_products(packed, classes, columns, panels, rights, givens, half, last):
    step_count, slots = packed.shape[1:]
    rounds = -(-step_count // columns)
    width = rights[0].shape[2]
    lefts = [piece for panel in panels for piece in panel]
    rows = lefts[0].shape[1]
    left_slots = sum(piece.shape[0] for piece in lefts)
    right_slots = sum(piece.shape[0] for piece in rights)
    assert left_slots <= 1024 and right_slots <= 1024 and half < 1024 and slots % 8 == 0
    anywhere = pl.BlockSpec(memory_space=pl.ANY)
    in_scalar = pl.BlockSpec(memory_space=pltpu.SMEM)
    out_shape = (
        jax.ShapeDtypeStruct((half, rows, width), jnp.bfloat16)
        if last
        else jax.ShapeDtypeStruct((half + 1, rows, width), jnp.float32)
    )
    operands = [*lefts, *rights, *givens]
    room = len(panels) * rounds * 2 * slots + UNROLL
    shape = (step_count, columns, slots, rounds)
    return pl.pallas_call(
        functools.partial(adding_kernel, shape, [len(panel) for panel in panels], len(rights), len(givens)),
        out_shape=out_shape,
        in_specs=[in_scalar, in_scalar] + [anywhere] * len(operands),
        out_specs=pl.BlockSpec(memory_space=pltpu.VMEM) if last else anywhere,
        scratch_shapes=[
            pltpu.VMEM((half + 1, rows, width), jnp.float32),
            pltpu.VMEM((left_slots, rows, width), jnp.bfloat16),
            pltpu.VMEM((right_slots, width, width), jnp.bfloat16),
            pltpu.SMEM((room,), jnp.int32),
            pltpu.SemaphoreType.DMA((len(operands),)),
            pltpu.SemaphoreType.DMA,
        ],
        compiler_params=pltpu.CompilerParams(vmem_limit_bytes=56 << 20),
        cost_estimate=pl.CostEstimate(
            flops=len(panels) * 4 * slots * rows * width**2, bytes_accessed=32 << 20, transcendentals=0
        ),
    )(packed.reshape(-1), classes, *operands)


def swapped(value):
    return lax.ppermute(value, "dep", [(0, 1), (1, 0)])


def paired(value):
    return lax.all_gather(value, "dep", axis=0, tiled=True)


def local(left_blocks, right_blocks, triples):
    own = left_blocks[0, 0, 0]
    right_own = right_blocks[0, 0, 0]
    step_lists = triples[0, 0, 0]
    slots = own.shape[0]
    part = right_own.shape[0]
    step_count = step_lists.shape[0]
    centre = step_count // 2
    columns, row_count = lax.axis_size("col"), lax.axis_size("row")
    place, layer = lax.axis_index("col"), lax.axis_index("dep")
    cyclic = columns >= step_count
    half = (2 * step_count - 2 + row_count) // row_count * NBQ // 2

    lists = paired(step_lists).reshape(2, step_count, 3, slots)
    result = lists[:, :, 2] - layer * half
    wanted = (result >= 0) & (result < half)
    layers = jnp.arange(2, dtype=jnp.int32)[:, None, None]
    given_first, given_second = lists[:, :, 0], lists[:, :, 1]
    first = layers * slots + given_first
    if row_count == 2:
        met = lax.ppermute(right_own, "row", [(0, 1), (1, 0)])
        rights = [paired(right_own), paired(met)]
        second = (((given_second // part) ^ lax.axis_index("row")) * 2 + layers) * part + given_second % part
    else:
        rights = [paired(lax.all_gather(right_own, "row", axis=0, tiled=True))]
        second = layers * (row_count * part) + given_second
    packed = jnp.where(wanted, second << 20 | first << 10 | result, -1)

    def kinds(*values):
        return jnp.stack([jnp.asarray(value, jnp.int32) for value in values])

    if cyclic:
        rising, falling, total = own, own, None
        panels, offsets = [[paired(own)]], [0]
        for distance in range(1, centre + 1):
            rising = lax.ppermute(rising, "col", [(i, (i + 1) % columns) for i in range(columns)])
            falling = lax.ppermute(falling, "col", [(i, (i - 1) % columns) for i in range(columns)])
            panels += [[paired(rising)], [paired(falling)]]
            offsets += [columns - distance, distance]
            givens = [] if total is None else [total]
            total = add_products(
                packed, kinds(*offsets), columns, panels, rights, givens, half, distance == centre
            )
            panels, offsets = [], []
        return total[None, None, None]

    assert columns == 4
    rising = lax.ppermute(own, "col", [(0, 1), (1, 2), (2, 3)])
    falling = lax.ppermute(own, "col", [(1, 0), (2, 1), (3, 2)])
    rising_two = lax.ppermute(rising, "col", [(1, 2), (2, 3)])
    falling_two = lax.ppermute(falling, "col", [(1, 0), (2, 1)])
    rising_three = lax.ppermute(rising_two, "col", [(2, 3)])
    falling_three = lax.ppermute(falling_two, "col", [(1, 0)])
    two = jnp.where(place > 1, rising_two, falling_two)
    panels = [[paired(value)] for value in (own, rising, falling, two)]
    classes = kinds(0, jnp.where(place > 0, 3, -1), jnp.where(place < 3, 1, -1), 2)
    total = add_products(packed, classes, columns, panels, rights, [], half, False)
    rising_three, falling_three, total = lax.optimization_barrier((rising_three, falling_three, total))
    three = jnp.where(place > 1, rising_three, falling_three)
    classes = kinds(jnp.where(place == 3, 1, jnp.where(place == 0, 3, -1)))
    packed_far = jnp.where(packed >= 0, packed ^ (layer * slots << 10), -1)
    total = add_products(packed_far, classes, columns, [[three, swapped(three)]], rights, [total], half, True)
    return total[None, None, None]


def solution(mesh):
    return jax.shard_map(
        local,
        mesh=mesh,
        in_specs=(
            P(("grp", "row"), "col", "dep", None, None, None),
            P(("grp", "row"), "col", "dep", None, None, None),
            P(("grp", "row"), "col", "dep", None, None, None),
        ),
        out_specs=P(("grp", "row"), "col", "dep", None, None, None),
        check_vma=False,
    )
```

```python
import functools

import jax
import jax.numpy as jnp
from jax import lax
from jax.experimental import pallas as pl
from jax.experimental.pallas import tpu as pltpu
from jax.sharding import PartitionSpec as P

NBQ = 32
UNROLL = 8


def adding_kernel(shape, left_counts, right_count, given_count, *refs):
    step_count, columns, slots, rounds = shape
    packed, classes, refs = refs[0], refs[1], refs[2:]
    lefts, refs = refs[: sum(left_counts)], refs[sum(left_counts) :]
    rights, refs = refs[:right_count], refs[right_count:]
    givens, refs = refs[:given_count], refs[given_count:]
    out, work, left_all, right_all, todo, sems, out_sem = refs
    half = work.shape[0] - 1
    copies, needed = [], []
    owners = [panel for panel, pieces in enumerate(left_counts) for _ in range(pieces)]
    for group, target, panels in ((rights, right_all, [None] * right_count), (lefts, left_all, owners)):
        start = 0
        for source, panel in zip(group, panels):
            count = source.shape[0]
            copies.append(pltpu.make_async_copy(source, target.at[pl.ds(start, count)], sems.at[len(copies)]))
            needed.append(None if panel is None else classes[panel] >= 0)
            start += count
    if givens:
        copies.append(pltpu.make_async_copy(givens[0], work, sems.at[len(copies)]))
        needed.append(None)

    def each_copy(method):
        for copy, when in zip(copies, needed):
            if when is None:
                getattr(copy, method)()
            else:
                pl.when(when)(getattr(copy, method))

    each_copy("start")

    count = jnp.int32(0)
    for panel in range(len(left_counts)):
        kind = classes[panel]
        for extra in range(rounds):
            step = lax.rem(kind + step_count // 2, columns) + extra * columns
            groups = jnp.where((kind >= 0) & (step < step_count), slots // 8, 0)
            for layer in range(2):
                base = (layer * step_count + step) * slots

                def keep(group, count):
                    for lane in range(8):
                        entry = packed[base + group * 8 + lane]
                        todo[count] = entry + (panel * 2 * slots << 10)
                        count += (entry >= 0).astype(jnp.int32)
                    return count

                count = lax.fori_loop(0, groups, keep, count)
    for extra in range(UNROLL - 1):
        todo[count + extra] = jnp.int32(half)
    if not givens:
        work[...] = jnp.zeros_like(work)
    each_copy("wait")

    def several(group, carry):
        entries = [todo[group * UNROLL + lane] for lane in range(UNROLL)]
        products = [
            jnp.dot(left_all[(entry >> 10) & 1023], right_all[entry >> 20], preferred_element_type=jnp.float32)
            for entry in entries
        ]
        for entry, product in zip(entries, products):
            work[entry & 1023] += product
        return carry

    lax.fori_loop(0, (count + UNROLL - 1) // UNROLL, several, jnp.int32(0))
    if out.dtype == work.dtype:
        copy = pltpu.make_async_copy(work, out, out_sem)
        copy.start()
        copy.wait()
    else:
        out[...] = work[:half].astype(out.dtype)


def add_products(packed, classes, columns, panels, rights, givens, half, last):
    step_count, slots = packed.shape[1:]
    rounds = -(-step_count // columns)
    width = rights[0].shape[2]
    lefts = [piece for panel in panels for piece in panel]
    rows = lefts[0].shape[1]
    left_slots = sum(piece.shape[0] for piece in lefts)
    right_slots = sum(piece.shape[0] for piece in rights)
    assert left_slots <= 1024 and right_slots <= 1024 and half < 1024 and slots % 8 == 0
    anywhere = pl.BlockSpec(memory_space=pl.ANY)
    in_scalar = pl.BlockSpec(memory_space=pltpu.SMEM)
    out_shape = (
        jax.ShapeDtypeStruct((half, rows, width), jnp.bfloat16)
        if last
        else jax.ShapeDtypeStruct((half + 1, rows, width), jnp.float32)
    )
    operands = [*lefts, *rights, *givens]
    room = len(panels) * rounds * 2 * slots + UNROLL
    shape = (step_count, columns, slots, rounds)
    return pl.pallas_call(
        functools.partial(adding_kernel, shape, [len(panel) for panel in panels], len(rights), len(givens)),
        out_shape=out_shape,
        in_specs=[in_scalar, in_scalar] + [anywhere] * len(operands),
        out_specs=pl.BlockSpec(memory_space=pltpu.VMEM) if last else anywhere,
        scratch_shapes=[
            pltpu.VMEM((half + 1, rows, width), jnp.float32),
            pltpu.VMEM((left_slots, rows, width), jnp.bfloat16),
            pltpu.VMEM((right_slots, width, width), jnp.bfloat16),
            pltpu.SMEM((room,), jnp.int32),
            pltpu.SemaphoreType.DMA((len(operands),)),
            pltpu.SemaphoreType.DMA,
        ],
        compiler_params=pltpu.CompilerParams(vmem_limit_bytes=56 << 20),
        cost_estimate=pl.CostEstimate(
            flops=len(panels) * 4 * slots * rows * width**2, bytes_accessed=32 << 20, transcendentals=0
        ),
    )(packed.reshape(-1), classes, *operands)


def swapped(value):
    return lax.ppermute(value, "dep", [(0, 1), (1, 0)])


def paired(value):
    return lax.all_gather(value, "dep", axis=0, tiled=True)


def local(left_blocks, right_blocks, triples):
    own = left_blocks[0, 0, 0]
    right_own = right_blocks[0, 0, 0]
    step_lists = triples[0, 0, 0]
    slots = own.shape[0]
    part = right_own.shape[0]
    step_count = step_lists.shape[0]
    centre = step_count // 2
    columns, row_count = lax.axis_size("col"), lax.axis_size("row")
    place, layer = lax.axis_index("col"), lax.axis_index("dep")
    cyclic = columns >= step_count
    half = (2 * step_count - 2 + row_count) // row_count * NBQ // 2

    lists = paired(step_lists).reshape(2, step_count, 3, slots)
    result = lists[:, :, 2] - layer * half
    wanted = (result >= 0) & (result < half)
    layers = jnp.arange(2, dtype=jnp.int32)[:, None, None]
    given_first, given_second = lists[:, :, 0], lists[:, :, 1]
    first = layers * slots + given_first
    if row_count == 2:
        met = lax.ppermute(right_own, "row", [(0, 1), (1, 0)])
        rights = [right_own, met, swapped(right_own), swapped(met)]
        nearer = (given_second // part) ^ lax.axis_index("row")
        second = ((layers ^ layer) * 2 + nearer) * part + given_second % part
    else:
        rights = [paired(lax.all_gather(right_own, "row", axis=0, tiled=True))]
        second = layers * (row_count * part) + given_second
    packed = jnp.where(wanted, second << 20 | first << 10 | result, -1)

    def kinds(*values):
        return jnp.stack([jnp.asarray(value, jnp.int32) for value in values])

    if cyclic:
        rising, falling, total = own, own, None
        panels, offsets = [[paired(own)]], [0]
        for distance in range(1, centre + 1):
            rising = lax.ppermute(rising, "col", [(i, (i + 1) % columns) for i in range(columns)])
            falling = lax.ppermute(falling, "col", [(i, (i - 1) % columns) for i in range(columns)])
            panels += [[paired(rising)], [paired(falling)]]
            offsets += [columns - distance, distance]
            givens = [] if total is None else [total]
            total = add_products(
                packed, kinds(*offsets), columns, panels, rights, givens, half, distance == centre
            )
            panels, offsets = [], []
        return total[None, None, None]

    assert columns == 4
    rising = lax.ppermute(own, "col", [(0, 1), (1, 2), (2, 3)])
    falling = lax.ppermute(own, "col", [(1, 0), (2, 1), (3, 2)])
    rising, falling, rights = lax.optimization_barrier((rising, falling, rights))
    rising_two = lax.ppermute(rising, "col", [(1, 2), (2, 3)])
    falling_two = lax.ppermute(falling, "col", [(1, 0), (2, 1)])
    rising_two, falling_two = lax.optimization_barrier((rising_two, falling_two))
    two = jnp.where(place > 1, rising_two, falling_two)
    three = lax.ppermute(two, "col", [(2, 3), (1, 0)])
    panels = [[paired(value)] for value in (own, rising, falling, two)]
    classes = kinds(0, jnp.where(place > 0, 3, -1), jnp.where(place < 3, 1, -1), 2)
    total = add_products(packed, classes, columns, panels, rights, [], half, False)
    three, total = lax.optimization_barrier((three, total))
    classes = kinds(jnp.where(place == 3, 1, jnp.where(place == 0, 3, -1)))
    packed_far = jnp.where(packed >= 0, packed ^ (layer * slots << 10), -1)
    total = add_products(packed_far, classes, columns, [[three, swapped(three)]], rights, [total], half, True)
    return total[None, None, None]


def solution(mesh):
    return jax.shard_map(
        local,
        mesh=mesh,
        in_specs=(
            P(("grp", "row"), "col", "dep", None, None, None),
            P(("grp", "row"), "col", "dep", None, None, None),
            P(("grp", "row"), "col", "dep", None, None, None),
        ),
        out_specs=P(("grp", "row"), "col", "dep", None, None, None),
        check_vma=False,
    )
```

```python
import functools

import jax
import jax.numpy as jnp
from jax import lax
from jax.experimental import pallas as pl
from jax.experimental.pallas import tpu as pltpu
from jax.sharding import PartitionSpec as P

NBQ = 32
NEAR = 0.75
DIRECT = 0.65


def chosen_products(packed, classes, panels, todo, shape, unroll, spare):
    step_count, columns, slots = shape
    count = jnp.int32(0)
    for panel in range(panels):
        kind = classes[panel]
        for extra in range(-(-step_count // columns)):
            step = lax.rem(kind + step_count // 2, columns) + extra * columns
            groups = jnp.where((kind >= 0) & (step < step_count), slots // 8, 0)
            for layer in range(2):
                base = (layer * step_count + step) * slots

                def keep(group, count):
                    for lane in range(8):
                        entry = packed[base + group * 8 + lane]
                        todo[count] = entry + (panel * 2 * slots << 10)
                        count += (entry >= 0).astype(jnp.int32)
                    return count

                count = lax.fori_loop(0, groups, keep, count)
    for extra in range(unroll - 1):
        todo[count + extra] = jnp.int32(spare)
    return count


def add_chosen(todo, count, left, right, work, unroll):
    rows, width = work.shape[1:]

    def several(group, carry):
        entries = [todo[group * unroll + lane] for lane in range(unroll)]
        products = []
        for entry in entries:
            first = pl.multiple_of(((entry >> 10) & 1023) * rows, rows)
            second = pl.multiple_of((entry >> 20) * width, width)
            products.append(
                jnp.dot(left[pl.ds(first, rows)], right[pl.ds(second, width)], preferred_element_type=jnp.float32)
            )
        for entry, product in zip(entries, products):
            work[entry & 1023] += product
        return carry

    lax.fori_loop(0, (count + unroll - 1) // unroll, several, jnp.int32(0))


def sum_kernel(groups, right_spans, has_given, shape, half, operand_count, layer_at, *refs):
    packed, classes, refs = refs[0], refs[1], refs[2:]
    operands, refs = refs[:operand_count], refs[operand_count:]
    out, refs = refs[0], refs[1:]
    works, lefts = refs[: len(groups)], refs[len(groups) : 2 * len(groups)]
    right, todo, sems, out_sem = refs[2 * len(groups) :]
    slots = shape[2]
    other = 1 - classes[layer_at]
    copies = []

    def plan(source, target, when):
        copies.append((pltpu.make_async_copy(source, target, sems.at[len(copies)]), when))

    any_class = classes[0]
    for at in range(1, layer_at):
        any_class = jnp.maximum(any_class, classes[at])
    start = 0
    for operand, first, size in right_spans:
        plan(operands[operand].at[pl.ds(first, size)], right.at[pl.ds(start, size)], any_class >= 0)
        start += size
    class_at = 0
    for (panels, rows), left in zip(groups, lefts):
        start, size = 0, slots * rows
        for panel, pieces in enumerate(panels):
            for operand, first, gathered in pieces:
                if gathered:
                    first = pl.multiple_of(first + other * gathered, 16)
                source = operands[operand].at[pl.ds(first, size)]
                plan(source, left.at[pl.ds(start, size)], classes[class_at + panel] >= 0)
                start += size
        class_at += len(panels)
    if has_given:
        plan(operands[operand_count - 1], works[0], None)
    for copy, when in copies:
        copy.start() if when is None else pl.when(when)(copy.start)
    for index, work in enumerate(works):
        if index > 0 or not has_given:
            work[...] = jnp.zeros_like(work)

    class_at = 0
    for index, ((panels, rows), work, left) in enumerate(zip(groups, works, lefts)):
        unroll = 16 if rows <= 64 else 8
        kinds = [classes[class_at + panel] for panel in range(len(panels))]
        class_at += len(panels)
        count = chosen_products(packed, kinds, len(panels), todo, shape, unroll, half)
        if index == 0:
            for copy, when in copies:
                copy.wait() if when is None else pl.when(when)(copy.wait)
        add_chosen(todo, count, left, right, work, unroll)
    if out.dtype == works[0].dtype:
        copy = pltpu.make_async_copy(works[0], out, out_sem)
        copy.start()
        copy.wait()
    else:
        start = 0
        for (panels, rows), work in zip(groups, works):
            out[:, start : start + rows] = work[:half].astype(out.dtype)
            start += rows


def flat(value):
    return value.reshape(-1, value.shape[-1])


def product_sums(packed, classes, layer, shape, groups, rights, given, half, finished):
    step_count, columns, slots = shape
    width = rights[0][0].shape[-1]
    operands, known = [], []

    def number(value):
        for index, other in enumerate(known):
            if other is value:
                return index
        known.append(value)
        operands.append(flat(value))
        return len(operands) - 1

    right_spans = [(number(value), first, size) for value, first, size in rights]
    numbered = [
        ([[(number(value), first, gathered) for value, first, gathered in panel] for panel in panels], rows)
        for panels, rows in groups
    ]
    if given is not None:
        operands.append(given)
    right_rows = sum(size for _, _, size in rights)
    most = max(len(panels) for panels, _ in groups)
    assert right_rows <= 1024 * width and most * 2 * slots <= 1024 and half < 1024 and slots % 8 == 0
    anywhere = pl.BlockSpec(memory_space=pl.ANY)
    in_scalar = pl.BlockSpec(memory_space=pltpu.SMEM)
    all_rows = sum(rows for _, rows in groups)
    out_shape = (
        jax.ShapeDtypeStruct((half, all_rows, width), jnp.bfloat16)
        if finished
        else jax.ShapeDtypeStruct((half + 1, all_rows, width), jnp.float32)
    )
    copy_count = len(rights) + sum(len(panel) for panels, _ in groups for panel in panels) + 1
    scalars = jnp.stack([jnp.asarray(value, jnp.int32) for value in [*classes, layer]])
    return pl.pallas_call(
        functools.partial(
            sum_kernel, numbered, right_spans, given is not None, shape, half, len(operands), len(classes)
        ),
        out_shape=out_shape,
        in_specs=[in_scalar, in_scalar] + [anywhere] * len(operands),
        out_specs=pl.BlockSpec(memory_space=pltpu.VMEM) if finished else anywhere,
        scratch_shapes=[pltpu.VMEM((half + 1, rows, width), jnp.float32) for _, rows in groups]
        + [pltpu.VMEM((len(panels) * 2 * slots * rows, width), jnp.bfloat16) for panels, rows in groups]
        + [
            pltpu.VMEM((right_rows, width), jnp.bfloat16),
            pltpu.SMEM((most * 4 * slots + 16,), jnp.int32),
            pltpu.SemaphoreType.DMA((copy_count,)),
            pltpu.SemaphoreType.DMA,
        ],
        compiler_params=pltpu.CompilerParams(vmem_limit_bytes=48 << 20),
        cost_estimate=pl.CostEstimate(flops=1, bytes_accessed=1, transcendentals=0),
    )(packed, scalars, *operands)


def place_rows_kernel(first, rows, takes, block, received, out, sem):
    del block

    @pl.when(takes[0] > 0)
    def _():
        copy = pltpu.make_async_copy(received, out.at[:, pl.ds(first, rows)], sem)
        copy.start()
        copy.wait()


def place_rows(takes, block, received, first):
    anywhere = pl.BlockSpec(memory_space=pl.ANY)
    return pl.pallas_call(
        functools.partial(place_rows_kernel, first, received.shape[1]),
        out_shape=jax.ShapeDtypeStruct(block.shape, block.dtype),
        in_specs=[pl.BlockSpec(memory_space=pltpu.SMEM), anywhere, anywhere],
        out_specs=anywhere,
        scratch_shapes=[pltpu.SemaphoreType.DMA],
        input_output_aliases={1: 0},
    )(takes.astype(jnp.int32).reshape(1), block, received)


def swapped(value):
    return lax.ppermute(value, "dep", [(0, 1), (1, 0)])


def paired(value):
    return lax.all_gather(value, "dep", axis=0, tiled=True)


def packed_lists(step_lists, layer, half, right_place):
    step_count, _, slots = step_lists.shape
    both = paired(step_lists).reshape(2, step_count, 3, slots)
    both = jnp.where(layer > 0, both[::-1], both)
    result = both[:, :, 2] - layer * half
    wanted = (result >= 0) & (result < half)
    layers = jnp.arange(2, dtype=jnp.int32)[:, None, None]
    packed = right_place(both[:, :, 1], layers) << 20 | (layers * slots + both[:, :, 0]) << 10 | result
    return jnp.where(wanted, packed, -1).reshape(-1)


def ring(left_blocks, right_blocks, triples, half):
    own, right_own, step_lists = left_blocks[0, 0, 0], right_blocks[0, 0, 0], triples[0, 0, 0]
    slots, rows = own.shape[0], own.shape[1]
    columns, layer = lax.axis_size("col"), lax.axis_index("dep")
    gathered = lax.all_gather(right_own, "row", axis=0, tiled=True)
    right_slots = gathered.shape[0]
    packed = packed_lists(step_lists, layer, half, lambda slot, layers: layers * right_slots + slot)
    rights = [(value, 0, right_slots * rows) for value in (gathered, swapped(gathered))]
    shape = (step_lists.shape[0], columns, slots)
    rising, falling, total = own, own, None
    size = slots * rows
    panels, classes = [[(own, 0, 0), (paired(own), 0, size)]], [0]
    reach = step_lists.shape[0] // 2
    for distance in range(1, reach + 1):
        rising = lax.ppermute(rising, "col", [(i, (i + 1) % columns) for i in range(columns)])
        falling = lax.ppermute(falling, "col", [(i, (i - 1) % columns) for i in range(columns)])
        panels += [[(value, 0, 0), (paired(value), 0, size)] for value in (rising, falling)]
        classes += [columns - distance, distance]
        total = product_sums(
            packed, classes, layer, shape, [(panels, rows)], rights, total, half, distance == reach
        )
        panels, classes = [], []
    return total[None, None, None]


def line(left_blocks, right_blocks, triples, half):
    own, right_own, step_lists = left_blocks[0, 0, 0], right_blocks[0, 0, 0], triples[0, 0, 0]
    slots, rows, part = own.shape[0], own.shape[1], right_own.shape[0]
    columns, layer, place = lax.axis_size("col"), lax.axis_index("dep"), lax.axis_index("col")
    shape = (step_lists.shape[0], columns, slots)
    near = int(rows * NEAR) // 16 * 16
    far = rows - near
    cut = int(part * DIRECT)
    up, down = [(0, 1), (1, 2), (2, 3)], [(1, 0), (2, 1), (3, 2)]
    inward, across, outward = [(0, 1), (3, 2)], [(1, 2), (2, 1)], [(2, 3), (1, 0)]
    high, inner = place == 2, (place == 1) | (place == 2)

    own_near, own_far = own[:, :near], flat(own[:, near:])
    met = lax.ppermute(right_own, "row", [(0, 1), (1, 0)])
    rising = lax.ppermute(own_near, "col", up)
    falling = lax.ppermute(own_near, "col", down)
    near_other, far_other, right_pair = swapped(own_near), swapped(own_far), paired(right_own)

    def right_place(slot, layers):
        farther, within = (slot // part) ^ lax.axis_index("row"), slot % part
        first = jnp.where(within < cut, farther * cut + within, 2 * cut + farther * (part - cut) + within - cut)
        return layers * 2 * part + first

    packed = packed_lists(step_lists, layer, half, right_place)
    first_inward = jnp.concatenate([own_far, flat(right_own[:cut])])

    rising, falling, near_other, far_other, packed, first_inward = lax.optimization_barrier(
        (rising, falling, near_other, far_other, packed, first_inward)
    )
    rising_two = lax.ppermute(rising, "col", [(1, 2), (2, 3)])
    falling_two = lax.ppermute(falling, "col", [(2, 1), (1, 0)])
    end_far = lax.ppermute(first_inward, "col", inward)
    end_rest = lax.ppermute(jnp.concatenate([flat(right_own[cut:]), flat(met[cut:])]), "col", inward)
    end_packed = lax.ppermute(packed, "col", inward)
    met_pair, rising_pair, falling_pair = paired(met), paired(rising), paired(falling)

    rising_two, falling_two, end_far, end_packed, rising, falling = lax.optimization_barrier(
        (rising_two, falling_two, end_far, end_packed, rising, falling)
    )
    two = jnp.where(place > 1, rising_two, falling_two)
    near_size, far_size = slots * near, slots * far
    crossing = jnp.concatenate([own_far, end_far[:far_size]])
    two, crossing, end_right = lax.optimization_barrier((two, crossing, end_far[far_size:]))
    three = lax.ppermute(two, "col", outward)
    crossed = lax.ppermute(crossing, "col", across)
    end_met = lax.ppermute(end_right, "row", [(0, 1), (1, 0)])
    end_pair, two_pair = paired(end_far), paired(two)

    right_other = lax.dynamic_slice_in_dim(right_pair, (1 - layer) * part, part)
    met_other = lax.dynamic_slice_in_dim(met_pair, (1 - layer) * part, part)
    rights = []
    for nearer, farther in ((right_own, met), (right_other, met_other)):
        for first, size in ((0, cut), (cut, part - cut)):
            rights += [(nearer, first * rows, size * rows), (farther, first * rows, size * rows)]
    panels = [
        [(own_near, 0, 0), (near_other, 0, 0)],
        [(rising, 0, 0), (rising_pair, 0, near_size)],
        [(falling, 0, 0), (falling_pair, 0, near_size)],
    ]
    classes = [0, jnp.where(place > 0, 3, -1), jnp.where(place < 3, 1, -1)]
    total = product_sums(packed, classes, layer, shape, [(panels, near)], rights, None, half, False)

    crossed, end_met, end_rest, total = lax.optimization_barrier((crossed, end_met, end_rest, total))
    crossed_other, end_met_other, end_rest_other = swapped(crossed), swapped(end_met), swapped(end_rest)
    far_panels = [
        [(own_far, 0, 0), (far_other, 0, 0)],
        [(end_far, 0, 0), (end_pair, 0, end_far.shape[0])],
        [(crossed, 0, 0), (crossed_other, 0, 0)],
        [(crossed, far_size, 0), (crossed_other, far_size, 0)],
    ]
    end_other = lax.dynamic_slice_in_dim(end_pair, (1 - layer) * end_far.shape[0] + far_size, cut * rows)
    end_rights = [
        (end_far, far_size, cut * rows),
        (end_met, 0, cut * rows),
        (end_rest, 0, end_rest.shape[0]),
        (end_other, 0, cut * rows),
        (end_met_other, 0, cut * rows),
        (end_rest_other, 0, end_rest.shape[0]),
    ]
    classes = [jnp.where(high, 3, 1), 0, 2, jnp.where(high, 1, 3)]
    classes = [jnp.where(inner, kind, -1) for kind in classes]
    end_rows = product_sums(
        end_packed, classes, layer, shape, [(far_panels, far)], end_rights, None, half, True
    )

    end_rows, total, three, two_pair = lax.optimization_barrier((end_rows, total, three, two_pair))
    received = lax.ppermute(end_rows, "col", outward)
    near_panels = [
        [(two, 0, 0), (two_pair, 0, near_size)],
        [(three, 0, 0), (swapped(three), 0, 0)],
    ]
    classes = [2, jnp.where(place == 3, 1, jnp.where(place == 0, 3, -1))]
    far_classes = [0, jnp.where(high, 1, 3), jnp.where(high, 3, 1), 2]
    classes += [jnp.where(inner, kind, -1) for kind in far_classes]
    groups = [(near_panels, near), (far_panels, far)]
    block = product_sums(packed, classes, layer, shape, groups, rights, total, half, True)
    return place_rows(~inner, block, received, near)[None, None, None]


def local(left_blocks, right_blocks, triples):
    step_count = triples.shape[3]
    row_count, columns = lax.axis_size("row"), lax.axis_size("col")
    half = (2 * step_count - 2 + row_count) // row_count * NBQ // 2
    if columns >= step_count:
        return ring(left_blocks, right_blocks, triples, half)
    assert columns == 4 and row_count == 2
    return line(left_blocks, right_blocks, triples, half)


def solution(mesh):
    return jax.shard_map(
        local,
        mesh=mesh,
        in_specs=(
            P(("grp", "row"), "col", "dep", None, None, None),
            P(("grp", "row"), "col", "dep", None, None, None),
            P(("grp", "row"), "col", "dep", None, None, None),
        ),
        out_specs=P(("grp", "row"), "col", "dep", None, None, None),
        check_vma=False,
    )
```

```python
import functools

import jax
import jax.numpy as jnp
from jax import lax
from jax.experimental import pallas as pl
from jax.experimental.pallas import tpu as pltpu
from jax.sharding import PartitionSpec as P

NBQ = 32
NEAR = 0.75
DIRECT = 0.65


def chosen_products(packed, classes, panels, todo, shape, unroll, spare):
    step_count, columns, slots = shape
    count = jnp.int32(0)
    for panel in range(panels):
        kind = classes[panel]
        for extra in range(-(-step_count // columns)):
            step = lax.rem(kind + step_count // 2, columns) + extra * columns
            groups = jnp.where((kind >= 0) & (step < step_count), slots // 8, 0)
            for layer in range(2):
                base = (layer * step_count + step) * slots

                def keep(group, count):
                    for lane in range(8):
                        entry = packed[base + group * 8 + lane]
                        todo[count] = entry + (panel * 2 * slots << 10)
                        count += (entry >= 0).astype(jnp.int32)
                    return count

                count = lax.fori_loop(0, groups, keep, count)
    for extra in range(unroll - 1):
        todo[count + extra] = jnp.int32(spare)
    return count


def add_chosen(todo, count, left, right, work, unroll):
    rows, width = work.shape[1:]

    def several(group, carry):
        entries = [todo[group * unroll + lane] for lane in range(unroll)]
        products = []
        for entry in entries:
            first = pl.multiple_of(((entry >> 10) & 1023) * rows, rows)
            second = pl.multiple_of((entry >> 20) * width, width)
            products.append(
                jnp.dot(left[pl.ds(first, rows)], right[pl.ds(second, width)], preferred_element_type=jnp.float32)
            )
        for entry, product in zip(entries, products):
            work[entry & 1023] += product
        return carry

    lax.fori_loop(0, (count + unroll - 1) // unroll, several, jnp.int32(0))


def sum_kernel(groups, right_spans, has_given, shape, half, operand_count, layer_at, *refs):
    packed, classes, refs = refs[0], refs[1], refs[2:]
    operands, refs = refs[:operand_count], refs[operand_count:]
    out, refs = refs[0], refs[1:]
    works, lefts = refs[: len(groups)], refs[len(groups) : 2 * len(groups)]
    right, todo, sems, out_sem = refs[2 * len(groups) :]
    slots = shape[2]
    other = 1 - classes[layer_at]
    copies = []

    def plan(source, target, when):
        copies.append((pltpu.make_async_copy(source, target, sems.at[len(copies)]), when))

    any_class = classes[0]
    for at in range(1, layer_at):
        any_class = jnp.maximum(any_class, classes[at])
    start = 0
    for operand, first, size, gathered in right_spans:
        if gathered:
            first = pl.multiple_of(first + other * gathered, 16)
        plan(operands[operand].at[pl.ds(first, size)], right.at[pl.ds(start, size)], any_class >= 0)
        start += size
    class_at = 0
    for (panels, rows), left in zip(groups, lefts):
        start, size = 0, slots * rows
        for panel, pieces in enumerate(panels):
            for operand, first, gathered in pieces:
                if gathered:
                    first = pl.multiple_of(first + other * gathered, 16)
                source = operands[operand].at[pl.ds(first, size)]
                plan(source, left.at[pl.ds(start, size)], classes[class_at + panel] >= 0)
                start += size
        class_at += len(panels)
    if has_given:
        plan(operands[operand_count - 1], works[0], None)
    for copy, when in copies:
        copy.start() if when is None else pl.when(when)(copy.start)
    for index, work in enumerate(works):
        if index > 0 or not has_given:
            work[...] = jnp.zeros_like(work)

    class_at = 0
    for index, ((panels, rows), work, left) in enumerate(zip(groups, works, lefts)):
        unroll = 16 if rows <= 64 else 8
        kinds = [classes[class_at + panel] for panel in range(len(panels))]
        class_at += len(panels)
        count = chosen_products(packed, kinds, len(panels), todo, shape, unroll, half)
        if index == 0:
            for copy, when in copies:
                copy.wait() if when is None else pl.when(when)(copy.wait)
        add_chosen(todo, count, left, right, work, unroll)
    if out.dtype == works[0].dtype:
        copy = pltpu.make_async_copy(works[0], out, out_sem)
        copy.start()
        copy.wait()
    else:
        start = 0
        for (panels, rows), work in zip(groups, works):
            out[:, start : start + rows] = work[:half].astype(out.dtype)
            start += rows


def flat(value):
    return value.reshape(-1, value.shape[-1])


def product_sums(packed, classes, layer, shape, groups, rights, given, half, finished):
    step_count, columns, slots = shape
    width = rights[0][0].shape[-1]
    operands, known = [], []

    def number(value):
        for index, other in enumerate(known):
            if other is value:
                return index
        known.append(value)
        operands.append(flat(value))
        return len(operands) - 1

    right_spans = [(number(value), first, size, gathered) for value, first, size, gathered in rights]
    numbered = [
        ([[(number(value), first, gathered) for value, first, gathered in panel] for panel in panels], rows)
        for panels, rows in groups
    ]
    if given is not None:
        operands.append(given)
    right_rows = sum(span[2] for span in rights)
    most = max(len(panels) for panels, _ in groups)
    assert right_rows <= 1024 * width and most * 2 * slots <= 1024 and half < 1024 and slots % 8 == 0
    anywhere = pl.BlockSpec(memory_space=pl.ANY)
    in_scalar = pl.BlockSpec(memory_space=pltpu.SMEM)
    all_rows = sum(rows for _, rows in groups)
    out_shape = (
        jax.ShapeDtypeStruct((half, all_rows, width), jnp.bfloat16)
        if finished
        else jax.ShapeDtypeStruct((half + 1, all_rows, width), jnp.float32)
    )
    copy_count = len(rights) + sum(len(panel) for panels, _ in groups for panel in panels) + 1
    scalars = jnp.stack([jnp.asarray(value, jnp.int32) for value in [*classes, layer]])
    return pl.pallas_call(
        functools.partial(
            sum_kernel, numbered, right_spans, given is not None, shape, half, len(operands), len(classes)
        ),
        out_shape=out_shape,
        in_specs=[in_scalar, in_scalar] + [anywhere] * len(operands),
        out_specs=pl.BlockSpec(memory_space=pltpu.VMEM) if finished else anywhere,
        scratch_shapes=[pltpu.VMEM((half + 1, rows, width), jnp.float32) for _, rows in groups]
        + [pltpu.VMEM((len(panels) * 2 * slots * rows, width), jnp.bfloat16) for panels, rows in groups]
        + [
            pltpu.VMEM((right_rows, width), jnp.bfloat16),
            pltpu.SMEM((most * 4 * slots + 16,), jnp.int32),
            pltpu.SemaphoreType.DMA((copy_count,)),
            pltpu.SemaphoreType.DMA,
        ],
        compiler_params=pltpu.CompilerParams(vmem_limit_bytes=48 << 20),
        cost_estimate=pl.CostEstimate(flops=1, bytes_accessed=1, transcendentals=0),
    )(packed, scalars, *operands)


def place_rows_kernel(first, takes, block, received, out, sem):
    del block

    @pl.when(takes[0] > 0)
    def _():
        copy = pltpu.make_async_copy(received, out.at[:, pl.ds(first, received.shape[1])], sem)
        copy.start()
        copy.wait()


def place_rows(takes, block, received, first):
    anywhere = pl.BlockSpec(memory_space=pl.ANY)
    return pl.pallas_call(
        functools.partial(place_rows_kernel, first),
        out_shape=jax.ShapeDtypeStruct(block.shape, block.dtype),
        in_specs=[pl.BlockSpec(memory_space=pltpu.SMEM), anywhere, pl.BlockSpec(memory_space=pltpu.VMEM)],
        out_specs=anywhere,
        scratch_shapes=[pltpu.SemaphoreType.DMA],
        input_output_aliases={1: 0},
    )(takes.astype(jnp.int32).reshape(1), block, received)


def swapped(value):
    return lax.ppermute(value, "dep", [(0, 1), (1, 0)])


def paired(value):
    return lax.all_gather(value, "dep", axis=0, tiled=True)


def packed_lists(both, layer, half, right_place):
    step_count, _, slots = both.shape[1:]
    both = jnp.where(layer > 0, both[::-1], both)
    result = both[:, :, 2] - layer * half
    wanted = (result >= 0) & (result < half)
    layers = jnp.arange(2, dtype=jnp.int32)[:, None, None]
    packed = right_place(both[:, :, 1], layers) << 20 | (layers * slots + both[:, :, 0]) << 10 | result
    return jnp.where(wanted, packed, -1).reshape(-1)


def ring(left_blocks, right_blocks, triples, half):
    own, right_own, step_lists = left_blocks[0, 0, 0], right_blocks[0, 0, 0], triples[0, 0, 0]
    slots, rows = own.shape[0], own.shape[1]
    columns, layer = lax.axis_size("col"), lax.axis_index("dep")
    gathered = lax.all_gather(right_own, "row", axis=0, tiled=True)
    right_slots = gathered.shape[0]
    both = lax.all_gather(step_lists, "dep")
    packed = packed_lists(both, layer, half, lambda slot, layers: layers * right_slots + slot)
    rights = [(value, 0, right_slots * rows, 0) for value in (gathered, swapped(gathered))]
    shape = (step_lists.shape[0], columns, slots)
    rising, falling, total = own, own, None
    size = slots * rows
    panels, classes = [[(own, 0, 0), (paired(own), 0, size)]], [0]
    reach = step_lists.shape[0] // 2
    for distance in range(1, reach + 1):
        rising = lax.ppermute(rising, "col", [(i, (i + 1) % columns) for i in range(columns)])
        falling = lax.ppermute(falling, "col", [(i, (i - 1) % columns) for i in range(columns)])
        panels += [[(value, 0, 0), (paired(value), 0, size)] for value in (rising, falling)]
        classes += [columns - distance, distance]
        total = product_sums(
            packed, classes, layer, shape, [(panels, rows)], rights, total, half, distance == reach
        )
        panels, classes = [], []
    return total[None, None, None]


def line(left_blocks, right_blocks, triples, half):
    own, right_own, step_lists = left_blocks[0, 0, 0], right_blocks[0, 0, 0], triples[0, 0, 0]
    slots, rows, part = own.shape[0], own.shape[1], right_own.shape[0]
    columns, layer, place = lax.axis_size("col"), lax.axis_index("dep"), lax.axis_index("col")
    shape = (step_lists.shape[0], columns, slots)
    near = int(rows * NEAR) // 16 * 16
    far = rows - near
    cut = int(part * DIRECT)
    up, down = [(0, 1), (1, 2), (2, 3)], [(1, 0), (2, 1), (3, 2)]
    inward, across, outward = [(0, 1), (3, 2)], [(1, 2), (2, 1)], [(2, 3), (1, 0)]
    high, inner = place == 2, (place == 1) | (place == 2)

    own_near, own_far = own[:, :near], flat(own[:, near:])
    near_size, far_size = slots * near, slots * far
    met = lax.ppermute(right_own, "row", [(0, 1), (1, 0)])
    rising = lax.ppermute(own_near, "col", up)
    falling = lax.ppermute(own_near, "col", down)
    near_other, far_other = swapped(own_near), swapped(own_far)
    lists = lax.all_gather(step_lists, ("col", "dep")).reshape(columns, 2, *step_lists.shape)
    right_pair = paired(right_own)

    def right_place(slot, layers):
        farther, within = (slot // part) ^ lax.axis_index("row"), slot % part
        first = jnp.where(within < cut, farther * cut + within, 2 * cut + farther * (part - cut) + within - cut)
        return layers * 2 * part + first

    def lists_of(column):
        return packed_lists(lax.dynamic_index_in_dim(lists, column, 0, False), layer, half, right_place)

    packed, end_packed = lists_of(place), lists_of(jnp.where(place > 1, 3, 0))
    end_right = right_own[:cut]

    rising, falling, met, near_other, far_other, packed, end_packed, end_right = lax.optimization_barrier(
        (rising, falling, met, near_other, far_other, packed, end_packed, end_right)
    )
    rising_two = lax.ppermute(rising, "col", [(1, 2), (2, 3)])
    falling_two = lax.ppermute(falling, "col", [(2, 1), (1, 0)])
    outer_far = lax.ppermute(own_far, "col", inward)
    outer_far, end_right = lax.optimization_barrier((outer_far, end_right))
    end_right = lax.ppermute(end_right, "col", inward)
    met_pair, rising_pair, falling_pair = paired(met), paired(rising), paired(falling)
    outer_other = swapped(outer_far)
    end_rest = jnp.concatenate([flat(right_own[cut:]), flat(met[cut:])])

    rising_two, falling_two, outer_far, outer_other, end_right, end_rest = lax.optimization_barrier(
        (rising_two, falling_two, outer_far, outer_other, end_right, end_rest)
    )
    rising_three = lax.ppermute(rising_two, "col", [(2, 3)])
    falling_three = lax.ppermute(falling_two, "col", [(1, 0)])
    crossed = lax.ppermute(jnp.concatenate([own_far, outer_far]), "col", across)
    end_met = lax.ppermute(end_right, "row", [(0, 1), (1, 0)])
    end_rest = lax.ppermute(end_rest, "col", inward)
    end_pair = paired(end_right)

    rights = []
    for nearer, farther, stride in ((right_own, met, 0), (right_pair, met_pair, part * rows)):
        for first, size in ((0, cut), (cut, part - cut)):
            rights += [(value, first * rows, size * rows, stride) for value in (nearer, farther)]
    panels = [
        [(own_near, 0, 0), (near_other, 0, 0)],
        [(rising, 0, 0), (rising_pair, 0, near_size)],
        [(falling, 0, 0), (falling_pair, 0, near_size)],
    ]
    classes = [0, jnp.where(place > 0, 3, -1), jnp.where(place < 3, 1, -1)]
    total = product_sums(packed, classes, layer, shape, [(panels, near)], rights, None, half, False)

    crossed, end_met, end_rest, end_pair, total = lax.optimization_barrier(
        (crossed, end_met, end_rest, end_pair, total)
    )
    crossed_other, end_met_other, end_rest_other = swapped(crossed), swapped(end_met), swapped(end_rest)
    far_panels = [
        [(own_far, 0, 0), (far_other, 0, 0)],
        [(outer_far, 0, 0), (outer_other, 0, 0)],
        [(crossed, 0, 0), (crossed_other, 0, 0)],
        [(crossed, far_size, 0), (crossed_other, far_size, 0)],
    ]
    rest = 2 * (part - cut) * rows
    end_rights = [
        (end_right, 0, cut * rows, 0),
        (end_met, 0, cut * rows, 0),
        (end_rest, 0, rest, 0),
        (end_pair, 0, cut * rows, cut * rows),
        (end_met_other, 0, cut * rows, 0),
        (end_rest_other, 0, rest, 0),
    ]
    classes = [jnp.where(high, 3, 1), 0, 2, jnp.where(high, 1, 3)]
    classes = [jnp.where(inner, kind, -1) for kind in classes]
    end_rows = product_sums(
        end_packed, classes, layer, shape, [(far_panels, far)], end_rights, None, half, True
    )

    two = jnp.where(place > 1, rising_two, falling_two)
    two_pair = paired(two)
    end_rows, total, rising_three, falling_three = lax.optimization_barrier(
        (end_rows, total, rising_three, falling_three)
    )
    received = lax.ppermute(end_rows, "col", outward)
    three = jnp.where(place > 1, rising_three, falling_three)
    near_panels = [
        [(two, 0, 0), (two_pair, 0, near_size)],
        [(three, 0, 0), (swapped(three), 0, 0)],
    ]
    classes = [2, jnp.where(place == 3, 1, jnp.where(place == 0, 3, -1))]
    far_classes = [0, jnp.where(high, 1, 3), jnp.where(high, 3, 1), 2]
    classes += [jnp.where(inner, kind, -1) for kind in far_classes]
    groups = [(near_panels, near), (far_panels, far)]
    block = product_sums(packed, classes, layer, shape, groups, rights, total, half, True)
    return place_rows(~inner, block, received, near)[None, None, None]


def local(left_blocks, right_blocks, triples):
    step_count = triples.shape[3]
    row_count, columns = lax.axis_size("row"), lax.axis_size("col")
    half = (2 * step_count - 2 + row_count) // row_count * NBQ // 2
    if columns >= step_count:
        return ring(left_blocks, right_blocks, triples, half)
    assert columns == 4 and row_count == 2
    return line(left_blocks, right_blocks, triples, half)


def solution(mesh):
    return jax.shard_map(
        local,
        mesh=mesh,
        in_specs=(
            P(("grp", "row"), "col", "dep", None, None, None),
            P(("grp", "row"), "col", "dep", None, None, None),
            P(("grp", "row"), "col", "dep", None, None, None),
        ),
        out_specs=P(("grp", "row"), "col", "dep", None, None, None),
        check_vma=False,
    )
```

```python
import functools

import jax
import jax.numpy as jnp
from jax import lax
from jax.experimental import pallas as pl
from jax.experimental.pallas import tpu as pltpu
from jax.sharding import PartitionSpec as P

NBQ = 32
NEAR = 0.75
DIRECT = 0.65


def chosen_products(packed, classes, panels, todo, shape, unroll, spare):
    step_count, columns, slots = shape
    count = jnp.int32(0)
    for panel in range(panels):
        kind = classes[panel]
        for extra in range(-(-step_count // columns)):
            step = lax.rem(kind + step_count // 2, columns) + extra * columns
            groups = jnp.where((kind >= 0) & (step < step_count), slots // 8, 0)
            for layer in range(2):
                base = (layer * step_count + step) * slots

                def keep(group, count):
                    for lane in range(8):
                        entry = packed[base + group * 8 + lane]
                        todo[count] = entry + (panel * 2 * slots << 10)
                        count += (entry >= 0).astype(jnp.int32)
                    return count

                count = lax.fori_loop(0, groups, keep, count)
    for extra in range(unroll - 1):
        todo[count + extra] = jnp.int32(spare)
    return count


def add_chosen(todo, count, left, right, work, unroll):
    rows, width = work.shape[1:]

    def several(group, carry):
        entries = [todo[group * unroll + lane] for lane in range(unroll)]
        products = []
        for entry in entries:
            first = pl.multiple_of(((entry >> 10) & 1023) * rows, rows)
            second = pl.multiple_of((entry >> 20) * width, width)
            products.append(
                jnp.dot(left[pl.ds(first, rows)], right[pl.ds(second, width)], preferred_element_type=jnp.float32)
            )
        for entry, product in zip(entries, products):
            work[entry & 1023] += product
        return carry

    lax.fori_loop(0, (count + unroll - 1) // unroll, several, jnp.int32(0))


def sum_kernel(groups, right_spans, has_given, shape, half, operand_count, layer_at, *refs):
    packed, classes, refs = refs[0], refs[1], refs[2:]
    operands, refs = refs[:operand_count], refs[operand_count:]
    out, refs = refs[0], refs[1:]
    works, lefts = refs[: len(groups)], refs[len(groups) : 2 * len(groups)]
    right, todo, sems, out_sem = refs[2 * len(groups) :]
    slots = shape[2]
    other = 1 - classes[layer_at]
    copies = []

    def plan(source, target, when):
        copies.append((pltpu.make_async_copy(source, target, sems.at[len(copies)]), when))

    any_class = classes[0]
    for at in range(1, layer_at):
        any_class = jnp.maximum(any_class, classes[at])
    start = 0
    for operand, first, size, gathered in right_spans:
        if gathered:
            first = pl.multiple_of(first + other * gathered, 16)
        plan(operands[operand].at[pl.ds(first, size)], right.at[pl.ds(start, size)], any_class >= 0)
        start += size
    class_at = 0
    for (panels, rows), left in zip(groups, lefts):
        start, size = 0, slots * rows
        for panel, pieces in enumerate(panels):
            for operand, first, gathered in pieces:
                if gathered:
                    first = pl.multiple_of(first + other * gathered, 16)
                source = operands[operand].at[pl.ds(first, size)]
                plan(source, left.at[pl.ds(start, size)], classes[class_at + panel] >= 0)
                start += size
        class_at += len(panels)
    if has_given:
        plan(operands[operand_count - 1], works[0], None)
    for copy, when in copies:
        copy.start() if when is None else pl.when(when)(copy.start)
    for index, work in enumerate(works):
        if index > 0 or not has_given:
            work[...] = jnp.zeros_like(work)

    class_at = 0
    for index, ((panels, rows), work, left) in enumerate(zip(groups, works, lefts)):
        unroll = 16 if rows <= 64 else 8
        kinds = [classes[class_at + panel] for panel in range(len(panels))]
        class_at += len(panels)
        count = chosen_products(packed, kinds, len(panels), todo, shape, unroll, half)
        if index == 0:
            for copy, when in copies:
                copy.wait() if when is None else pl.when(when)(copy.wait)
        add_chosen(todo, count, left, right, work, unroll)
    if out.dtype == works[0].dtype:
        copy = pltpu.make_async_copy(works[0], out, out_sem)
        copy.start()
        copy.wait()
    else:
        start = 0
        for (panels, rows), work in zip(groups, works):
            out[:, start : start + rows] = work[:half].astype(out.dtype)
            start += rows


def flat(value):
    return value.reshape(-1, value.shape[-1])


def product_sums(packed, classes, layer, shape, groups, rights, given, half, finished):
    step_count, columns, slots = shape
    width = rights[0][0].shape[-1]
    operands, known = [], []

    def number(value):
        for index, other in enumerate(known):
            if other is value:
                return index
        known.append(value)
        operands.append(flat(value))
        return len(operands) - 1

    right_spans = [(number(value), first, size, gathered) for value, first, size, gathered in rights]
    numbered = [
        ([[(number(value), first, gathered) for value, first, gathered in panel] for panel in panels], rows)
        for panels, rows in groups
    ]
    if given is not None:
        operands.append(given)
    right_rows = sum(span[2] for span in rights)
    most = max(len(panels) for panels, _ in groups)
    assert right_rows <= 1024 * width and most * 2 * slots <= 1024 and half < 1024 and slots % 8 == 0
    anywhere = pl.BlockSpec(memory_space=pl.ANY)
    in_scalar = pl.BlockSpec(memory_space=pltpu.SMEM)
    all_rows = sum(rows for _, rows in groups)
    out_shape = (
        jax.ShapeDtypeStruct((half, all_rows, width), jnp.bfloat16)
        if finished
        else jax.ShapeDtypeStruct((half + 1, all_rows, width), jnp.float32)
    )
    copy_count = len(rights) + sum(len(panel) for panels, _ in groups for panel in panels) + 1
    scratch_bytes = 4 * (half + 1) * all_rows * width + 2 * right_rows * width
    scratch_bytes += sum(4 * len(panels) * slots * rows * width for panels, rows in groups)
    scratch_bytes += 2 * half * all_rows * width if finished else 0
    scalars = jnp.stack([jnp.asarray(value, jnp.int32) for value in [*classes, layer]])
    return pl.pallas_call(
        functools.partial(
            sum_kernel, numbered, right_spans, given is not None, shape, half, len(operands), len(classes)
        ),
        out_shape=out_shape,
        in_specs=[in_scalar, in_scalar] + [anywhere] * len(operands),
        out_specs=pl.BlockSpec(memory_space=pltpu.VMEM) if finished else anywhere,
        scratch_shapes=[pltpu.VMEM((half + 1, rows, width), jnp.float32) for _, rows in groups]
        + [pltpu.VMEM((len(panels) * 2 * slots * rows, width), jnp.bfloat16) for panels, rows in groups]
        + [
            pltpu.VMEM((right_rows, width), jnp.bfloat16),
            pltpu.SMEM((most * 4 * slots + 16,), jnp.int32),
            pltpu.SemaphoreType.DMA((copy_count,)),
            pltpu.SemaphoreType.DMA,
        ],
        compiler_params=pltpu.CompilerParams(vmem_limit_bytes=scratch_bytes + (6 << 20)),
        cost_estimate=pl.CostEstimate(flops=1, bytes_accessed=1, transcendentals=0),
    )(packed, scalars, *operands)


def place_rows_kernel(first, takes, block, received, out, sem):
    del block

    @pl.when(takes[0] > 0)
    def _():
        copy = pltpu.make_async_copy(received, out.at[:, pl.ds(first, received.shape[1])], sem)
        copy.start()
        copy.wait()


def place_rows(takes, block, received, first):
    anywhere = pl.BlockSpec(memory_space=pl.ANY)
    return pl.pallas_call(
        functools.partial(place_rows_kernel, first),
        out_shape=jax.ShapeDtypeStruct(block.shape, block.dtype),
        in_specs=[pl.BlockSpec(memory_space=pltpu.SMEM), anywhere, pl.BlockSpec(memory_space=pltpu.VMEM)],
        out_specs=anywhere,
        scratch_shapes=[pltpu.SemaphoreType.DMA],
        input_output_aliases={1: 0},
    )(takes.astype(jnp.int32).reshape(1), block, received)


def swapped(value):
    return lax.ppermute(value, "dep", [(0, 1), (1, 0)])


def paired(value):
    return lax.all_gather(value, "dep", axis=0, tiled=True)


def packed_lists(both, layer, half, right_place):
    step_count, _, slots = both.shape[1:]
    both = jnp.where(layer > 0, both[::-1], both)
    result = both[:, :, 2] - layer * half
    wanted = (result >= 0) & (result < half)
    layers = jnp.arange(2, dtype=jnp.int32)[:, None, None]
    packed = right_place(both[:, :, 1], layers) << 20 | (layers * slots + both[:, :, 0]) << 10 | result
    return jnp.where(wanted, packed, -1).reshape(-1)


def ring(left_blocks, right_blocks, triples, half):
    own, right_own, step_lists = left_blocks[0, 0, 0], right_blocks[0, 0, 0], triples[0, 0, 0]
    slots, rows = own.shape[0], own.shape[1]
    columns, layer = lax.axis_size("col"), lax.axis_index("dep")
    gathered = lax.all_gather(right_own, "row", axis=0, tiled=True)
    right_slots = gathered.shape[0]
    both = lax.all_gather(step_lists, "dep")
    packed = packed_lists(both, layer, half, lambda slot, layers: layers * right_slots + slot)
    rights = [(value, 0, right_slots * rows, 0) for value in (gathered, swapped(gathered))]
    shape = (step_lists.shape[0], columns, slots)
    rising, falling, total = own, own, None
    size = slots * rows
    panels, classes = [[(own, 0, 0), (paired(own), 0, size)]], [0]
    reach = step_lists.shape[0] // 2
    for distance in range(1, reach + 1):
        rising = lax.ppermute(rising, "col", [(i, (i + 1) % columns) for i in range(columns)])
        falling = lax.ppermute(falling, "col", [(i, (i - 1) % columns) for i in range(columns)])
        panels += [[(value, 0, 0), (paired(value), 0, size)] for value in (rising, falling)]
        classes += [columns - distance, distance]
        total = product_sums(
            packed, classes, layer, shape, [(panels, rows)], rights, total, half, distance == reach
        )
        panels, classes = [], []
    return total[None, None, None]


def line(left_blocks, right_blocks, triples, half):
    own, right_own, step_lists = left_blocks[0, 0, 0], right_blocks[0, 0, 0], triples[0, 0, 0]
    slots, rows, part = own.shape[0], own.shape[1], right_own.shape[0]
    columns, layer, place = lax.axis_size("col"), lax.axis_index("dep"), lax.axis_index("col")
    shape = (step_lists.shape[0], columns, slots)
    near = int(rows * NEAR) // 16 * 16
    far = rows - near
    cut = int(part * DIRECT)
    up, down = [(0, 1), (1, 2), (2, 3)], [(1, 0), (2, 1), (3, 2)]
    inward, across, outward = [(0, 1), (3, 2)], [(1, 2), (2, 1)], [(2, 3), (1, 0)]
    high, inner = place == 2, (place == 1) | (place == 2)

    own_near, own_far = own[:, :near], flat(own[:, near:])
    near_size, far_size = slots * near, slots * far
    met = lax.ppermute(right_own, "row", [(0, 1), (1, 0)])
    rising = lax.ppermute(own_near, "col", up)
    falling = lax.ppermute(own_near, "col", down)
    near_other, far_other = swapped(own_near), swapped(own_far)
    both = lax.all_gather(step_lists, "dep")
    right_pair = paired(right_own)

    def right_place(slot, layers):
        farther, within = (slot // part) ^ lax.axis_index("row"), slot % part
        first = jnp.where(within < cut, farther * cut + within, 2 * cut + farther * (part - cut) + within - cut)
        return layers * 2 * part + first

    packed = packed_lists(both, layer, half, right_place)
    end_right = right_own[:cut]

    rising, falling, met, near_other, far_other, packed, end_right = lax.optimization_barrier(
        (rising, falling, met, near_other, far_other, packed, end_right)
    )
    rising_two = lax.ppermute(rising, "col", [(1, 2), (2, 3)])
    falling_two = lax.ppermute(falling, "col", [(2, 1), (1, 0)])
    outer_far = lax.ppermute(own_far, "col", inward)
    end_right = lax.ppermute(end_right, "col", inward)
    end_packed = lax.ppermute(packed, "col", inward)
    met_pair = paired(met)
    rising, falling, token = lax.optimization_barrier((rising, falling, swapped(packed)))
    hop_pair = paired(jnp.concatenate([flat(rising), flat(falling)]))
    end_rest = jnp.concatenate([flat(right_own[cut:]), flat(met[cut:])])

    rising_two, falling_two, outer_far, end_right, end_rest, end_packed = lax.optimization_barrier(
        (rising_two, falling_two, outer_far, end_right, end_rest, end_packed)
    )
    rising_three = lax.ppermute(rising_two, "col", [(2, 3)])
    falling_three = lax.ppermute(falling_two, "col", [(1, 0)])
    crossing = jnp.concatenate([own_far, outer_far])
    crossing, end_right, end_rest, outer_far = lax.optimization_barrier((crossing, end_right, end_rest, outer_far))
    crossed = lax.ppermute(crossing, "col", across)
    end_met = lax.ppermute(end_right, "row", [(0, 1), (1, 0)])
    end_rest = lax.ppermute(end_rest, "col", inward)
    outer_pair, end_pair = paired(outer_far), paired(end_right)

    rights = []
    for nearer, farther, stride in ((right_own, met, 0), (right_pair, met_pair, part * rows)):
        for first, size in ((0, cut), (cut, part - cut)):
            rights += [(value, first * rows, size * rows, stride) for value in (nearer, farther)]
    panels = [
        [(own_near, 0, 0), (near_other, 0, 0)],
        [(rising, 0, 0), (hop_pair, 0, 2 * near_size)],
        [(falling, 0, 0), (hop_pair, near_size, 2 * near_size)],
    ]
    classes = [0, jnp.where(place > 0, 3, -1), jnp.where(place < 3, 1, -1)]
    known_layer = jnp.where(token[0] < -1, 2, layer)
    total = product_sums(packed, classes, known_layer, shape, [(panels, near)], rights, None, half, False)

    crossed, end_met, end_rest, outer_pair, end_pair, total = lax.optimization_barrier(
        (crossed, end_met, end_rest, outer_pair, end_pair, total)
    )
    crossed_other, end_met_other, end_rest_other = swapped(crossed), swapped(end_met), swapped(end_rest)
    far_panels = [
        [(own_far, 0, 0), (far_other, 0, 0)],
        [(outer_far, 0, 0), (outer_pair, 0, far_size)],
        [(crossed, 0, 0), (crossed_other, 0, 0)],
        [(crossed, far_size, 0), (crossed_other, far_size, 0)],
    ]
    rest = 2 * (part - cut) * rows
    end_rights = [
        (end_right, 0, cut * rows, 0),
        (end_met, 0, cut * rows, 0),
        (end_rest, 0, rest, 0),
        (end_pair, 0, cut * rows, cut * rows),
        (end_met_other, 0, cut * rows, 0),
        (end_rest_other, 0, rest, 0),
    ]
    classes = [jnp.where(high, 3, 1), 0, 2, jnp.where(high, 1, 3)]
    classes = [jnp.where(inner, kind, -1) for kind in classes]
    end_rows = product_sums(
        end_packed, classes, layer, shape, [(far_panels, far)], end_rights, None, half, True
    )

    rising_pair, falling_pair = paired(rising_two), paired(falling_two)
    end_rows, total, rising_three, falling_three = lax.optimization_barrier(
        (end_rows, total, rising_three, falling_three)
    )
    received = lax.ppermute(end_rows, "col", outward)
    near_panels = [
        [(rising_two, 0, 0), (rising_pair, 0, near_size)],
        [(falling_two, 0, 0), (falling_pair, 0, near_size)],
        [(rising_three, 0, 0), (swapped(rising_three), 0, 0)],
        [(falling_three, 0, 0), (swapped(falling_three), 0, 0)],
    ]
    classes = [jnp.where(place > 1, 2, -1), jnp.where(place < 2, 2, -1)]
    classes += [jnp.where(place == 3, 1, -1), jnp.where(place == 0, 3, -1)]
    far_classes = [0, jnp.where(high, 1, 3), jnp.where(high, 3, 1), 2]
    classes += [jnp.where(inner, kind, -1) for kind in far_classes]
    groups = [(near_panels, near), (far_panels, far)]
    block = product_sums(packed, classes, layer, shape, groups, rights, total, half, True)
    return place_rows(~inner, block, received, near)[None, None, None]


def local(left_blocks, right_blocks, triples):
    step_count = triples.shape[3]
    row_count, columns = lax.axis_size("row"), lax.axis_size("col")
    half = (2 * step_count - 2 + row_count) // row_count * NBQ // 2
    if columns >= step_count:
        return ring(left_blocks, right_blocks, triples, half)
    assert columns == 4 and row_count == 2
    return line(left_blocks, right_blocks, triples, half)


def solution(mesh):
    return jax.shard_map(
        local,
        mesh=mesh,
        in_specs=(
            P(("grp", "row"), "col", "dep", None, None, None),
            P(("grp", "row"), "col", "dep", None, None, None),
            P(("grp", "row"), "col", "dep", None, None, None),
        ),
        out_specs=P(("grp", "row"), "col", "dep", None, None, None),
        check_vma=False,
    )
```

```python
import functools

import jax
import jax.numpy as jnp
from jax import lax
from jax.experimental import pallas as pl
from jax.experimental.pallas import tpu as pltpu
from jax.sharding import PartitionSpec as P

NBQ = 32
UNROLL = 8


def chosen_products(packed, classes, panels, todo, shape, layers, spare):
    step_count, columns, slots = shape
    count = jnp.int32(0)
    for panel in range(panels):
        kind = classes[panel]
        for extra in range(-(-step_count // columns)):
            step = lax.rem(kind + step_count // 2, columns) + extra * columns
            groups = jnp.where((kind >= 0) & (step < step_count), slots // 8, 0)
            for layer in range(layers):
                base = (layer * step_count + step) * slots

                def keep(group, count):
                    for lane in range(8):
                        entry = packed[base + group * 8 + lane]
                        todo[count] = entry + (panel * layers * slots << 10)
                        count += (entry >= 0).astype(jnp.int32)
                    return count

                count = lax.fori_loop(0, groups, keep, count)
    for extra in range(UNROLL - 1):
        todo[count + extra] = jnp.int32(spare)
    return count


def add_chosen(todo, count, left, right, work):
    def several(group, carry):
        entries = [todo[group * UNROLL + lane] for lane in range(UNROLL)]
        products = [
            jnp.dot(left[(entry >> 10) & 1023], right[entry >> 20], preferred_element_type=jnp.float32)
            for entry in entries
        ]
        for entry, product in zip(entries, products):
            work[entry & 1023] += product
        return carry

    lax.fori_loop(0, (count + UNROLL - 1) // UNROLL, several, jnp.int32(0))


def sum_kernel(panels, rights, givens, saved, shape, layers, operand_count, layer_at, *refs):
    packed, classes, refs = refs[0], refs[1], refs[2:]
    operands, refs = refs[:operand_count], refs[operand_count:]
    outs, refs = refs[: max(len(saved), 1)], refs[max(len(saved), 1) :]
    work, left, right, todo, sems = refs
    spare = work.shape[0] - 1
    other = 1 - classes[layer_at]
    copies = []

    def plan(source, target, when=None):
        copies.append((pltpu.make_async_copy(source, target, sems.at[len(copies)]), when))

    start = 0
    for operand, size, gathered in rights:
        source = operands[operand]
        if gathered:
            source = source.at[pl.ds(other * size, size)]
        plan(source, right.at[pl.ds(start, size)])
        start += size
    start = 0
    for panel, pieces in enumerate(panels):
        for operand, size, gathered in pieces:
            source = operands[operand]
            if gathered:
                source = source.at[pl.ds(other * size, size)]
            plan(source, left.at[pl.ds(start, size)], classes[panel] >= 0)
            start += size
    start = 0
    for operand, size in givens:
        plan(operands[operand], work.at[pl.ds(start, size)])
        start += size
    for copy, when in copies:
        copy.start() if when is None else pl.when(when)(copy.start)
    if givens:
        work[spare] = jnp.zeros_like(work[spare])
    else:
        work[...] = jnp.zeros_like(work)
    kinds = [classes[panel] for panel in range(len(panels))]
    count = chosen_products(packed, kinds, len(panels), todo, shape, layers, spare)
    for copy, when in copies:
        copy.wait() if when is None else pl.when(when)(copy.wait)
    add_chosen(todo, count, left, right, work)
    if saved:
        start, copies = 0, []
        for out, size in zip(outs, saved):
            copies.append(pltpu.make_async_copy(work.at[pl.ds(start, size)], out, sems.at[len(copies)]))
            start += size
        for copy in copies:
            copy.start()
        for copy in copies:
            copy.wait()
    else:
        outs[0][...] = work[:spare].astype(outs[0].dtype)


def product_sums(packed, classes, layer, shape, layers, panels, rights, givens, result_slots, saved):
    step_count, columns, slots = shape
    rows, width = rights[0][0].shape[1:]
    operands = []

    def number(value):
        for index, known in enumerate(operands):
            if known is value:
                return index
        operands.append(value)
        return len(operands) - 1

    def spans(pieces):
        return [
            (number(value), value.shape[0] // 2 if gathered else value.shape[0], gathered)
            for value, gathered in pieces
        ]

    right_spans = spans(rights)
    panel_spans = [spans(pieces) for pieces in panels]
    given_spans = [(number(value), value.shape[0]) for value in givens]
    right_slots = sum(size for _, size, _ in right_spans)
    left_slots = len(panels) * layers * slots
    assert right_slots <= 1024 and left_slots <= 1024 and result_slots < 1024 and slots % 8 == 0
    assert all(sum(size for _, size, _ in pieces) == layers * slots for pieces in panel_spans)
    anywhere = pl.BlockSpec(memory_space=pl.ANY)
    in_scalar = pl.BlockSpec(memory_space=pltpu.SMEM)
    copy_count = len(rights) + sum(len(pieces) for pieces in panels) + len(givens) + len(saved)
    scalars = jnp.stack([jnp.asarray(value, jnp.int32) for value in [*classes, layer]])
    if saved:
        out_shape = [jax.ShapeDtypeStruct((size, rows, width), jnp.float32) for size in saved]
    else:
        out_shape = [jax.ShapeDtypeStruct((result_slots, rows, width), jnp.bfloat16)]
    return pl.pallas_call(
        functools.partial(
            sum_kernel, panel_spans, right_spans, given_spans, saved, shape, layers, len(operands), len(classes)
        ),
        out_shape=out_shape,
        in_specs=[in_scalar, in_scalar] + [anywhere] * len(operands),
        out_specs=[anywhere if saved else pl.BlockSpec(memory_space=pltpu.VMEM)] * len(out_shape),
        scratch_shapes=[
            pltpu.VMEM((result_slots + 1, rows, width), jnp.float32),
            pltpu.VMEM((left_slots, rows, width), jnp.bfloat16),
            pltpu.VMEM((right_slots, width, width), jnp.bfloat16),
            pltpu.SMEM((len(panels) * -(-step_count // columns) * layers * slots + UNROLL,), jnp.int32),
            pltpu.SemaphoreType.DMA((copy_count,)),
        ],
        compiler_params=pltpu.CompilerParams(vmem_limit_bytes=56 << 20),
        cost_estimate=pl.CostEstimate(flops=1, bytes_accessed=1, transcendentals=0),
    )(packed, scalars, *operands)


def swapped(value):
    return lax.ppermute(value, "dep", [(0, 1), (1, 0)])


def paired(value):
    return lax.all_gather(value, "dep", axis=0, tiled=True)


def kept_products(both, layer, half, right_slot):
    both = jnp.where(layer > 0, both[::-1], both)
    slots = both.shape[3]
    result = both[:, :, 2] - layer * half
    wanted = (result >= 0) & (result < half)
    layers = jnp.arange(2, dtype=jnp.int32)[:, None, None]
    packed = right_slot(both[:, :, 1], layers) << 20 | (layers * slots + both[:, :, 0]) << 10 | result
    return jnp.where(wanted, packed, -1).reshape(-1)


def layer_products(step_lists, layer, half, right_slot):
    result = step_lists[:, 2]
    turned = (result + layer * half) % (2 * half)
    packed = right_slot(step_lists[:, 1], 0) << 20 | step_lists[:, 0] << 10 | turned
    return jnp.where(result < 2 * half, packed, -1).reshape(-1)


def ring(left_blocks, right_blocks, triples, half):
    own, right_own, step_lists = left_blocks[0, 0, 0], right_blocks[0, 0, 0], triples[0, 0, 0]
    columns, layer = lax.axis_size("col"), lax.axis_index("dep")
    gathered = lax.all_gather(right_own, "row", axis=0, tiled=True)
    right_slots = gathered.shape[0]
    both = lax.all_gather(step_lists, "dep")
    packed = kept_products(both, layer, half, lambda slot, layers: layers * right_slots + slot)
    rights = [(gathered, False), (swapped(gathered), False)]
    shape = (step_lists.shape[0], columns, own.shape[0])
    rising, falling, total = own, own, []
    panels, classes = [[(own, False), (paired(own), True)]], [0]
    reach = step_lists.shape[0] // 2
    for distance in range(1, reach + 1):
        rising = lax.ppermute(rising, "col", [(i, (i + 1) % columns) for i in range(columns)])
        falling = lax.ppermute(falling, "col", [(i, (i - 1) % columns) for i in range(columns)])
        panels += [[(value, False), (paired(value), True)] for value in (rising, falling)]
        classes += [columns - distance, distance]
        saved = [] if distance == reach else [half]
        total = product_sums(packed, classes, layer, shape, 2, panels, rights, total, half, saved)
        panels, classes = [], []
    return total[0][None, None, None]


def line(left_blocks, right_blocks, triples, half):
    own, right_own, step_lists = left_blocks[0, 0, 0], right_blocks[0, 0, 0], triples[0, 0, 0]
    slots, part = own.shape[0], right_own.shape[0]
    columns, layer, place = lax.axis_size("col"), lax.axis_index("dep"), lax.axis_index("col")
    shape = (step_lists.shape[0], columns, slots)
    pieces = [own[: slots // 2], own[slots // 2 :]]
    fence = lax.optimization_barrier

    def hop(values, pairs):
        return [lax.ppermute(value, "col", pairs) for value in values]

    def right_slot(slot, layers):
        return (layers * 2 + ((slot // part) ^ lax.axis_index("row"))) * part + slot % part

    rising = hop(pieces, [(0, 1), (1, 2), (2, 3)])
    falling = hop(pieces, [(1, 0), (2, 1), (3, 2)])
    met = lax.ppermute(right_own, "row", [(0, 1), (1, 0)])
    both = lax.all_gather(step_lists, "dep")
    kept = kept_products(both, layer, half, right_slot)
    listed = layer_products(step_lists, layer, half, right_slot)
    right_pair = paired(right_own)

    rising[0], falling[0] = fence((rising[0], falling[0]))
    rising_two = hop(rising[:1], [(1, 2), (2, 3)])
    falling_two = hop(falling[:1], [(1, 0), (2, 1)])
    rising[1], falling[1], met, kept, listed = fence((rising[1], falling[1], met, kept, listed))
    rising_two += hop(rising[1:], [(1, 2), (2, 3)])
    falling_two += hop(falling[1:], [(1, 0), (2, 1)])
    met_pair = paired(met)
    rights = [(right_own, False), (met, False)]
    panels = [[(value, False) for value in values] for values in (pieces, rising, falling)]
    classes = [0, jnp.where(place > 0, 3, -1), jnp.where(place < 3, 1, -1)]
    sums = product_sums(listed, classes, layer, shape, 1, panels, rights, [], 2 * half, [half, half])

    rising_two[0], falling_two[0], sums = fence((rising_two[0], falling_two[0], sums))
    rising_three = hop(rising_two[:1], [(2, 3)])
    falling_three = hop(falling_two[:1], [(1, 0)])
    rising_two[1], falling_two[1] = fence((rising_two[1], falling_two[1]))
    rising_three += hop(rising_two[1:], [(2, 3)])
    falling_three += hop(falling_two[1:], [(1, 0)])
    panels = [[(value, False) for value in values] for values in (rising_two, falling_two)]
    classes = [jnp.where(place > 1, 2, -1), jnp.where(place < 2, 2, -1)]
    sums = product_sums(listed, classes, layer, shape, 1, panels, rights, sums, 2 * half, [half, half])
    total = sums[0] + swapped(sums[1])

    rising_three, falling_three, total = fence((rising_three, falling_three, total))
    panels = [
        [(value, False) for value in [*values, *[swapped(value) for value in values]]]
        for values in (rising_three, falling_three)
    ]
    classes = [jnp.where(place == 3, 1, -1), jnp.where(place == 0, 3, -1)]
    rights += [(right_pair, True), (met_pair, True)]
    return product_sums(kept, classes, layer, shape, 2, panels, rights, [total], half, [])[0][None, None, None]


def local(left_blocks, right_blocks, triples):
    step_count = triples.shape[3]
    row_count, columns = lax.axis_size("row"), lax.axis_size("col")
    half = (2 * step_count - 2 + row_count) // row_count * NBQ // 2
    if columns >= step_count:
        return ring(left_blocks, right_blocks, triples, half)
    assert columns == 4 and row_count == 2
    return line(left_blocks, right_blocks, triples, half)


def solution(mesh):
    return jax.shard_map(
        local,
        mesh=mesh,
        in_specs=(
            P(("grp", "row"), "col", "dep", None, None, None),
            P(("grp", "row"), "col", "dep", None, None, None),
            P(("grp", "row"), "col", "dep", None, None, None),
        ),
        out_specs=P(("grp", "row"), "col", "dep", None, None, None),
        check_vma=False,
    )
```

```python
import functools

import jax
import jax.numpy as jnp
from jax import lax
from jax.experimental import pallas as pl
from jax.experimental.pallas import tpu as pltpu
from jax.sharding import PartitionSpec as P

NBQ = 32
UNROLL = 8


def chosen_products(packed, classes, panels, todo, shape, layers, spare):
    step_count, columns, slots = shape
    count = jnp.int32(0)
    for panel in range(panels):
        kind = classes[panel]
        for extra in range(-(-step_count // columns)):
            step = lax.rem(kind + step_count // 2, columns) + extra * columns
            groups = jnp.where((kind >= 0) & (step < step_count), slots // 8, 0)
            for layer in range(layers):
                base = (layer * step_count + step) * slots

                def keep(group, count):
                    for lane in range(8):
                        entry = packed[base + group * 8 + lane]
                        todo[count] = entry + (panel * layers * slots << 10)
                        count += (entry >= 0).astype(jnp.int32)
                    return count

                count = lax.fori_loop(0, groups, keep, count)
    for extra in range(UNROLL - 1):
        todo[count + extra] = jnp.int32(spare)
    return count


def add_chosen(todo, count, left, right, work):
    def several(group, carry):
        entries = [todo[group * UNROLL + lane] for lane in range(UNROLL)]
        products = [
            jnp.dot(left[(entry >> 10) & 1023], right[entry >> 20], preferred_element_type=jnp.float32)
            for entry in entries
        ]
        for entry, product in zip(entries, products):
            work[entry & 1023] += product
        return carry

    lax.fori_loop(0, (count + UNROLL - 1) // UNROLL, several, jnp.int32(0))


def sum_kernel(panels, rights, givens, saved, shape, layers, operand_count, layer_at, *refs):
    packed, classes, refs = refs[0], refs[1], refs[2:]
    operands, refs = refs[:operand_count], refs[operand_count:]
    outs, refs = refs[: max(len(saved), 1)], refs[max(len(saved), 1) :]
    work, left, right, todo, sems = refs
    spare = work.shape[0] - 1
    other = 1 - classes[layer_at]
    copies = []

    def plan(source, target, when=None):
        copies.append((pltpu.make_async_copy(source, target, sems.at[len(copies)]), when))

    start = 0
    for operand, size, gathered in rights:
        source = operands[operand]
        if gathered:
            source = source.at[pl.ds(other * size, size)]
        plan(source, right.at[pl.ds(start, size)])
        start += size
    start = 0
    for panel, pieces in enumerate(panels):
        for operand, size, gathered in pieces:
            source = operands[operand]
            if gathered:
                source = source.at[pl.ds(other * size, size)]
            plan(source, left.at[pl.ds(start, size)], classes[panel] >= 0)
            start += size
    start = 0
    for operand, size in givens:
        plan(operands[operand], work.at[pl.ds(start, size)])
        start += size
    for copy, when in copies:
        copy.start() if when is None else pl.when(when)(copy.start)
    if givens:
        work[spare] = jnp.zeros_like(work[spare])
    else:
        work[...] = jnp.zeros_like(work)
    kinds = [classes[panel] for panel in range(len(panels))]
    count = chosen_products(packed, kinds, len(panels), todo, shape, layers, spare)
    for copy, when in copies:
        copy.wait() if when is None else pl.when(when)(copy.wait)
    add_chosen(todo, count, left, right, work)
    if saved:
        start, copies = 0, []
        for out, size in zip(outs, saved):
            copies.append(pltpu.make_async_copy(work.at[pl.ds(start, size)], out, sems.at[len(copies)]))
            start += size
        for copy in copies:
            copy.start()
        for copy in copies:
            copy.wait()
    else:
        outs[0][...] = work[:spare].astype(outs[0].dtype)


def product_sums(packed, classes, layer, shape, layers, panels, rights, givens, result_slots, saved):
    step_count, columns, slots = shape
    rows, width = rights[0][0].shape[1:]
    operands = []

    def number(value):
        for index, known in enumerate(operands):
            if known is value:
                return index
        operands.append(value)
        return len(operands) - 1

    def spans(pieces):
        return [
            (number(value), value.shape[0] // 2 if gathered else value.shape[0], gathered)
            for value, gathered in pieces
        ]

    right_spans = spans(rights)
    panel_spans = [spans(pieces) for pieces in panels]
    given_spans = [(number(value), value.shape[0]) for value in givens]
    right_slots = sum(size for _, size, _ in right_spans)
    left_slots = len(panels) * layers * slots
    assert right_slots <= 1024 and left_slots <= 1024 and result_slots < 1024 and slots % 8 == 0
    assert all(sum(size for _, size, _ in pieces) == layers * slots for pieces in panel_spans)
    anywhere = pl.BlockSpec(memory_space=pl.ANY)
    in_scalar = pl.BlockSpec(memory_space=pltpu.SMEM)
    copy_count = len(rights) + sum(len(pieces) for pieces in panels) + len(givens) + len(saved)
    scalars = jnp.stack([jnp.asarray(value, jnp.int32) for value in [*classes, layer]])
    if saved:
        out_shape = [jax.ShapeDtypeStruct((size, rows, width), jnp.float32) for size in saved]
    else:
        out_shape = [jax.ShapeDtypeStruct((result_slots, rows, width), jnp.bfloat16)]
    return pl.pallas_call(
        functools.partial(
            sum_kernel, panel_spans, right_spans, given_spans, saved, shape, layers, len(operands), len(classes)
        ),
        out_shape=out_shape,
        in_specs=[in_scalar, in_scalar] + [anywhere] * len(operands),
        out_specs=[anywhere if saved else pl.BlockSpec(memory_space=pltpu.VMEM)] * len(out_shape),
        scratch_shapes=[
            pltpu.VMEM((result_slots + 1, rows, width), jnp.float32),
            pltpu.VMEM((left_slots, rows, width), jnp.bfloat16),
            pltpu.VMEM((right_slots, width, width), jnp.bfloat16),
            pltpu.SMEM((len(panels) * -(-step_count // columns) * layers * slots + UNROLL,), jnp.int32),
            pltpu.SemaphoreType.DMA((copy_count,)),
        ],
        compiler_params=pltpu.CompilerParams(vmem_limit_bytes=56 << 20),
        cost_estimate=pl.CostEstimate(flops=1, bytes_accessed=1, transcendentals=0),
    )(packed, scalars, *operands)


def swapped(value):
    return lax.ppermute(value, "dep", [(0, 1), (1, 0)])


def paired(value):
    return lax.all_gather(value, "dep", axis=0, tiled=True)


def kept_products(both, layer, half, right_slot):
    both = jnp.where(layer > 0, both[::-1], both)
    slots = both.shape[3]
    result = both[:, :, 2] - layer * half
    wanted = (result >= 0) & (result < half)
    layers = jnp.arange(2, dtype=jnp.int32)[:, None, None]
    packed = right_slot(both[:, :, 1], layers) << 20 | (layers * slots + both[:, :, 0]) << 10 | result
    return jnp.where(wanted, packed, -1).reshape(-1)


def ring(left_blocks, right_blocks, triples, half):
    own, right_own, step_lists = left_blocks[0, 0, 0], right_blocks[0, 0, 0], triples[0, 0, 0]
    columns, layer = lax.axis_size("col"), lax.axis_index("dep")
    gathered = lax.all_gather(right_own, "row", axis=0, tiled=True)
    right_slots = gathered.shape[0]
    both = lax.all_gather(step_lists, "dep")
    packed = kept_products(both, layer, half, lambda slot, layers: layers * right_slots + slot)
    rights = [(gathered, False), (swapped(gathered), False)]
    shape = (step_lists.shape[0], columns, own.shape[0])
    rising, falling, total = own, own, []
    panels, classes = [[(own, False), (paired(own), True)]], [0]
    reach = step_lists.shape[0] // 2
    for distance in range(1, reach + 1):
        rising = lax.ppermute(rising, "col", [(i, (i + 1) % columns) for i in range(columns)])
        falling = lax.ppermute(falling, "col", [(i, (i - 1) % columns) for i in range(columns)])
        panels += [[(value, False), (paired(value), True)] for value in (rising, falling)]
        classes += [columns - distance, distance]
        saved = [] if distance == reach else [half]
        total = product_sums(packed, classes, layer, shape, 2, panels, rights, total, half, saved)
        panels, classes = [], []
    return total[0][None, None, None]


def line(left_blocks, right_blocks, triples, half):
    own, right_own, step_lists = left_blocks[0, 0, 0], right_blocks[0, 0, 0], triples[0, 0, 0]
    slots, part = own.shape[0], right_own.shape[0]
    columns, layer, place = lax.axis_size("col"), lax.axis_index("dep"), lax.axis_index("col")
    shape = (step_lists.shape[0], columns, slots)
    inner = (place == 1) | (place == 2)
    low = place < 2
    outward, across, inward = [(2, 3), (1, 0)], [(1, 2), (2, 1)], [(0, 1), (3, 2)]
    fence = lax.optimization_barrier

    def hop(value, pairs):
        return lax.ppermute(value, "col", pairs)

    def right_slot(slot, layers):
        return (layers * 2 + ((slot // part) ^ lax.axis_index("row"))) * part + slot % part

    pieces = [own[: slots // 2], own[slots // 2 :]]
    outer_one = hop(own, outward)
    across_one = hop(own, across)
    inward_one = [hop(piece, inward) for piece in pieces]
    met = lax.ppermute(right_own, "row", [(0, 1), (1, 0)])
    kept = kept_products(lax.all_gather(step_lists, "dep"), layer, half, right_slot)
    right_pair, own_pair = paired(right_own), paired(own)

    outer_one, across_one, inward_one, met, kept = fence((outer_one, across_one, inward_one, met, kept))
    outer_two = hop(across_one, outward)
    across_two = [hop(piece, across) for piece in inward_one]
    met_pair = paired(met)
    one = jnp.where(inner, across_one, outer_one)
    one_pair, inward_pair = paired(one), [paired(piece) for piece in inward_one]

    across_two = fence(across_two)
    outer_three = [hop(piece, outward) for piece in across_two]
    two = jnp.where(inner, jnp.concatenate(across_two), outer_two)
    cuts = [0, slots * 3 // 8, slots * 3 // 4, slots]
    two = [two[first:last] for first, last in zip(cuts, cuts[1:])]
    rights = [(right_own, False), (met, False), (right_pair, True), (met_pair, True)]
    panels = [
        [(own, False), (own_pair, True)],
        [(one, False), (one_pair, True)],
        [(piece, False) for piece in inward_one] + [(piece, True) for piece in inward_pair],
        [(piece, False) for piece in two] + [(swapped(piece), False) for piece in two],
    ]
    classes = [0, jnp.where(low, 1, 3), jnp.where(inner, jnp.where(low, 3, 1), -1), 2]
    (total,) = product_sums(kept, classes, layer, shape, 2, panels, rights, [], half, [half])

    outer_three[0], total = fence((outer_three[0], total))
    others = [swapped(outer_three[0])]
    outer_three[1], others[0] = fence((outer_three[1], others[0]))
    others.append(swapped(outer_three[1]))
    panels = [[(piece, False) for piece in [*outer_three, *others]]]
    classes = [jnp.where(inner, -1, jnp.where(low, 3, 1))]
    return product_sums(kept, classes, layer, shape, 2, panels, rights, [total], half, [])[0][None, None, None]


def local(left_blocks, right_blocks, triples):
    step_count = triples.shape[3]
    row_count, columns = lax.axis_size("row"), lax.axis_size("col")
    half = (2 * step_count - 2 + row_count) // row_count * NBQ // 2
    if columns >= step_count:
        return ring(left_blocks, right_blocks, triples, half)
    assert columns == 4 and row_count == 2
    return line(left_blocks, right_blocks, triples, half)


def solution(mesh):
    return jax.shard_map(
        local,
        mesh=mesh,
        in_specs=(
            P(("grp", "row"), "col", "dep", None, None, None),
            P(("grp", "row"), "col", "dep", None, None, None),
            P(("grp", "row"), "col", "dep", None, None, None),
        ),
        out_specs=P(("grp", "row"), "col", "dep", None, None, None),
        check_vma=False,
    )
```

```python
import functools

import jax
import jax.numpy as jnp
from jax import lax
from jax.experimental import pallas as pl
from jax.experimental.pallas import tpu as pltpu
from jax.sharding import PartitionSpec as P

NBQ = 32
UNROLL = 8


def chosen_products(packed, classes, panels, todo, shape, layers, spare, first_left=0):
    step_count, columns, slots = shape
    count = jnp.int32(0)
    for panel in range(panels):
        kind = classes[panel]
        for extra in range(-(-step_count // columns)):
            step = lax.rem(kind + step_count // 2, columns) + extra * columns
            groups = jnp.where((kind >= 0) & (step < step_count), slots // 8, 0)
            for layer in range(layers):
                base = (layer * step_count + step) * slots

                def keep(group, count):
                    for lane in range(8):
                        entry = packed[base + group * 8 + lane]
                        todo[count] = entry + (panel * layers * slots << 10)
                        count += (entry >= 0).astype(jnp.int32)
                    return count

                count = lax.fori_loop(0, groups, keep, count)
    for extra in range(UNROLL - 1):
        todo[count + extra] = jnp.int32(first_left << 10 | spare)
    return count


def add_chosen(todo, count, left, right, work, first_left=0):
    def several(group, carry):
        entries = [todo[group * UNROLL + lane] for lane in range(UNROLL)]
        products = [
            jnp.dot(
                left[((entry >> 10) & 1023) - first_left],
                right[entry >> 20],
                preferred_element_type=jnp.float32,
            )
            for entry in entries
        ]
        for entry, product in zip(entries, products):
            work[entry & 1023] += product
        return carry

    lax.fori_loop(0, (count + UNROLL - 1) // UNROLL, several, jnp.int32(0))


def sum_kernel(panels, rights, givens, saved, resident, shape, layers, operand_count, layer_at, *refs):
    packed, classes, refs = refs[0], refs[1], refs[2:]
    operands, refs = refs[:operand_count], refs[operand_count:]
    if resident:
        (work, right), (left, todo, sems) = refs[:2], refs[2:]
    else:
        out_count = max(len(saved), 1)
        outs, (work, left, right, todo, sems) = refs[:out_count], refs[out_count:]
    spare = work.shape[0] - 1
    other = 1 - classes[layer_at]
    copies = []

    def plan(source, target, when=None):
        copies.append((pltpu.make_async_copy(source, target, sems.at[len(copies)]), when))

    start = 0
    for operand, size, gathered in rights:
        source = operands[operand]
        if gathered:
            source = source.at[pl.ds(other * size, size)]
        plan(source, right.at[pl.ds(start, size)])
        start += size
    start = 0
    for panel, pieces in enumerate(panels):
        for operand, size, gathered in pieces:
            source = operands[operand]
            if gathered:
                source = source.at[pl.ds(other * size, size)]
            plan(source, left.at[pl.ds(start, size)], classes[panel] >= 0)
            start += size
    start = 0
    for operand, size in givens:
        plan(operands[operand], work.at[pl.ds(start, size)])
        start += size
    for copy, when in copies:
        copy.start() if when is None else pl.when(when)(copy.start)
    if givens:
        work[spare] = jnp.zeros_like(work[spare])
    else:
        work[...] = jnp.zeros_like(work)
    kinds = [classes[panel] for panel in range(len(panels))]
    count = chosen_products(packed, kinds, len(panels), todo, shape, layers, spare)
    for copy, when in copies:
        copy.wait() if when is None else pl.when(when)(copy.wait)
    add_chosen(todo, count, left, right, work)
    if resident:
        return
    if saved:
        start, copies = 0, []
        for out, size in zip(outs, saved):
            copies.append(pltpu.make_async_copy(work.at[pl.ds(start, size)], out, sems.at[len(copies)]))
            start += size
        for copy in copies:
            copy.start()
        for copy in copies:
            copy.wait()
    else:
        outs[0][...] = work[:spare].astype(outs[0].dtype)


def product_sums(packed, classes, layer, shape, layers, panels, rights, givens, result_slots, saved, resident=False):
    step_count, columns, slots = shape
    rows, width = rights[0][0].shape[1:]
    operands = []

    def number(value):
        for index, known in enumerate(operands):
            if known is value:
                return index
        operands.append(value)
        return len(operands) - 1

    def spans(pieces):
        return [
            (number(value), value.shape[0] // 2 if gathered else value.shape[0], gathered)
            for value, gathered in pieces
        ]

    right_spans = spans(rights)
    panel_spans = [spans(pieces) for pieces in panels]
    given_spans = [(number(value), value.shape[0]) for value in givens]
    right_slots = sum(size for _, size, _ in right_spans)
    left_slots = len(panels) * layers * slots
    assert right_slots <= 1024 and left_slots <= 1024 and result_slots < 1024 and slots % 8 == 0
    assert all(sum(size for _, size, _ in pieces) == layers * slots for pieces in panel_spans)
    anywhere = pl.BlockSpec(memory_space=pl.ANY)
    in_scalar = pl.BlockSpec(memory_space=pltpu.SMEM)
    copy_count = len(rights) + sum(len(pieces) for pieces in panels) + len(givens) + len(saved) + 1
    scalars = jnp.stack([jnp.asarray(value, jnp.int32) for value in [*classes, layer]])
    if saved:
        out_shape = [jax.ShapeDtypeStruct((size, rows, width), jnp.float32) for size in saved]
    else:
        out_shape = [jax.ShapeDtypeStruct((result_slots, rows, width), jnp.bfloat16)]
    scratch = [
        pltpu.VMEM((result_slots + 1, rows, width), jnp.float32),
        pltpu.VMEM((left_slots, rows, width), jnp.bfloat16),
        pltpu.VMEM((right_slots, width, width), jnp.bfloat16),
    ]
    if resident:
        out_shape, scratch = [scratch[0], scratch[2]], [scratch[1]]
    return pl.pallas_call(
        functools.partial(
            sum_kernel,
            panel_spans,
            right_spans,
            given_spans,
            saved,
            resident,
            shape,
            layers,
            len(operands),
            len(classes),
        ),
        out_shape=out_shape,
        in_specs=[in_scalar, in_scalar] + [anywhere] * len(operands),
        out_specs=[anywhere if saved else pl.BlockSpec(memory_space=pltpu.VMEM)] * len(out_shape),
        scratch_shapes=scratch
        + [
            pltpu.SMEM((len(panels) * -(-step_count // columns) * layers * slots + UNROLL,), jnp.int32),
            pltpu.SemaphoreType.DMA((copy_count,)),
        ],
        compiler_params=pltpu.CompilerParams(vmem_limit_bytes=(40 if resident else 56) << 20),
        cost_estimate=pl.CostEstimate(flops=1, bytes_accessed=1, transcendentals=0),
    )(packed, scalars, *operands)


def last_kernel(shape, packed, classes, right, given, own, other, out, work, todo):
    del given
    step_count, columns, slots = shape
    spare = work.shape[0] - 1
    for layer, left in enumerate((own, other)):
        base = layer * step_count * slots
        part = packed.at[pl.ds(base, step_count * slots)]
        count = chosen_products(part, [classes[0]], 1, todo, shape, 1, spare, layer * slots)
        add_chosen(todo, count, left, right, work, layer * slots)
    out[...] = work[:spare].astype(out.dtype)


def last_sums(packed, kind, shape, own, other, right, given):
    step_count, columns, slots = shape
    result_slots, rows, width = given.shape[0] - 1, *given.shape[1:]
    in_scalar, in_vector = pl.BlockSpec(memory_space=pltpu.SMEM), pl.BlockSpec(memory_space=pltpu.VMEM)
    return pl.pallas_call(
        functools.partial(last_kernel, shape),
        out_shape=[
            jax.ShapeDtypeStruct((result_slots, rows, width), jnp.bfloat16),
            pltpu.VMEM(given.shape, given.dtype),
        ],
        in_specs=[in_scalar] * 2 + [in_vector] * 4,
        out_specs=[in_vector] * 2,
        scratch_shapes=[pltpu.SMEM((-(-step_count // columns) * slots + UNROLL,), jnp.int32)],
        input_output_aliases={3: 1},
        compiler_params=pltpu.CompilerParams(vmem_limit_bytes=20 << 20),
        cost_estimate=pl.CostEstimate(flops=1, bytes_accessed=1, transcendentals=0),
    )(packed, kind.astype(jnp.int32).reshape(1), right, given, own, other)[0]


def swapped(value):
    return lax.ppermute(value, "dep", [(0, 1), (1, 0)])


def paired(value):
    return lax.all_gather(value, "dep", axis=0, tiled=True)


def kept_products(both, layer, half, right_slot):
    both = jnp.where(layer > 0, both[::-1], both)
    slots = both.shape[3]
    result = both[:, :, 2] - layer * half
    wanted = (result >= 0) & (result < half)
    layers = jnp.arange(2, dtype=jnp.int32)[:, None, None]
    packed = right_slot(both[:, :, 1], layers) << 20 | (layers * slots + both[:, :, 0]) << 10 | result
    return jnp.where(wanted, packed, -1).reshape(-1)


def ring(left_blocks, right_blocks, triples, half):
    own, right_own, step_lists = left_blocks[0, 0, 0], right_blocks[0, 0, 0], triples[0, 0, 0]
    columns, layer = lax.axis_size("col"), lax.axis_index("dep")
    gathered = lax.all_gather(right_own, "row", axis=0, tiled=True)
    right_slots = gathered.shape[0]
    both = lax.all_gather(step_lists, "dep")
    packed = kept_products(both, layer, half, lambda slot, layers: layers * right_slots + slot)
    rights = [(gathered, False), (swapped(gathered), False)]
    shape = (step_lists.shape[0], columns, own.shape[0])
    rising, falling, total = own, own, []
    panels, classes = [[(own, False), (paired(own), True)]], [0]
    reach = step_lists.shape[0] // 2
    for distance in range(1, reach + 1):
        rising = lax.ppermute(rising, "col", [(i, (i + 1) % columns) for i in range(columns)])
        falling = lax.ppermute(falling, "col", [(i, (i - 1) % columns) for i in range(columns)])
        panels += [[(value, False), (paired(value), True)] for value in (rising, falling)]
        classes += [columns - distance, distance]
        saved = [] if distance == reach else [half]
        total = product_sums(packed, classes, layer, shape, 2, panels, rights, total, half, saved)
        panels, classes = [], []
    return total[0][None, None, None]


def line(left_blocks, right_blocks, triples, half):
    own, right_own, step_lists = left_blocks[0, 0, 0], right_blocks[0, 0, 0], triples[0, 0, 0]
    slots, part = own.shape[0], right_own.shape[0]
    columns, layer, place = lax.axis_size("col"), lax.axis_index("dep"), lax.axis_index("col")
    shape = (step_lists.shape[0], columns, slots)
    inner = (place == 1) | (place == 2)
    low = place < 2
    outward, across, inward = [(2, 3), (1, 0)], [(1, 2), (2, 1)], [(0, 1), (3, 2)]
    fence = lax.optimization_barrier

    def hop(value, pairs):
        return lax.ppermute(value, "col", pairs)

    def right_slot(slot, layers):
        return (layers * 2 + ((slot // part) ^ lax.axis_index("row"))) * part + slot % part

    across_one, inward_one, outer_one = hop(own, across), hop(own, inward), hop(own, outward)
    met = lax.ppermute(right_own, "row", [(0, 1), (1, 0)])
    kept = kept_products(lax.all_gather(step_lists, "dep"), layer, half, right_slot)
    right_pair, own_pair = paired(right_own), paired(own)

    across_one, inward_one, outer_one, met, kept = fence((across_one, inward_one, outer_one, met, kept))
    outer_two, across_two = hop(across_one, outward), hop(inward_one, across)
    met_pair, inward_pair, across_pair, outer_pair = [
        paired(value) for value in (met, inward_one, across_one, outer_one)
    ]

    across_two = fence(across_two)
    outer_three = hop(across_two, outward)
    two = jnp.where(inner, across_two, outer_two)
    two = [two[: slots // 2], two[slots // 2 :]]
    rights = [(right_own, False), (met, False), (right_pair, True), (met_pair, True)]
    panels = [
        [(own, False), (own_pair, True)],
        [(across_one, False), (across_pair, True)],
        [(inward_one, False), (inward_pair, True)],
        [(outer_one, False), (outer_pair, True)],
        [(piece, False) for piece in two] + [(swapped(piece), False) for piece in two],
    ]
    classes = [0, jnp.where(inner, jnp.where(low, 1, 3), -1), jnp.where(inner, jnp.where(low, 3, 1), -1)]
    classes += [jnp.where(inner, -1, jnp.where(low, 1, 3)), 2]
    total, right = product_sums(kept, classes, layer, shape, 2, panels, rights, [], half, [], True)

    outer_three, total, right = fence((outer_three, total, right))
    kind = jnp.where(inner, -1, jnp.where(low, 3, 1))
    block = last_sums(kept, kind, shape, outer_three, swapped(outer_three), right, total)
    return block[None, None, None]


def local(left_blocks, right_blocks, triples):
    step_count = triples.shape[3]
    row_count, columns = lax.axis_size("row"), lax.axis_size("col")
    half = (2 * step_count - 2 + row_count) // row_count * NBQ // 2
    if columns >= step_count:
        return ring(left_blocks, right_blocks, triples, half)
    assert columns == 4 and row_count == 2
    return line(left_blocks, right_blocks, triples, half)


def solution(mesh):
    return jax.shard_map(
        local,
        mesh=mesh,
        in_specs=(
            P(("grp", "row"), "col", "dep", None, None, None),
            P(("grp", "row"), "col", "dep", None, None, None),
            P(("grp", "row"), "col", "dep", None, None, None),
        ),
        out_specs=P(("grp", "row"), "col", "dep", None, None, None),
        check_vma=False,
    )
```

```python
import functools

import jax
import jax.numpy as jnp
from jax import lax
from jax.experimental import pallas as pl
from jax.experimental.pallas import tpu as pltpu
from jax.sharding import PartitionSpec as P

NBQ = 32
UNROLL = 8
PARTS = 4


def chosen_products(packed, classes, panels, todo, shape, layers, spare, first_left=0):
    step_count, columns, slots = shape
    count = jnp.int32(0)
    for panel in range(panels):
        kind = classes[panel]
        for extra in range(-(-step_count // columns)):
            step = lax.rem(kind + step_count // 2, columns) + extra * columns
            groups = jnp.where((kind >= 0) & (step < step_count), slots // 8, 0)
            for layer in range(layers):
                base = (layer * step_count + step) * slots

                def keep(group, count):
                    for lane in range(8):
                        entry = packed[base + group * 8 + lane]
                        todo[count] = entry + (panel * layers * slots << 10)
                        count += (entry >= 0).astype(jnp.int32)
                    return count

                count = lax.fori_loop(0, groups, keep, count)
    for extra in range(UNROLL - 1):
        todo[count + extra] = jnp.int32(first_left << 10 | spare)
    return count


def add_chosen(todo, count, left, right, work, first_left=0):
    def several(group, carry):
        entries = [todo[group * UNROLL + lane] for lane in range(UNROLL)]
        products = [
            jnp.dot(
                left[((entry >> 10) & 1023) - first_left],
                right[entry >> 20],
                preferred_element_type=jnp.float32,
            )
            for entry in entries
        ]
        for entry, product in zip(entries, products):
            work[entry & 1023] += product
        return carry

    lax.fori_loop(0, (count + UNROLL - 1) // UNROLL, several, jnp.int32(0))


def sum_kernel(panels, rights, givens, saved, resident, shape, layers, operand_count, layer_at, *refs):
    packed, classes, refs = refs[0], refs[1], refs[2:]
    operands, refs = refs[:operand_count], refs[operand_count:]
    if resident:
        (work, right), (left, todo, sems) = refs[:2], refs[2:]
    else:
        out_count = max(len(saved), 1)
        outs, (work, left, right, todo, sems) = refs[:out_count], refs[out_count:]
    spare = work.shape[0] - 1
    other = 1 - classes[layer_at]
    copies = []

    def plan(source, target, when=None):
        copies.append((pltpu.make_async_copy(source, target, sems.at[len(copies)]), when))

    start = 0
    for operand, size, gathered in rights:
        source = operands[operand]
        if gathered:
            source = source.at[pl.ds(other * size, size)]
        plan(source, right.at[pl.ds(start, size)])
        start += size
    start = 0
    for panel, pieces in enumerate(panels):
        for operand, size, gathered in pieces:
            source = operands[operand]
            if gathered:
                source = source.at[pl.ds(other * size, size)]
            plan(source, left.at[pl.ds(start, size)], classes[panel] >= 0)
            start += size
    start = 0
    for operand, size in givens:
        plan(operands[operand], work.at[pl.ds(start, size)])
        start += size
    for copy, when in copies:
        copy.start() if when is None else pl.when(when)(copy.start)
    if givens:
        work[spare] = jnp.zeros_like(work[spare])
    else:
        work[...] = jnp.zeros_like(work)
    kinds = [classes[panel] for panel in range(len(panels))]
    count = chosen_products(packed, kinds, len(panels), todo, shape, layers, spare)
    for copy, when in copies:
        copy.wait() if when is None else pl.when(when)(copy.wait)
    add_chosen(todo, count, left, right, work)
    if resident:
        return
    if saved:
        start, copies = 0, []
        for out, size in zip(outs, saved):
            copies.append(pltpu.make_async_copy(work.at[pl.ds(start, size)], out, sems.at[len(copies)]))
            start += size
        for copy in copies:
            copy.start()
        for copy in copies:
            copy.wait()
    else:
        outs[0][...] = work[:spare].astype(outs[0].dtype)


def product_sums(packed, scalars, shape, layers, panels, rights, givens, result_slots, saved, resident=False):
    step_count, columns, slots = shape
    rows, width = rights[0][0].shape[1:]
    operands = []

    def number(value):
        for index, known in enumerate(operands):
            if known is value:
                return index
        operands.append(value)
        return len(operands) - 1

    def spans(pieces):
        return [
            (number(value), value.shape[0] // 2 if gathered else value.shape[0], gathered)
            for value, gathered in pieces
        ]

    right_spans = spans(rights)
    panel_spans = [spans(pieces) for pieces in panels]
    given_spans = [(number(value), value.shape[0]) for value in givens]
    right_slots = sum(size for _, size, _ in right_spans)
    left_slots = len(panels) * layers * slots
    assert right_slots <= 1024 and left_slots <= 1024 and result_slots < 1024 and slots % 8 == 0
    assert all(sum(size for _, size, _ in pieces) == layers * slots for pieces in panel_spans)
    anywhere = pl.BlockSpec(memory_space=pl.ANY)
    in_scalar = pl.BlockSpec(memory_space=pltpu.SMEM)
    copy_count = len(rights) + sum(len(pieces) for pieces in panels) + len(givens) + len(saved) + 1
    if saved:
        out_shape = [jax.ShapeDtypeStruct((size, rows, width), jnp.float32) for size in saved]
    else:
        out_shape = [jax.ShapeDtypeStruct((result_slots, rows, width), jnp.bfloat16)]
    scratch = [
        pltpu.VMEM((result_slots + 1, rows, width), jnp.float32),
        pltpu.VMEM((left_slots, rows, width), jnp.bfloat16),
        pltpu.VMEM((right_slots, width, width), jnp.bfloat16),
    ]
    if resident:
        out_shape, scratch = [scratch[0], scratch[2]], [scratch[1]]
    return pl.pallas_call(
        functools.partial(
            sum_kernel,
            panel_spans,
            right_spans,
            given_spans,
            saved,
            resident,
            shape,
            layers,
            len(operands),
            len(panels),
        ),
        out_shape=out_shape,
        in_specs=[in_scalar, in_scalar] + [anywhere] * len(operands),
        out_specs=[anywhere if saved else pl.BlockSpec(memory_space=pltpu.VMEM)] * len(out_shape),
        scratch_shapes=scratch
        + [
            pltpu.SMEM((len(panels) * -(-step_count // columns) * layers * slots + UNROLL,), jnp.int32),
            pltpu.SemaphoreType.DMA((copy_count,)),
        ],
        compiler_params=pltpu.CompilerParams(vmem_limit_bytes=(40 if resident else 56) << 20),
        cost_estimate=pl.CostEstimate(flops=1, bytes_accessed=1, transcendentals=0),
    )(packed, scalars, *operands)


def panel_kernel(shape, layer, kind_at, finish, packed, scalars, right, given, left, *refs):
    del given
    step_count, columns, slots = shape
    work, todo = (refs[1], refs[2]) if finish else (refs[0], refs[1])
    spare, first = work.shape[0] - 1, layer * slots
    part = packed.at[pl.ds(layer * step_count * slots, step_count * slots)]
    count = chosen_products(part, [scalars[kind_at]], 1, todo, shape, 1, spare, first)
    add_chosen(todo, count, left, right, work, first)
    if finish:
        out, rounded, sems = refs[0], refs[3], refs[4]
        size = spare // PARTS
        copies = []
        for index in range(PARTS):
            span = pl.ds(index * size, size if index < PARTS - 1 else spare - index * size)
            rounded[span] = work[span].astype(rounded.dtype)
            copies.append(pltpu.make_async_copy(rounded.at[span], out.at[span], sems.at[index]))
            copies[-1].start()
        for copy in copies:
            copy.wait()


def add_panel(packed, scalars, kind_at, shape, layer, panel, right, given, finish):
    step_count, columns, slots = shape
    result_slots, rows, width = given.shape[0] - 1, *given.shape[1:]
    in_scalar, in_vector = pl.BlockSpec(memory_space=pltpu.SMEM), pl.BlockSpec(memory_space=pltpu.VMEM)
    out_shape, out_specs = [pltpu.VMEM(given.shape, given.dtype)], [in_vector]
    scratch = [pltpu.SMEM((-(-step_count // columns) * slots + UNROLL,), jnp.int32)]
    if finish:
        out_shape.insert(0, jax.ShapeDtypeStruct((result_slots, rows, width), jnp.bfloat16))
        out_specs.insert(0, pl.BlockSpec(memory_space=pl.ANY))
        scratch.append(pltpu.VMEM((result_slots, rows, width), jnp.bfloat16))
        scratch.append(pltpu.SemaphoreType.DMA((PARTS,)))
    return pl.pallas_call(
        functools.partial(panel_kernel, shape, layer, kind_at, finish),
        out_shape=out_shape,
        in_specs=[in_scalar] * 2 + [in_vector] * 3,
        out_specs=out_specs,
        scratch_shapes=scratch,
        input_output_aliases={3: len(out_shape) - 1},
        compiler_params=pltpu.CompilerParams(vmem_limit_bytes=12 << 20),
        cost_estimate=pl.CostEstimate(flops=1, bytes_accessed=1, transcendentals=0),
    )(packed, scalars, right, given, panel)[0]


def scalar_list(*values):
    return jnp.stack([jnp.asarray(value, jnp.int32) for value in values])


def swapped(value):
    return lax.ppermute(value, "dep", [(0, 1), (1, 0)])


def paired(value):
    return lax.all_gather(value, "dep", axis=0, tiled=True)


def kept_products(both, layer, half, right_slot):
    both = jnp.where(layer > 0, both[::-1], both)
    slots = both.shape[3]
    result = both[:, :, 2] - layer * half
    wanted = (result >= 0) & (result < half)
    layers = jnp.arange(2, dtype=jnp.int32)[:, None, None]
    packed = right_slot(both[:, :, 1], layers) << 20 | (layers * slots + both[:, :, 0]) << 10 | result
    return jnp.where(wanted, packed, -1).reshape(-1)


def ring(left_blocks, right_blocks, triples, half):
    own, right_own, step_lists = left_blocks[0, 0, 0], right_blocks[0, 0, 0], triples[0, 0, 0]
    columns, layer = lax.axis_size("col"), lax.axis_index("dep")
    gathered = lax.all_gather(right_own, "row", axis=0, tiled=True)
    right_slots = gathered.shape[0]
    both = lax.all_gather(step_lists, "dep")
    packed = kept_products(both, layer, half, lambda slot, layers: layers * right_slots + slot)
    rights = [(gathered, False), (swapped(gathered), False)]
    shape = (step_lists.shape[0], columns, own.shape[0])
    rising, falling, total = own, own, []
    panels, classes = [[(own, False), (paired(own), True)]], [0]
    reach = step_lists.shape[0] // 2
    for distance in range(1, reach + 1):
        rising = lax.ppermute(rising, "col", [(i, (i + 1) % columns) for i in range(columns)])
        falling = lax.ppermute(falling, "col", [(i, (i - 1) % columns) for i in range(columns)])
        panels += [[(value, False), (paired(value), True)] for value in (rising, falling)]
        classes += [columns - distance, distance]
        saved = [] if distance == reach else [half]
        scalars = scalar_list(*classes, layer)
        total = product_sums(packed, scalars, shape, 2, panels, rights, total, half, saved)
        panels, classes = [], []
    return total[0][None, None, None]


def line(left_blocks, right_blocks, triples, half):
    own, right_own, step_lists = left_blocks[0, 0, 0], right_blocks[0, 0, 0], triples[0, 0, 0]
    slots, part = own.shape[0], right_own.shape[0]
    columns, layer, place = lax.axis_size("col"), lax.axis_index("dep"), lax.axis_index("col")
    shape = (step_lists.shape[0], columns, slots)
    inner = (place == 1) | (place == 2)
    low = place < 2
    outward, across, inward = [(2, 3), (1, 0)], [(1, 2), (2, 1)], [(0, 1), (3, 2)]
    fence = lax.optimization_barrier

    def hop(value, pairs):
        return lax.ppermute(value, "col", pairs)

    def right_slot(slot, layers):
        return (layers * 2 + ((slot // part) ^ lax.axis_index("row"))) * part + slot % part

    outer_one, inward_one, across_one = hop(own, outward), hop(own, inward), hop(own, across)
    met = lax.ppermute(right_own, "row", [(0, 1), (1, 0)])
    kept = kept_products(lax.all_gather(step_lists, "dep"), layer, half, right_slot)
    right_pair, own_pair = paired(right_own), paired(own)

    across_one, inward_one, outer_one, met, kept = fence((across_one, inward_one, outer_one, met, kept))
    outer_two, across_two = hop(across_one, outward), hop(inward_one, across)
    met_pair, inward_pair, across_pair, outer_pair = [
        paired(value) for value in (met, inward_one, across_one, outer_one)
    ]

    across_two = fence(across_two)
    outer_three = hop(across_two, outward)
    two = jnp.where(inner, across_two, outer_two)
    two = [two[: slots // 2], two[slots // 2 :]]
    rights = [(right_own, False), (met, False), (right_pair, True), (met_pair, True)]
    panels = [
        [(own, False), (own_pair, True)],
        [(outer_one, False), (outer_pair, True)],
        [(inward_one, False), (inward_pair, True)],
        [(across_one, False), (across_pair, True)],
        [(piece, False) for piece in two] + [(swapped(piece), False) for piece in two],
    ]
    classes = [0, jnp.where(inner, -1, jnp.where(low, 1, 3)), jnp.where(inner, jnp.where(low, 3, 1), -1)]
    classes += [jnp.where(inner, jnp.where(low, 1, 3), -1), 2]
    scalars = scalar_list(*classes, layer, jnp.where(inner, -1, jnp.where(low, 3, 1)))
    total, right = product_sums(kept, scalars, shape, 2, panels, rights, [], half, [], True)

    outer_three, total, right = fence((outer_three, total, right))
    kind_at = len(classes) + 1
    total = add_panel(kept, scalars, kind_at, shape, 0, outer_three, right, total, False)
    block = add_panel(kept, scalars, kind_at, shape, 1, swapped(outer_three), right, total, True)
    return block[None, None, None]


def local(left_blocks, right_blocks, triples):
    step_count = triples.shape[3]
    row_count, columns = lax.axis_size("row"), lax.axis_size("col")
    half = (2 * step_count - 2 + row_count) // row_count * NBQ // 2
    if columns >= step_count:
        return ring(left_blocks, right_blocks, triples, half)
    assert columns == 4 and row_count == 2
    return line(left_blocks, right_blocks, triples, half)


def solution(mesh):
    return jax.shard_map(
        local,
        mesh=mesh,
        in_specs=(
            P(("grp", "row"), "col", "dep", None, None, None),
            P(("grp", "row"), "col", "dep", None, None, None),
            P(("grp", "row"), "col", "dep", None, None, None),
        ),
        out_specs=P(("grp", "row"), "col", "dep", None, None, None),
        check_vma=False,
    )
```

```python
import functools

import jax
import jax.numpy as jnp
from jax import lax
from jax.experimental import pallas as pl
from jax.experimental.pallas import tpu as pltpu
from jax.sharding import PartitionSpec as P

NBQ = 32
UNROLL = 8
PARTS = 4


def chosen_products(packed, classes, panels, todo, shape, layers, spare, first_left=0):
    step_count, columns, slots = shape
    count = jnp.int32(0)
    for panel in range(panels):
        kind = classes[panel]
        for extra in range(-(-step_count // columns)):
            step = lax.rem(kind + step_count // 2, columns) + extra * columns
            groups = jnp.where((kind >= 0) & (step < step_count), slots // 8, 0)
            for layer in range(layers):
                base = (layer * step_count + step) * slots

                def keep(group, count):
                    for lane in range(8):
                        entry = packed[base + group * 8 + lane]
                        todo[count] = entry + (panel * layers * slots << 10)
                        count += (entry >= 0).astype(jnp.int32)
                    return count

                count = lax.fori_loop(0, groups, keep, count)
    for extra in range(UNROLL - 1):
        todo[count + extra] = jnp.int32(first_left << 10 | spare)
    return count


def add_chosen(todo, count, left, right, work, first_left=0):
    def several(group, carry):
        entries = [todo[group * UNROLL + lane] for lane in range(UNROLL)]
        products = [
            jnp.dot(
                left[((entry >> 10) & 1023) - first_left],
                right[entry >> 20],
                preferred_element_type=jnp.float32,
            )
            for entry in entries
        ]
        for entry, product in zip(entries, products):
            work[entry & 1023] += product
        return carry

    lax.fori_loop(0, (count + UNROLL - 1) // UNROLL, several, jnp.int32(0))


def sum_kernel(panels, rights, givens, saved, resident, shape, layers, operand_count, layer_at, *refs):
    packed, classes, refs = refs[0], refs[1], refs[2:]
    operands, refs = refs[:operand_count], refs[operand_count:]
    if resident:
        (work, right), (left, todo, sems) = refs[:2], refs[2:]
    else:
        out_count = max(len(saved), 1)
        outs, (work, left, right, todo, sems) = refs[:out_count], refs[out_count:]
    spare = work.shape[0] - 1
    other = 1 - classes[layer_at]
    copies = []

    def plan(source, target, when=None):
        copies.append((pltpu.make_async_copy(source, target, sems.at[len(copies)]), when))

    start = 0
    for operand, size, gathered in rights:
        source = operands[operand]
        if gathered:
            source = source.at[pl.ds(other * size, size)]
        plan(source, right.at[pl.ds(start, size)])
        start += size
    start = 0
    for panel, pieces in enumerate(panels):
        for operand, size, gathered in pieces:
            source = operands[operand]
            if gathered:
                source = source.at[pl.ds(other * size, size)]
            plan(source, left.at[pl.ds(start, size)], classes[panel] >= 0)
            start += size
    start = 0
    for operand, size in givens:
        plan(operands[operand], work.at[pl.ds(start, size)])
        start += size
    for copy, when in copies:
        copy.start() if when is None else pl.when(when)(copy.start)
    if givens:
        work[spare] = jnp.zeros_like(work[spare])
    else:
        work[...] = jnp.zeros_like(work)
    kinds = [classes[panel] for panel in range(len(panels))]
    count = chosen_products(packed, kinds, len(panels), todo, shape, layers, spare)
    for copy, when in copies:
        copy.wait() if when is None else pl.when(when)(copy.wait)
    add_chosen(todo, count, left, right, work)
    if resident:
        return
    if saved:
        start, copies = 0, []
        for out, size in zip(outs, saved):
            copies.append(pltpu.make_async_copy(work.at[pl.ds(start, size)], out, sems.at[len(copies)]))
            start += size
        for copy in copies:
            copy.start()
        for copy in copies:
            copy.wait()
    else:
        outs[0][...] = work[:spare].astype(outs[0].dtype)


def product_sums(packed, scalars, shape, layers, panels, rights, givens, result_slots, saved, resident=False):
    step_count, columns, slots = shape
    rows, width = rights[0][0].shape[1:]
    operands = []

    def number(value):
        for index, known in enumerate(operands):
            if known is value:
                return index
        operands.append(value)
        return len(operands) - 1

    def spans(pieces):
        return [
            (number(value), value.shape[0] // 2 if gathered else value.shape[0], gathered)
            for value, gathered in pieces
        ]

    right_spans = spans(rights)
    panel_spans = [spans(pieces) for pieces in panels]
    given_spans = [(number(value), value.shape[0]) for value in givens]
    right_slots = sum(size for _, size, _ in right_spans)
    left_slots = len(panels) * layers * slots
    assert right_slots <= 1024 and left_slots <= 1024 and result_slots < 1024 and slots % 8 == 0
    assert all(sum(size for _, size, _ in pieces) == layers * slots for pieces in panel_spans)
    anywhere = pl.BlockSpec(memory_space=pl.ANY)
    in_scalar = pl.BlockSpec(memory_space=pltpu.SMEM)
    copy_count = len(rights) + sum(len(pieces) for pieces in panels) + len(givens) + len(saved) + 1
    if saved:
        out_shape = [jax.ShapeDtypeStruct((size, rows, width), jnp.float32) for size in saved]
    else:
        out_shape = [jax.ShapeDtypeStruct((result_slots, rows, width), jnp.bfloat16)]
    scratch = [
        pltpu.VMEM((result_slots + 1, rows, width), jnp.float32),
        pltpu.VMEM((left_slots, rows, width), jnp.bfloat16),
        pltpu.VMEM((right_slots, width, width), jnp.bfloat16),
    ]
    if resident:
        out_shape, scratch = [scratch[0], scratch[2]], [scratch[1]]
    return pl.pallas_call(
        functools.partial(
            sum_kernel,
            panel_spans,
            right_spans,
            given_spans,
            saved,
            resident,
            shape,
            layers,
            len(operands),
            len(panels),
        ),
        out_shape=out_shape,
        in_specs=[in_scalar, in_scalar] + [anywhere] * len(operands),
        out_specs=[anywhere if saved else pl.BlockSpec(memory_space=pltpu.VMEM)] * len(out_shape),
        scratch_shapes=scratch
        + [
            pltpu.SMEM((len(panels) * -(-step_count // columns) * layers * slots + UNROLL,), jnp.int32),
            pltpu.SemaphoreType.DMA((copy_count,)),
        ],
        compiler_params=pltpu.CompilerParams(vmem_limit_bytes=(40 if resident else 56) << 20),
        cost_estimate=pl.CostEstimate(flops=1, bytes_accessed=1, transcendentals=0),
    )(packed, scalars, *operands)


def panel_kernel(shape, layer, kind_at, finish, packed, scalars, right, given, left, *refs):
    del given
    step_count, columns, slots = shape
    work, todo = (refs[1], refs[2]) if finish else (refs[0], refs[1])
    spare, first = work.shape[0] - 1, layer * slots
    part = packed.at[pl.ds(layer * step_count * slots, step_count * slots)]
    count = chosen_products(part, [scalars[kind_at]], 1, todo, shape, 1, spare, first)
    add_chosen(todo, count, left, right, work, first)
    if finish:
        out, rounded, sems = refs[0], refs[3], refs[4]
        size = spare // PARTS
        copies = []
        for index in range(PARTS):
            span = pl.ds(index * size, size if index < PARTS - 1 else spare - index * size)
            rounded[span] = work[span].astype(rounded.dtype)
            copies.append(pltpu.make_async_copy(rounded.at[span], out.at[span], sems.at[index]))
            copies[-1].start()
        for copy in copies:
            copy.wait()


def add_panel(packed, scalars, kind_at, shape, layer, panel, right, given, finish):
    step_count, columns, slots = shape
    result_slots, rows, width = given.shape[0] - 1, *given.shape[1:]
    in_scalar, in_vector = pl.BlockSpec(memory_space=pltpu.SMEM), pl.BlockSpec(memory_space=pltpu.VMEM)
    out_shape, out_specs = [pltpu.VMEM(given.shape, given.dtype)], [in_vector]
    scratch = [pltpu.SMEM((-(-step_count // columns) * slots + UNROLL,), jnp.int32)]
    if finish:
        out_shape.insert(0, jax.ShapeDtypeStruct((result_slots, rows, width), jnp.bfloat16))
        out_specs.insert(0, pl.BlockSpec(memory_space=pl.ANY))
        scratch.append(pltpu.VMEM((result_slots, rows, width), jnp.bfloat16))
        scratch.append(pltpu.SemaphoreType.DMA((PARTS,)))
    return pl.pallas_call(
        functools.partial(panel_kernel, shape, layer, kind_at, finish),
        out_shape=out_shape,
        in_specs=[in_scalar] * 2 + [in_vector] * 3,
        out_specs=out_specs,
        scratch_shapes=scratch,
        input_output_aliases={3: len(out_shape) - 1},
        compiler_params=pltpu.CompilerParams(vmem_limit_bytes=12 << 20),
        cost_estimate=pl.CostEstimate(flops=1, bytes_accessed=1, transcendentals=0),
    )(packed, scalars, right, given, panel)[0]


def scalar_list(*values):
    return jnp.stack([jnp.asarray(value, jnp.int32) for value in values])


def swapped(value):
    return lax.ppermute(value, "dep", [(0, 1), (1, 0)])


def paired(value):
    return lax.all_gather(value, "dep", axis=0, tiled=True)


def kept_products(both, layer, half, right_slot):
    both = jnp.where(layer > 0, both[::-1], both)
    slots = both.shape[3]
    result = both[:, :, 2] - layer * half
    wanted = (result >= 0) & (result < half)
    layers = jnp.arange(2, dtype=jnp.int32)[:, None, None]
    packed = right_slot(both[:, :, 1], layers) << 20 | (layers * slots + both[:, :, 0]) << 10 | result
    return jnp.where(wanted, packed, -1).reshape(-1)


def ring(left_blocks, right_blocks, triples, half):
    own, right_own, step_lists = left_blocks[0, 0, 0], right_blocks[0, 0, 0], triples[0, 0, 0]
    columns, layer = lax.axis_size("col"), lax.axis_index("dep")
    gathered = lax.all_gather(right_own, "row", axis=0, tiled=True)
    right_slots = gathered.shape[0]
    both = lax.all_gather(step_lists, "dep")
    packed = kept_products(both, layer, half, lambda slot, layers: layers * right_slots + slot)
    rights = [(gathered, False), (swapped(gathered), False)]
    shape = (step_lists.shape[0], columns, own.shape[0])
    rising, falling, total = own, own, []
    panels, classes = [[(own, False), (paired(own), True)]], [0]
    reach = step_lists.shape[0] // 2
    for distance in range(1, reach + 1):
        rising = lax.ppermute(rising, "col", [(i, (i + 1) % columns) for i in range(columns)])
        falling = lax.ppermute(falling, "col", [(i, (i - 1) % columns) for i in range(columns)])
        panels += [[(value, False), (paired(value), True)] for value in (rising, falling)]
        classes += [columns - distance, distance]
        saved = [] if distance == reach else [half]
        scalars = scalar_list(*classes, layer)
        total = product_sums(packed, scalars, shape, 2, panels, rights, total, half, saved)
        panels, classes = [], []
    return total[0][None, None, None]


def line(left_blocks, right_blocks, triples, half):
    own, right_own, step_lists = left_blocks[0, 0, 0], right_blocks[0, 0, 0], triples[0, 0, 0]
    slots, part = own.shape[0], right_own.shape[0]
    columns, layer, place = lax.axis_size("col"), lax.axis_index("dep"), lax.axis_index("col")
    shape = (step_lists.shape[0], columns, slots)
    inner = (place == 1) | (place == 2)
    low = place < 2
    outward, across, inward = [(2, 3), (1, 0)], [(1, 2), (2, 1)], [(0, 1), (3, 2)]
    fence = lax.optimization_barrier

    def hop(value, pairs):
        return lax.ppermute(value, "col", pairs)

    def right_slot(slot, layers):
        return (layers * 2 + ((slot // part) ^ lax.axis_index("row"))) * part + slot % part

    outer_one, inward_one, across_one = hop(own, outward), hop(own, inward), hop(own, across)
    met = lax.ppermute(right_own, "row", [(0, 1), (1, 0)])
    kept = kept_products(lax.all_gather(step_lists, "dep"), layer, half, right_slot)
    right_pair, own_pair = paired(right_own), paired(own)

    outer_one, inward_one, across_one, met, kept = fence((outer_one, inward_one, across_one, met, kept))
    outer_two, across_two = hop(across_one, outward), hop(inward_one, across)
    met_pair, inward_pair, across_pair, outer_pair = [
        paired(value) for value in (met, inward_one, across_one, outer_one)
    ]

    across_two = fence(across_two)
    outer_three = hop(across_two, outward)
    two = jnp.where(inner, across_two, outer_two)
    two = [two[: slots // 2], two[slots // 2 :]]
    rights = [(right_own, False), (met, False), (right_pair, True), (met_pair, True)]
    panels = [
        [(own, False), (own_pair, True)],
        [(outer_one, False), (outer_pair, True)],
        [(inward_one, False), (inward_pair, True)],
        [(across_one, False), (across_pair, True)],
        [(piece, False) for piece in two] + [(swapped(piece), False) for piece in two],
    ]
    classes = [0, jnp.where(inner, -1, jnp.where(low, 1, 3)), jnp.where(inner, jnp.where(low, 3, 1), -1)]
    classes += [jnp.where(inner, jnp.where(low, 1, 3), -1), 2]
    scalars = scalar_list(*classes, layer, jnp.where(inner, -1, jnp.where(low, 3, 1)))
    total, right = product_sums(kept, scalars, shape, 2, panels, rights, [], half, [], True)

    outer_three, total, right = fence((outer_three, total, right))
    kind_at = len(classes) + 1
    total = add_panel(kept, scalars, kind_at, shape, 0, outer_three, right, total, False)
    block = add_panel(kept, scalars, kind_at, shape, 1, swapped(outer_three), right, total, True)
    return block[None, None, None]


def local(left_blocks, right_blocks, triples):
    step_count = triples.shape[3]
    row_count, columns = lax.axis_size("row"), lax.axis_size("col")
    half = (2 * step_count - 2 + row_count) // row_count * NBQ // 2
    if columns >= step_count:
        return ring(left_blocks, right_blocks, triples, half)
    assert columns == 4 and row_count == 2
    return line(left_blocks, right_blocks, triples, half)


def solution(mesh):
    return jax.shard_map(
        local,
        mesh=mesh,
        in_specs=(
            P(("grp", "row"), "col", "dep", None, None, None),
            P(("grp", "row"), "col", "dep", None, None, None),
            P(("grp", "row"), "col", "dep", None, None, None),
        ),
        out_specs=P(("grp", "row"), "col", "dep", None, None, None),
        check_vma=False,
    )
```

```python
import functools

import jax
import jax.numpy as jnp
from jax import lax
from jax.experimental import pallas as pl
from jax.experimental.pallas import tpu as pltpu
from jax.sharding import PartitionSpec as P

NBQ = 32
UNROLL = 8
PARTS = 4


def chosen_products(packed, classes, panels, todo, shape, layers, spare, first_left=0):
    step_count, columns, slots = shape
    count = jnp.int32(0)
    for panel in range(panels):
        kind = classes[panel]
        for extra in range(-(-step_count // columns)):
            step = lax.rem(kind + step_count // 2, columns) + extra * columns
            groups = jnp.where((kind >= 0) & (step < step_count), slots // 8, 0)
            for layer in range(layers):
                base = (layer * step_count + step) * slots

                def keep(group, count):
                    for lane in range(8):
                        entry = packed[base + group * 8 + lane]
                        todo[count] = entry + (panel * layers * slots << 10)
                        count += (entry >= 0).astype(jnp.int32)
                    return count

                count = lax.fori_loop(0, groups, keep, count)
    for extra in range(UNROLL - 1):
        todo[count + extra] = jnp.int32(first_left << 10 | spare)
    return count


def add_chosen(todo, count, left, right, work, first_left=0):
    def several(group, carry):
        entries = [todo[group * UNROLL + lane] for lane in range(UNROLL)]
        products = [
            jnp.dot(
                left[((entry >> 10) & 1023) - first_left],
                right[entry >> 20],
                preferred_element_type=jnp.float32,
            )
            for entry in entries
        ]
        for entry, product in zip(entries, products):
            work[entry & 1023] += product
        return carry

    lax.fori_loop(0, (count + UNROLL - 1) // UNROLL, several, jnp.int32(0))


def sum_kernel(panels, rights, givens, saved, mode, shape, layers, operand_count, layer_at, *refs):
    packed, classes, refs = refs[0], refs[1], refs[2:]
    operands, refs = refs[:operand_count], refs[operand_count:]
    out_count = max(len(saved), 1)
    outs, refs = refs[:out_count], refs[out_count:]
    if mode == "split":
        (right, kept), (work, left, todo, sems) = refs[:2], refs[2:]
    else:
        work, left, right, todo, sems = refs
    spare = work.shape[0] - 1
    other = 1 - classes[layer_at]
    copies = []

    def plan(source, target, when=None):
        copies.append((pltpu.make_async_copy(source, target, sems.at[len(copies)]), when))

    start = 0
    for operand, size, gathered in rights:
        source = operands[operand]
        if gathered:
            source = source.at[pl.ds(other * size, size)]
        plan(source, right.at[pl.ds(start, size)])
        start += size
    start = 0
    for panel, pieces in enumerate(panels):
        for operand, size, gathered in pieces:
            source = operands[operand]
            if gathered:
                source = source.at[pl.ds(other * size, size)]
            plan(source, left.at[pl.ds(start, size)], classes[panel] >= 0)
            start += size
    start = 0
    for operand, size in givens:
        plan(operands[operand], work.at[pl.ds(start, size)])
        start += size
    for copy, when in copies:
        copy.start() if when is None else pl.when(when)(copy.start)
    if givens:
        work[spare] = jnp.zeros_like(work[spare])
    else:
        work[...] = jnp.zeros_like(work)
    kinds = [classes[panel] for panel in range(len(panels))]
    count = chosen_products(packed, kinds, len(panels), todo, shape, layers, spare)
    for copy, when in copies:
        copy.wait() if when is None else pl.when(when)(copy.wait)
    add_chosen(todo, count, left, right, work)
    if not saved:
        outs[0][...] = work[:spare].astype(outs[0].dtype)
        return
    start, copies, targets = 0, [], list(outs)
    if mode == "split":
        kept[kept.shape[0] - 1] = jnp.zeros(kept.shape[1:], kept.dtype)
        targets.insert(0, kept.at[pl.ds(0, kept.shape[0] - 1)])
    for out in targets:
        size = out.shape[0]
        copies.append(pltpu.make_async_copy(work.at[pl.ds(start, size)], out, sems.at[len(copies)]))
        start += size
    for copy in copies:
        copy.start()
    for copy in copies:
        copy.wait()


def product_sums(packed, scalars, shape, layers, panels, rights, givens, result_slots, saved, mode="whole"):
    step_count, columns, slots = shape
    rows, width = rights[0][0].shape[1:]
    operands = []

    def number(value):
        for index, known in enumerate(operands):
            if known is value:
                return index
        operands.append(value)
        return len(operands) - 1

    def spans(pieces):
        return [
            (number(value), value.shape[0] // 2 if gathered else value.shape[0], gathered)
            for value, gathered in pieces
        ]

    right_spans = spans(rights)
    panel_spans = [spans(pieces) for pieces in panels]
    given_spans = [(number(value), value.shape[0]) for value in givens]
    right_slots = sum(size for _, size, _ in right_spans)
    left_slots = len(panels) * layers * slots
    assert right_slots <= 1024 and left_slots <= 1024 and result_slots < 1024 and slots % 8 == 0
    assert all(sum(size for _, size, _ in pieces) == layers * slots for pieces in panel_spans)
    anywhere = pl.BlockSpec(memory_space=pl.ANY)
    in_scalar, in_vector = pl.BlockSpec(memory_space=pltpu.SMEM), pl.BlockSpec(memory_space=pltpu.VMEM)
    copy_count = len(rights) + sum(len(pieces) for pieces in panels) + len(givens) + len(saved) + 1
    scratch = [
        pltpu.VMEM((result_slots + 1, rows, width), jnp.float32),
        pltpu.VMEM((left_slots, rows, width), jnp.bfloat16),
        pltpu.VMEM((right_slots, width, width), jnp.bfloat16),
    ]
    if saved:
        out_shape = [jax.ShapeDtypeStruct((size, rows, width), jnp.float32) for size in saved]
    else:
        out_shape = [jax.ShapeDtypeStruct((result_slots, rows, width), jnp.bfloat16)]
    out_specs = [anywhere if saved else in_vector] * len(out_shape)
    if mode == "split":
        out_shape += [scratch.pop(), pltpu.VMEM((result_slots - sum(saved) + 1, rows, width), jnp.float32)]
        out_specs += [in_vector] * 2
    return pl.pallas_call(
        functools.partial(
            sum_kernel,
            panel_spans,
            right_spans,
            given_spans,
            saved,
            mode,
            shape,
            layers,
            len(operands),
            len(panels),
        ),
        out_shape=out_shape,
        in_specs=[in_scalar, in_scalar] + [anywhere] * len(operands),
        out_specs=out_specs,
        scratch_shapes=scratch
        + [
            pltpu.SMEM((len(panels) * -(-step_count // columns) * layers * slots + UNROLL,), jnp.int32),
            pltpu.SemaphoreType.DMA((copy_count,)),
        ],
        compiler_params=pltpu.CompilerParams(vmem_limit_bytes=(34 if mode == "split" else 56) << 20),
        cost_estimate=pl.CostEstimate(flops=1, bytes_accessed=1, transcendentals=0),
    )(packed, scalars, *operands)


def received_kernel(given, *refs):
    del given
    work, start = refs[-1], 0
    for piece in refs[:-1]:
        span = pl.ds(start, piece.shape[0])
        work[span] += piece[...]
        start += piece.shape[0]


def add_received(given, pieces):
    in_vector = pl.BlockSpec(memory_space=pltpu.VMEM)
    return pl.pallas_call(
        received_kernel,
        out_shape=pltpu.VMEM(given.shape, given.dtype),
        in_specs=[in_vector] * (1 + len(pieces)),
        out_specs=in_vector,
        input_output_aliases={0: 0},
        compiler_params=pltpu.CompilerParams(vmem_limit_bytes=12 << 20),
        cost_estimate=pl.CostEstimate(flops=1, bytes_accessed=1, transcendentals=0),
    )(given, *pieces)


def panel_kernel(shape, layer, kind_at, finish, packed, scalars, right, given, left, *refs):
    del given
    step_count, columns, slots = shape
    work, todo = (refs[1], refs[2]) if finish else (refs[0], refs[1])
    spare, first = work.shape[0] - 1, layer * slots
    part = packed.at[pl.ds(layer * step_count * slots, step_count * slots)]
    count = chosen_products(part, [scalars[kind_at]], 1, todo, shape, 1, spare, first)
    add_chosen(todo, count, left, right, work, first)
    if finish:
        out, rounded, sems = refs[0], refs[3], refs[4]
        size = spare // PARTS
        copies = []
        for index in range(PARTS):
            span = pl.ds(index * size, size if index < PARTS - 1 else spare - index * size)
            rounded[span] = work[span].astype(rounded.dtype)
            copies.append(pltpu.make_async_copy(rounded.at[span], out.at[span], sems.at[index]))
            copies[-1].start()
        for copy in copies:
            copy.wait()


def add_panel(packed, scalars, kind_at, shape, layer, panel, right, given, finish):
    step_count, columns, slots = shape
    result_slots, rows, width = given.shape[0] - 1, *given.shape[1:]
    in_scalar, in_vector = pl.BlockSpec(memory_space=pltpu.SMEM), pl.BlockSpec(memory_space=pltpu.VMEM)
    out_shape, out_specs = [pltpu.VMEM(given.shape, given.dtype)], [in_vector]
    scratch = [pltpu.SMEM((-(-step_count // columns) * slots + UNROLL,), jnp.int32)]
    if finish:
        out_shape.insert(0, jax.ShapeDtypeStruct((result_slots, rows, width), jnp.bfloat16))
        out_specs.insert(0, pl.BlockSpec(memory_space=pl.ANY))
        scratch.append(pltpu.VMEM((result_slots, rows, width), jnp.bfloat16))
        scratch.append(pltpu.SemaphoreType.DMA((PARTS,)))
    return pl.pallas_call(
        functools.partial(panel_kernel, shape, layer, kind_at, finish),
        out_shape=out_shape,
        in_specs=[in_scalar] * 2 + [in_vector] * 3,
        out_specs=out_specs,
        scratch_shapes=scratch,
        input_output_aliases={3: len(out_shape) - 1},
        compiler_params=pltpu.CompilerParams(vmem_limit_bytes=12 << 20),
        cost_estimate=pl.CostEstimate(flops=1, bytes_accessed=1, transcendentals=0),
    )(packed, scalars, right, given, panel)[0]


def scalar_list(*values):
    return jnp.stack([jnp.asarray(value, jnp.int32) for value in values])


def swapped(value):
    return lax.ppermute(value, "dep", [(0, 1), (1, 0)])


def paired(value):
    return lax.all_gather(value, "dep", axis=0, tiled=True)


def kept_products(both, layer, half, right_slot):
    slots = both.shape[3]
    result = both[:, :, 2] - layer * half
    wanted = (result >= 0) & (result < half)
    layers = jnp.arange(2, dtype=jnp.int32)[:, None, None]
    packed = right_slot(both[:, :, 1], layers) << 20 | (layers * slots + both[:, :, 0]) << 10 | result
    return jnp.where(wanted, packed, -1).reshape(-1)


def layer_products(step_lists, layer, half, right_slot):
    result = step_lists[:, 2]
    turned = jnp.where(result < half, result + layer * half, result - layer * half)
    packed = right_slot(step_lists[:, 1], 0) << 20 | step_lists[:, 0] << 10 | turned
    return jnp.where(result < 2 * half, packed, -1).reshape(-1)


def ring(left_blocks, right_blocks, triples, half):
    own, right_own, step_lists = left_blocks[0, 0, 0], right_blocks[0, 0, 0], triples[0, 0, 0]
    columns, layer = lax.axis_size("col"), lax.axis_index("dep")
    gathered = lax.all_gather(right_own, "row", axis=0, tiled=True)
    right_slots = gathered.shape[0]
    both = jnp.stack([step_lists, swapped(step_lists)])
    packed = kept_products(both, layer, half, lambda slot, layers: layers * right_slots + slot)
    rights = [(gathered, False), (swapped(gathered), False)]
    shape = (step_lists.shape[0], columns, own.shape[0])
    rising, falling, total = own, own, []
    panels, classes = [[(own, False), (paired(own), True)]], [0]
    reach = step_lists.shape[0] // 2
    for distance in range(1, reach + 1):
        rising = lax.ppermute(rising, "col", [(i, (i + 1) % columns) for i in range(columns)])
        falling = lax.ppermute(falling, "col", [(i, (i - 1) % columns) for i in range(columns)])
        panels += [[(value, False), (paired(value), True)] for value in (rising, falling)]
        classes += [columns - distance, distance]
        saved = [] if distance == reach else [half]
        scalars = scalar_list(*classes, layer)
        total = product_sums(packed, scalars, shape, 2, panels, rights, total, half, saved)
        panels, classes = [], []
    return total[0][None, None, None]


def line(left_blocks, right_blocks, triples, half):
    own, right_own, step_lists = left_blocks[0, 0, 0], right_blocks[0, 0, 0], triples[0, 0, 0]
    slots, part = own.shape[0], right_own.shape[0]
    columns, layer, place = lax.axis_size("col"), lax.axis_index("dep"), lax.axis_index("col")
    shape = (step_lists.shape[0], columns, slots)
    inner = (place == 1) | (place == 2)
    low = place < 2
    outward, across, inward = [(2, 3), (1, 0)], [(1, 2), (2, 1)], [(0, 1), (3, 2)]
    fence = lax.optimization_barrier

    def hop(value, pairs):
        return lax.ppermute(value, "col", pairs)

    def right_slot(slot, layers):
        return (layers * 2 + ((slot // part) ^ lax.axis_index("row"))) * part + slot % part

    outer_one, inward_one, across_one = hop(own, outward), hop(own, inward), hop(own, across)
    met = lax.ppermute(right_own, "row", [(0, 1), (1, 0)])
    listed = layer_products(step_lists, layer, half, right_slot)
    classes = [0, jnp.where(inner, jnp.where(low, 1, 3), -1), jnp.where(inner, jnp.where(low, 3, 1), -1)]
    classes += [jnp.where(inner, -1, jnp.where(low, 1, 3)), jnp.where(inner, 2, -1), jnp.where(inner, -1, 2)]
    scalars = scalar_list(*classes, layer, jnp.where(inner, -1, jnp.where(low, 3, 1)))

    across_one, inward_one, outer_one, met, listed, scalars = fence(
        (across_one, inward_one, outer_one, met, listed, scalars)
    )
    outer_two, across_two = hop(across_one, outward), hop(inward_one, across)
    right_other, met_other = swapped(right_own), swapped(met)
    both = jnp.stack([step_lists, swapped(step_lists)])
    kept = kept_products(both, layer, half, right_slot)

    across_two, right_other, met_other, kept = fence((across_two, right_other, met_other, kept))
    outer_three = hop(across_two, outward)
    panels = [[(value, False)] for value in (own, across_one, inward_one, outer_one, across_two, outer_two)]
    rights = [(value, False) for value in (right_own, met, right_other, met_other)]
    saved = [half // PARTS] * (PARTS - 1) + [half - half // PARTS * (PARTS - 1)]
    *parts, right, total = product_sums(
        listed, scalars, shape, 1, panels, rights, [], 2 * half, saved, "split"
    )
    total = add_received(total, [swapped(part) for part in parts])

    outer_three, total, right = fence((outer_three, total, right))
    kind_at = len(classes) + 1
    total = add_panel(kept, scalars, kind_at, shape, 0, outer_three, right, total, False)
    block = add_panel(kept, scalars, kind_at, shape, 1, swapped(outer_three), right, total, True)
    return block[None, None, None]


def local(left_blocks, right_blocks, triples):
    step_count = triples.shape[3]
    row_count, columns = lax.axis_size("row"), lax.axis_size("col")
    half = (2 * step_count - 2 + row_count) // row_count * NBQ // 2
    if columns >= step_count:
        return ring(left_blocks, right_blocks, triples, half)
    assert columns == 4 and row_count == 2
    return line(left_blocks, right_blocks, triples, half)


def solution(mesh):
    return jax.shard_map(
        local,
        mesh=mesh,
        in_specs=(
            P(("grp", "row"), "col", "dep", None, None, None),
            P(("grp", "row"), "col", "dep", None, None, None),
            P(("grp", "row"), "col", "dep", None, None, None),
        ),
        out_specs=P(("grp", "row"), "col", "dep", None, None, None),
        check_vma=False,
    )
```

```python
import functools

import jax
import jax.numpy as jnp
from jax import lax
from jax.experimental import pallas as pl
from jax.experimental.pallas import tpu as pltpu
from jax.sharding import PartitionSpec as P

NBQ = 32
UNROLL = 8
PARTS = 4


def chosen_products(packed, classes, panels, todo, shape, layers, spare, first_left=0):
    step_count, columns, slots = shape
    count = jnp.int32(0)
    for panel in range(panels):
        kind = classes[panel]
        for extra in range(-(-step_count // columns)):
            step = lax.rem(kind + step_count // 2, columns) + extra * columns
            groups = jnp.where((kind >= 0) & (step < step_count), slots // 8, 0)
            for layer in range(layers):
                base = (layer * step_count + step) * slots

                def keep(group, count):
                    for lane in range(8):
                        entry = packed[base + group * 8 + lane]
                        todo[count] = entry + (panel * layers * slots << 10)
                        count += (entry >= 0).astype(jnp.int32)
                    return count

                count = lax.fori_loop(0, groups, keep, count)
    for extra in range(UNROLL - 1):
        todo[count + extra] = jnp.int32(first_left << 10 | spare)
    return count


def add_chosen(todo, count, left, right, work, first_left=0):
    def several(group, carry):
        entries = [todo[group * UNROLL + lane] for lane in range(UNROLL)]
        products = [
            jnp.dot(
                left[((entry >> 10) & 1023) - first_left],
                right[entry >> 20],
                preferred_element_type=jnp.float32,
            )
            for entry in entries
        ]
        for entry, product in zip(entries, products):
            work[entry & 1023] += product
        return carry

    lax.fori_loop(0, (count + UNROLL - 1) // UNROLL, several, jnp.int32(0))


def sum_kernel(panels, rights, givens, saved, mode, shape, layers, operand_count, layer_at, *refs):
    packed, classes, refs = refs[0], refs[1], refs[2:]
    operands, refs = refs[:operand_count], refs[operand_count:]
    out_count = max(len(saved), 1)
    outs, refs = refs[:out_count], refs[out_count:]
    if mode == "split":
        (right, kept), (work, left, todo, sems) = refs[:2], refs[2:]
    else:
        work, left, right, todo, sems = refs
    spare = work.shape[0] - 1
    other = 1 - classes[layer_at]
    copies = []

    def plan(source, target, when=None):
        copies.append((pltpu.make_async_copy(source, target, sems.at[len(copies)]), when))

    start = 0
    for operand, size, gathered in rights:
        source = operands[operand]
        if gathered:
            source = source.at[pl.ds(other * size, size)]
        plan(source, right.at[pl.ds(start, size)])
        start += size
    start = 0
    for panel, pieces in enumerate(panels):
        for operand, size, gathered in pieces:
            source = operands[operand]
            if gathered:
                source = source.at[pl.ds(other * size, size)]
            plan(source, left.at[pl.ds(start, size)], classes[panel] >= 0)
            start += size
    start = 0
    for operand, size in givens:
        plan(operands[operand], work.at[pl.ds(start, size)])
        start += size
    for copy, when in copies:
        copy.start() if when is None else pl.when(when)(copy.start)
    if givens:
        work[spare] = jnp.zeros_like(work[spare])
    else:
        work[...] = jnp.zeros_like(work)
    kinds = [classes[panel] for panel in range(len(panels))]
    count = chosen_products(packed, kinds, len(panels), todo, shape, layers, spare)
    for copy, when in copies:
        copy.wait() if when is None else pl.when(when)(copy.wait)
    add_chosen(todo, count, left, right, work)
    if not saved:
        outs[0][...] = work[:spare].astype(outs[0].dtype)
        return
    start, copies, targets = 0, [], list(outs)
    if mode == "split":
        kept[kept.shape[0] - 1] = jnp.zeros(kept.shape[1:], kept.dtype)
        targets.insert(0, kept.at[pl.ds(0, kept.shape[0] - 1)])
    for out in targets:
        size = out.shape[0]
        copies.append(pltpu.make_async_copy(work.at[pl.ds(start, size)], out, sems.at[len(copies)]))
        start += size
    for copy in copies:
        copy.start()
    for copy in copies:
        copy.wait()


def product_sums(packed, scalars, shape, layers, panels, rights, givens, result_slots, saved, mode="whole"):
    step_count, columns, slots = shape
    rows, width = rights[0][0].shape[1:]
    operands = []

    def number(value):
        for index, known in enumerate(operands):
            if known is value:
                return index
        operands.append(value)
        return len(operands) - 1

    def spans(pieces):
        return [
            (number(value), value.shape[0] // 2 if gathered else value.shape[0], gathered)
            for value, gathered in pieces
        ]

    right_spans = spans(rights)
    panel_spans = [spans(pieces) for pieces in panels]
    given_spans = [(number(value), value.shape[0]) for value in givens]
    right_slots = sum(size for _, size, _ in right_spans)
    left_slots = len(panels) * layers * slots
    assert right_slots <= 1024 and left_slots <= 1024 and result_slots < 1024 and slots % 8 == 0
    assert all(sum(size for _, size, _ in pieces) == layers * slots for pieces in panel_spans)
    anywhere = pl.BlockSpec(memory_space=pl.ANY)
    in_scalar, in_vector = pl.BlockSpec(memory_space=pltpu.SMEM), pl.BlockSpec(memory_space=pltpu.VMEM)
    copy_count = len(rights) + sum(len(pieces) for pieces in panels) + len(givens) + len(saved) + 1
    scratch = [
        pltpu.VMEM((result_slots + 1, rows, width), jnp.float32),
        pltpu.VMEM((left_slots, rows, width), jnp.bfloat16),
        pltpu.VMEM((right_slots, width, width), jnp.bfloat16),
    ]
    if saved:
        out_shape = [jax.ShapeDtypeStruct((size, rows, width), jnp.float32) for size in saved]
    else:
        out_shape = [jax.ShapeDtypeStruct((result_slots, rows, width), jnp.bfloat16)]
    out_specs = [anywhere if saved else in_vector] * len(out_shape)
    if mode == "split":
        out_shape += [scratch.pop(), pltpu.VMEM((result_slots - sum(saved) + 1, rows, width), jnp.float32)]
        out_specs += [in_vector] * 2
    return pl.pallas_call(
        functools.partial(
            sum_kernel,
            panel_spans,
            right_spans,
            given_spans,
            saved,
            mode,
            shape,
            layers,
            len(operands),
            len(panels),
        ),
        out_shape=out_shape,
        in_specs=[in_scalar, in_scalar] + [anywhere] * len(operands),
        out_specs=out_specs,
        scratch_shapes=scratch
        + [
            pltpu.SMEM((len(panels) * -(-step_count // columns) * layers * slots + UNROLL,), jnp.int32),
            pltpu.SemaphoreType.DMA((copy_count,)),
        ],
        compiler_params=pltpu.CompilerParams(vmem_limit_bytes=(34 if mode == "split" else 56) << 20),
        cost_estimate=pl.CostEstimate(flops=1, bytes_accessed=1, transcendentals=0),
    )(packed, scalars, *operands)


def received_kernel(given, *refs):
    del given
    work, start = refs[-1], 0
    for piece in refs[:-1]:
        span = pl.ds(start, piece.shape[0])
        work[span] += piece[...]
        start += piece.shape[0]


def add_received(given, pieces):
    in_vector = pl.BlockSpec(memory_space=pltpu.VMEM)
    return pl.pallas_call(
        received_kernel,
        out_shape=pltpu.VMEM(given.shape, given.dtype),
        in_specs=[in_vector] * (1 + len(pieces)),
        out_specs=in_vector,
        input_output_aliases={0: 0},
        compiler_params=pltpu.CompilerParams(vmem_limit_bytes=12 << 20),
        cost_estimate=pl.CostEstimate(flops=1, bytes_accessed=1, transcendentals=0),
    )(given, *pieces)


def panel_kernel(shape, layer, kind_at, finish, packed, scalars, right, given, left, *refs):
    del given
    step_count, columns, slots = shape
    work, todo = (refs[1], refs[2]) if finish else (refs[0], refs[1])
    spare, first = work.shape[0] - 1, layer * slots
    part = packed.at[pl.ds(layer * step_count * slots, step_count * slots)]
    count = chosen_products(part, [scalars[kind_at]], 1, todo, shape, 1, spare, first)
    add_chosen(todo, count, left, right, work, first)
    if finish:
        out, rounded, sems = refs[0], refs[3], refs[4]
        size = spare // PARTS
        copies = []
        for index in range(PARTS):
            span = pl.ds(index * size, size if index < PARTS - 1 else spare - index * size)
            rounded[span] = work[span].astype(rounded.dtype)
            copies.append(pltpu.make_async_copy(rounded.at[span], out.at[span], sems.at[index]))
            copies[-1].start()
        for copy in copies:
            copy.wait()


def add_panel(packed, scalars, kind_at, shape, layer, panel, right, given, finish):
    step_count, columns, slots = shape
    result_slots, rows, width = given.shape[0] - 1, *given.shape[1:]
    in_scalar, in_vector = pl.BlockSpec(memory_space=pltpu.SMEM), pl.BlockSpec(memory_space=pltpu.VMEM)
    out_shape, out_specs = [pltpu.VMEM(given.shape, given.dtype)], [in_vector]
    scratch = [pltpu.SMEM((-(-step_count // columns) * slots + UNROLL,), jnp.int32)]
    if finish:
        out_shape.insert(0, jax.ShapeDtypeStruct((result_slots, rows, width), jnp.bfloat16))
        out_specs.insert(0, pl.BlockSpec(memory_space=pl.ANY))
        scratch.append(pltpu.VMEM((result_slots, rows, width), jnp.bfloat16))
        scratch.append(pltpu.SemaphoreType.DMA((PARTS,)))
    return pl.pallas_call(
        functools.partial(panel_kernel, shape, layer, kind_at, finish),
        out_shape=out_shape,
        in_specs=[in_scalar] * 2 + [in_vector] * 3,
        out_specs=out_specs,
        scratch_shapes=scratch,
        input_output_aliases={3: len(out_shape) - 1},
        compiler_params=pltpu.CompilerParams(vmem_limit_bytes=12 << 20),
        cost_estimate=pl.CostEstimate(flops=1, bytes_accessed=1, transcendentals=0),
    )(packed, scalars, right, given, panel)[0]


def scalar_list(*values):
    return jnp.stack([jnp.asarray(value, jnp.int32) for value in values])


def swapped(value):
    return lax.ppermute(value, "dep", [(0, 1), (1, 0)])


def paired(value):
    return lax.all_gather(value, "dep", axis=0, tiled=True)


def kept_products(both, layer, half, right_slot):
    slots = both.shape[3]
    result = both[:, :, 2] - layer * half
    wanted = (result >= 0) & (result < half)
    layers = jnp.arange(2, dtype=jnp.int32)[:, None, None]
    packed = right_slot(both[:, :, 1], layers) << 20 | (layers * slots + both[:, :, 0]) << 10 | result
    return jnp.where(wanted, packed, -1).reshape(-1)


def layer_products(step_lists, layer, half, right_slot):
    result = step_lists[:, 2]
    turned = jnp.where(result < half, result + layer * half, result - layer * half)
    packed = right_slot(step_lists[:, 1], 0) << 20 | step_lists[:, 0] << 10 | turned
    return jnp.where(result < 2 * half, packed, -1).reshape(-1)


def ring(left_blocks, right_blocks, triples, half):
    own, right_own, step_lists = left_blocks[0, 0, 0], right_blocks[0, 0, 0], triples[0, 0, 0]
    columns, layer = lax.axis_size("col"), lax.axis_index("dep")
    gathered = lax.all_gather(right_own, "row", axis=0, tiled=True)
    right_slots = gathered.shape[0]
    both = jnp.stack([step_lists, swapped(step_lists)])
    packed = kept_products(both, layer, half, lambda slot, layers: layers * right_slots + slot)
    rights = [(gathered, False), (swapped(gathered), False)]
    shape = (step_lists.shape[0], columns, own.shape[0])
    rising, falling, total = own, own, []
    panels, classes = [[(own, False), (paired(own), True)]], [0]
    reach = step_lists.shape[0] // 2
    for distance in range(1, reach + 1):
        rising = lax.ppermute(rising, "col", [(i, (i + 1) % columns) for i in range(columns)])
        falling = lax.ppermute(falling, "col", [(i, (i - 1) % columns) for i in range(columns)])
        panels += [[(value, False), (paired(value), True)] for value in (rising, falling)]
        classes += [columns - distance, distance]
        saved = [] if distance == reach else [half]
        scalars = scalar_list(*classes, layer)
        total = product_sums(packed, scalars, shape, 2, panels, rights, total, half, saved)
        panels, classes = [], []
    return total[0][None, None, None]


def line(left_blocks, right_blocks, triples, half):
    own, right_own, step_lists = left_blocks[0, 0, 0], right_blocks[0, 0, 0], triples[0, 0, 0]
    slots, part = own.shape[0], right_own.shape[0]
    columns, layer, place = lax.axis_size("col"), lax.axis_index("dep"), lax.axis_index("col")
    shape = (step_lists.shape[0], columns, slots)
    inner = (place == 1) | (place == 2)
    low = place < 2
    outward, across, inward = [(2, 3), (1, 0)], [(1, 2), (2, 1)], [(0, 1), (3, 2)]
    fence = lax.optimization_barrier

    def hop(value, pairs):
        return lax.ppermute(value, "col", pairs)

    def right_slot(slot, layers):
        return (layers * 2 + ((slot // part) ^ lax.axis_index("row"))) * part + slot % part

    outer_one, inward_one, across_one = hop(own, outward), hop(own, inward), hop(own, across)
    met = lax.ppermute(right_own, "row", [(0, 1), (1, 0)])
    listed = layer_products(step_lists, layer, half, right_slot)
    classes = [0, jnp.where(inner, jnp.where(low, 1, 3), -1), jnp.where(inner, jnp.where(low, 3, 1), -1)]
    classes += [jnp.where(inner, -1, jnp.where(low, 1, 3)), jnp.where(inner, 2, -1), jnp.where(inner, -1, 2)]
    scalars = scalar_list(*classes, layer, jnp.where(inner, -1, jnp.where(low, 3, 1)))

    outer_two, across_two = hop(across_one, outward), hop(inward_one, across)
    inward_one, across_one, outer_one, met, listed, scalars = fence(
        (inward_one, across_one, outer_one, met, listed, scalars)
    )
    right_other, met_other = swapped(right_own), swapped(met)
    both = jnp.stack([step_lists, swapped(step_lists)])
    kept = kept_products(both, layer, half, right_slot)

    across_two, right_other, met_other, kept = fence((across_two, right_other, met_other, kept))
    outer_three = hop(across_two, outward)
    panels = [[(value, False)] for value in (own, across_one, inward_one, outer_one, across_two, outer_two)]
    rights = [(value, False) for value in (right_own, met, right_other, met_other)]
    saved = [half // PARTS] * (PARTS - 1) + [half - half // PARTS * (PARTS - 1)]
    *parts, right, total = product_sums(
        listed, scalars, shape, 1, panels, rights, [], 2 * half, saved, "split"
    )
    total = add_received(total, [swapped(part) for part in parts])

    outer_three, total, right = fence((outer_three, total, right))
    kind_at = len(classes) + 1
    total = add_panel(kept, scalars, kind_at, shape, 0, outer_three, right, total, False)
    block = add_panel(kept, scalars, kind_at, shape, 1, swapped(outer_three), right, total, True)
    return block[None, None, None]


def local(left_blocks, right_blocks, triples):
    step_count = triples.shape[3]
    row_count, columns = lax.axis_size("row"), lax.axis_size("col")
    half = (2 * step_count - 2 + row_count) // row_count * NBQ // 2
    if columns >= step_count:
        return ring(left_blocks, right_blocks, triples, half)
    assert columns == 4 and row_count == 2
    return line(left_blocks, right_blocks, triples, half)


def solution(mesh):
    return jax.shard_map(
        local,
        mesh=mesh,
        in_specs=(
            P(("grp", "row"), "col", "dep", None, None, None),
            P(("grp", "row"), "col", "dep", None, None, None),
            P(("grp", "row"), "col", "dep", None, None, None),
        ),
        out_specs=P(("grp", "row"), "col", "dep", None, None, None),
        check_vma=False,
    )
```

```python
import functools

import jax
import jax.numpy as jnp
from jax import lax
from jax.experimental import pallas as pl
from jax.experimental.pallas import tpu as pltpu
from jax.sharding import PartitionSpec as P

NBQ = 32
UNROLL = 8
PARTS = 4


def chosen_products(packed, classes, panels, todo, shape, layers, spare, first_left=0):
    step_count, columns, slots = shape
    count = jnp.int32(0)
    for panel in range(panels):
        kind = classes[panel]
        for extra in range(-(-step_count // columns)):
            step = lax.rem(kind + step_count // 2, columns) + extra * columns
            groups = jnp.where((kind >= 0) & (step < step_count), slots // 8, 0)
            for layer in range(layers):
                base = (layer * step_count + step) * slots

                def keep(group, count):
                    for lane in range(8):
                        entry = packed[base + group * 8 + lane]
                        todo[count] = entry + (panel * layers * slots << 10)
                        count += (entry >= 0).astype(jnp.int32)
                    return count

                count = lax.fori_loop(0, groups, keep, count)
    for extra in range(UNROLL - 1):
        todo[count + extra] = jnp.int32(first_left << 10 | spare)
    return count


def add_chosen(todo, count, left, right, work, first_left=0):
    def several(group, carry):
        entries = [todo[group * UNROLL + lane] for lane in range(UNROLL)]
        products = [
            jnp.dot(
                left[((entry >> 10) & 1023) - first_left],
                right[entry >> 20],
                preferred_element_type=jnp.float32,
            )
            for entry in entries
        ]
        for entry, product in zip(entries, products):
            work[entry & 1023] += product
        return carry

    lax.fori_loop(0, (count + UNROLL - 1) // UNROLL, several, jnp.int32(0))


def sum_kernel(panels, rights, givens, saved, mode, shape, layers, operand_count, layer_at, *refs):
    packed, classes, refs = refs[0], refs[1], refs[2:]
    operands, refs = refs[:operand_count], refs[operand_count:]
    out_count = max(len(saved), 1)
    outs, refs = refs[:out_count], refs[out_count:]
    if mode == "split":
        (right, kept), (work, left, todo, sems) = refs[:2], refs[2:]
    else:
        work, left, right, todo, sems = refs
    spare = work.shape[0] - 1
    other = 1 - classes[layer_at]
    copies = []

    def plan(source, target, when=None):
        copies.append((pltpu.make_async_copy(source, target, sems.at[len(copies)]), when))

    start = 0
    for operand, size, gathered in rights:
        source = operands[operand]
        if gathered:
            source = source.at[pl.ds(other * size, size)]
        plan(source, right.at[pl.ds(start, size)])
        start += size
    start = 0
    for panel, pieces in enumerate(panels):
        for operand, size, gathered in pieces:
            source = operands[operand]
            if gathered:
                source = source.at[pl.ds(other * size, size)]
            plan(source, left.at[pl.ds(start, size)], classes[panel] >= 0)
            start += size
    start = 0
    for operand, size in givens:
        plan(operands[operand], work.at[pl.ds(start, size)])
        start += size
    for copy, when in copies:
        copy.start() if when is None else pl.when(when)(copy.start)
    if givens:
        work[spare] = jnp.zeros_like(work[spare])
    else:
        work[...] = jnp.zeros_like(work)
    kinds = [classes[panel] for panel in range(len(panels))]
    count = chosen_products(packed, kinds, len(panels), todo, shape, layers, spare)
    for copy, when in copies:
        copy.wait() if when is None else pl.when(when)(copy.wait)
    add_chosen(todo, count, left, right, work)
    if not saved:
        outs[0][...] = work[:spare].astype(outs[0].dtype)
        return
    start, copies, targets = 0, [], list(outs)
    if mode == "split":
        kept[kept.shape[0] - 1] = jnp.zeros(kept.shape[1:], kept.dtype)
        targets.insert(0, kept.at[pl.ds(0, kept.shape[0] - 1)])
    for out in targets:
        size = out.shape[0]
        copies.append(pltpu.make_async_copy(work.at[pl.ds(start, size)], out, sems.at[len(copies)]))
        start += size
    for copy in copies:
        copy.start()
    for copy in copies:
        copy.wait()


def product_sums(packed, scalars, shape, layers, panels, rights, givens, result_slots, saved, mode="whole"):
    step_count, columns, slots = shape
    rows, width = rights[0][0].shape[1:]
    operands = []

    def number(value):
        for index, known in enumerate(operands):
            if known is value:
                return index
        operands.append(value)
        return len(operands) - 1

    def spans(pieces):
        return [
            (number(value), value.shape[0] // 2 if gathered else value.shape[0], gathered)
            for value, gathered in pieces
        ]

    right_spans = spans(rights)
    panel_spans = [spans(pieces) for pieces in panels]
    given_spans = [(number(value), value.shape[0]) for value in givens]
    right_slots = sum(size for _, size, _ in right_spans)
    left_slots = len(panels) * layers * slots
    assert right_slots <= 1024 and left_slots <= 1024 and result_slots < 1024 and slots % 8 == 0
    assert all(sum(size for _, size, _ in pieces) == layers * slots for pieces in panel_spans)
    anywhere = pl.BlockSpec(memory_space=pl.ANY)
    in_scalar, in_vector = pl.BlockSpec(memory_space=pltpu.SMEM), pl.BlockSpec(memory_space=pltpu.VMEM)
    copy_count = len(rights) + sum(len(pieces) for pieces in panels) + len(givens) + len(saved) + 1
    scratch = [
        pltpu.VMEM((result_slots + 1, rows, width), jnp.float32),
        pltpu.VMEM((left_slots, rows, width), jnp.bfloat16),
        pltpu.VMEM((right_slots, width, width), jnp.bfloat16),
    ]
    if saved:
        out_shape = [jax.ShapeDtypeStruct((size, rows, width), jnp.float32) for size in saved]
    else:
        out_shape = [jax.ShapeDtypeStruct((result_slots, rows, width), jnp.bfloat16)]
    out_specs = [anywhere if saved else in_vector] * len(out_shape)
    if mode == "split":
        out_shape += [scratch.pop(), pltpu.VMEM((result_slots - sum(saved) + 1, rows, width), jnp.float32)]
        out_specs += [in_vector] * 2
    return pl.pallas_call(
        functools.partial(
            sum_kernel,
            panel_spans,
            right_spans,
            given_spans,
            saved,
            mode,
            shape,
            layers,
            len(operands),
            len(panels),
        ),
        out_shape=out_shape,
        in_specs=[in_scalar, in_scalar] + [anywhere] * len(operands),
        out_specs=out_specs,
        scratch_shapes=scratch
        + [
            pltpu.SMEM((len(panels) * -(-step_count // columns) * layers * slots + UNROLL,), jnp.int32),
            pltpu.SemaphoreType.DMA((copy_count,)),
        ],
        compiler_params=pltpu.CompilerParams(vmem_limit_bytes=(34 if mode == "split" else 56) << 20),
        cost_estimate=pl.CostEstimate(flops=1, bytes_accessed=1, transcendentals=0),
    )(packed, scalars, *operands)


def received_kernel(given, *refs):
    del given
    work, start = refs[-1], 0
    for piece in refs[:-1]:
        span = pl.ds(start, piece.shape[0])
        work[span] += piece[...]
        start += piece.shape[0]


def add_received(given, pieces):
    in_vector = pl.BlockSpec(memory_space=pltpu.VMEM)
    return pl.pallas_call(
        received_kernel,
        out_shape=pltpu.VMEM(given.shape, given.dtype),
        in_specs=[in_vector] * (1 + len(pieces)),
        out_specs=in_vector,
        input_output_aliases={0: 0},
        compiler_params=pltpu.CompilerParams(vmem_limit_bytes=12 << 20),
        cost_estimate=pl.CostEstimate(flops=1, bytes_accessed=1, transcendentals=0),
    )(given, *pieces)


def panel_kernel(shape, layer, kind_at, finish, packed, scalars, right, given, left, *refs):
    del given
    step_count, columns, slots = shape
    work, todo = (refs[1], refs[2]) if finish else (refs[0], refs[1])
    spare, first = work.shape[0] - 1, layer * slots
    part = packed.at[pl.ds(layer * step_count * slots, step_count * slots)]
    count = chosen_products(part, [scalars[kind_at]], 1, todo, shape, 1, spare, first)
    add_chosen(todo, count, left, right, work, first)
    if finish:
        out, rounded, sems = refs[0], refs[3], refs[4]
        size = spare // PARTS
        copies = []
        for index in range(PARTS):
            span = pl.ds(index * size, size if index < PARTS - 1 else spare - index * size)
            rounded[span] = work[span].astype(rounded.dtype)
            copies.append(pltpu.make_async_copy(rounded.at[span], out.at[span], sems.at[index]))
            copies[-1].start()
        for copy in copies:
            copy.wait()


def add_panel(packed, scalars, kind_at, shape, layer, panel, right, given, finish):
    step_count, columns, slots = shape
    result_slots, rows, width = given.shape[0] - 1, *given.shape[1:]
    in_scalar, in_vector = pl.BlockSpec(memory_space=pltpu.SMEM), pl.BlockSpec(memory_space=pltpu.VMEM)
    out_shape, out_specs = [pltpu.VMEM(given.shape, given.dtype)], [in_vector]
    scratch = [pltpu.SMEM((-(-step_count // columns) * slots + UNROLL,), jnp.int32)]
    if finish:
        out_shape.insert(0, jax.ShapeDtypeStruct((result_slots, rows, width), jnp.bfloat16))
        out_specs.insert(0, pl.BlockSpec(memory_space=pl.ANY))
        scratch.append(pltpu.VMEM((result_slots, rows, width), jnp.bfloat16))
        scratch.append(pltpu.SemaphoreType.DMA((PARTS,)))
    return pl.pallas_call(
        functools.partial(panel_kernel, shape, layer, kind_at, finish),
        out_shape=out_shape,
        in_specs=[in_scalar] * 2 + [in_vector] * 3,
        out_specs=out_specs,
        scratch_shapes=scratch,
        input_output_aliases={3: len(out_shape) - 1},
        compiler_params=pltpu.CompilerParams(vmem_limit_bytes=12 << 20),
        cost_estimate=pl.CostEstimate(flops=1, bytes_accessed=1, transcendentals=0),
    )(packed, scalars, right, given, panel)[0]


def scalar_list(*values):
    return jnp.stack([jnp.asarray(value, jnp.int32) for value in values])


def swapped(value):
    return lax.ppermute(value, "dep", [(0, 1), (1, 0)])


def paired(value):
    return lax.all_gather(value, "dep", axis=0, tiled=True)


def kept_products(both, layer, half, right_slot):
    slots = both.shape[3]
    result = both[:, :, 2] - layer * half
    wanted = (result >= 0) & (result < half)
    layers = jnp.arange(2, dtype=jnp.int32)[:, None, None]
    packed = right_slot(both[:, :, 1], layers) << 20 | (layers * slots + both[:, :, 0]) << 10 | result
    return jnp.where(wanted, packed, -1).reshape(-1)


def layer_products(step_lists, layer, half, right_slot):
    result = step_lists[:, 2]
    turned = jnp.where(result < half, result + layer * half, result - layer * half)
    packed = right_slot(step_lists[:, 1], 0) << 20 | step_lists[:, 0] << 10 | turned
    return jnp.where(result < 2 * half, packed, -1).reshape(-1)


def ring(left_blocks, right_blocks, triples, half):
    own, right_own, step_lists = left_blocks[0, 0, 0], right_blocks[0, 0, 0], triples[0, 0, 0]
    columns, layer = lax.axis_size("col"), lax.axis_index("dep")
    gathered = lax.all_gather(right_own, "row", axis=0, tiled=True)
    right_slots = gathered.shape[0]
    both = jnp.stack([step_lists, swapped(step_lists)])
    packed = kept_products(both, layer, half, lambda slot, layers: layers * right_slots + slot)
    rights = [(gathered, False), (swapped(gathered), False)]
    shape = (step_lists.shape[0], columns, own.shape[0])
    rising, falling, total = own, own, []
    panels, classes = [[(own, False), (paired(own), True)]], [0]
    reach = step_lists.shape[0] // 2
    for distance in range(1, reach + 1):
        rising = lax.ppermute(rising, "col", [(i, (i + 1) % columns) for i in range(columns)])
        falling = lax.ppermute(falling, "col", [(i, (i - 1) % columns) for i in range(columns)])
        panels += [[(value, False), (paired(value), True)] for value in (rising, falling)]
        classes += [columns - distance, distance]
        saved = [] if distance == reach else [half]
        scalars = scalar_list(*classes, layer)
        total = product_sums(packed, scalars, shape, 2, panels, rights, total, half, saved)
        panels, classes = [], []
    return total[0][None, None, None]


def line(left_blocks, right_blocks, triples, half):
    own, right_own, step_lists = left_blocks[0, 0, 0], right_blocks[0, 0, 0], triples[0, 0, 0]
    slots, part = own.shape[0], right_own.shape[0]
    columns, layer, place = lax.axis_size("col"), lax.axis_index("dep"), lax.axis_index("col")
    shape = (step_lists.shape[0], columns, slots)
    inner = (place == 1) | (place == 2)
    low = place < 2
    outward, across, beside = [(2, 3), (1, 0)], [(1, 2), (2, 1)], [(0, 1), (1, 0), (2, 3), (3, 2)]
    fence = lax.optimization_barrier

    def hop(value, pairs):
        return lax.ppermute(value, "col", pairs)

    def right_slot(slot, layers):
        return (layers * 2 + ((slot // part) ^ lax.axis_index("row"))) * part + slot % part

    beside_one, across_one = hop(own, beside), hop(own, across)
    met = lax.ppermute(right_own, "row", [(0, 1), (1, 0)])
    listed = layer_products(step_lists, layer, half, right_slot)
    classes = [0, jnp.where(place % 2 == 0, 1, 3), jnp.where(inner, jnp.where(low, 1, 3), -1)]
    classes += [jnp.where(inner, 2, -1), jnp.where(inner, -1, 2)]
    scalars = scalar_list(*classes, layer, jnp.where(inner, -1, jnp.where(low, 3, 1)))

    outer_two, across_two = hop(across_one, outward), hop(beside_one, across)
    beside_one, across_one, met, listed, scalars = fence((beside_one, across_one, met, listed, scalars))
    right_other, met_other = swapped(right_own), swapped(met)
    both = jnp.stack([step_lists, swapped(step_lists)])
    kept = kept_products(both, layer, half, right_slot)

    across_two, right_other, met_other, kept = fence((across_two, right_other, met_other, kept))
    outer_three = hop(across_two, outward)
    panels = [[(value, False)] for value in (own, beside_one, across_one, across_two, outer_two)]
    rights = [(value, False) for value in (right_own, met, right_other, met_other)]
    saved = [half // PARTS] * (PARTS - 1) + [half - half // PARTS * (PARTS - 1)]
    *parts, right, total = product_sums(
        listed, scalars, shape, 1, panels, rights, [], 2 * half, saved, "split"
    )
    total = add_received(total, [swapped(part) for part in parts])

    outer_three, total, right = fence((outer_three, total, right))
    kind_at = len(classes) + 1
    total = add_panel(kept, scalars, kind_at, shape, 0, outer_three, right, total, False)
    block = add_panel(kept, scalars, kind_at, shape, 1, swapped(outer_three), right, total, True)
    return block[None, None, None]


def local(left_blocks, right_blocks, triples):
    step_count = triples.shape[3]
    row_count, columns = lax.axis_size("row"), lax.axis_size("col")
    half = (2 * step_count - 2 + row_count) // row_count * NBQ // 2
    if columns >= step_count:
        return ring(left_blocks, right_blocks, triples, half)
    assert columns == 4 and row_count == 2
    return line(left_blocks, right_blocks, triples, half)


def solution(mesh):
    return jax.shard_map(
        local,
        mesh=mesh,
        in_specs=(
            P(("grp", "row"), "col", "dep", None, None, None),
            P(("grp", "row"), "col", "dep", None, None, None),
            P(("grp", "row"), "col", "dep", None, None, None),
        ),
        out_specs=P(("grp", "row"), "col", "dep", None, None, None),
        check_vma=False,
    )
```

```python
import functools

import jax
import jax.numpy as jnp
from jax import lax
from jax.experimental import pallas as pl
from jax.experimental.pallas import tpu as pltpu
from jax.sharding import PartitionSpec as P

NBQ = 32
UNROLL = 8
PARTS = 4


def chosen_products(packed, classes, panels, todo, shape, layers, spare, first_left=0):
    step_count, columns, slots = shape
    count = jnp.int32(0)
    for panel in range(panels):
        kind = classes[panel]
        for extra in range(-(-step_count // columns)):
            step = lax.rem(kind + step_count // 2, columns) + extra * columns
            groups = jnp.where((kind >= 0) & (step < step_count), slots // 8, 0)
            for layer in range(layers):
                base = (layer * step_count + step) * slots

                def keep(group, count):
                    for lane in range(8):
                        entry = packed[base + group * 8 + lane]
                        todo[count] = entry + (panel * layers * slots << 10)
                        count += (entry >= 0).astype(jnp.int32)
                    return count

                count = lax.fori_loop(0, groups, keep, count)
    for extra in range(UNROLL - 1):
        todo[count + extra] = jnp.int32(first_left << 10 | spare)
    return count


def add_chosen(todo, count, left, right, work, first_left=0):
    def several(group, carry):
        entries = [todo[group * UNROLL + lane] for lane in range(UNROLL)]
        products = [
            jnp.dot(
                left[((entry >> 10) & 1023) - first_left],
                right[entry >> 20],
                preferred_element_type=jnp.float32,
            )
            for entry in entries
        ]
        for entry, product in zip(entries, products):
            work[entry & 1023] += product
        return carry

    lax.fori_loop(0, (count + UNROLL - 1) // UNROLL, several, jnp.int32(0))


def sum_kernel(panels, rights, givens, saved, mode, shape, layers, operand_count, layer_at, *refs):
    packed, classes, refs = refs[0], refs[1], refs[2:]
    operands, refs = refs[:operand_count], refs[operand_count:]
    out_count = max(len(saved), 1)
    outs, refs = refs[:out_count], refs[out_count:]
    if mode == "split":
        (right, kept), (work, left, todo, sems) = refs[:2], refs[2:]
    else:
        work, left, right, todo, sems = refs
    spare = work.shape[0] - 1
    other = 1 - classes[layer_at]
    copies = []

    def plan(source, target, when=None):
        copies.append((pltpu.make_async_copy(source, target, sems.at[len(copies)]), when))

    start = 0
    for operand, size, gathered in rights:
        source = operands[operand]
        if gathered:
            source = source.at[pl.ds(other * size, size)]
        plan(source, right.at[pl.ds(start, size)])
        start += size
    start = 0
    for panel, pieces in enumerate(panels):
        for operand, size, gathered in pieces:
            source = operands[operand]
            if gathered:
                source = source.at[pl.ds(other * size, size)]
            plan(source, left.at[pl.ds(start, size)], classes[panel] >= 0)
            start += size
    start = 0
    for operand, size in givens:
        plan(operands[operand], work.at[pl.ds(start, size)])
        start += size
    for copy, when in copies:
        copy.start() if when is None else pl.when(when)(copy.start)
    if givens:
        work[spare] = jnp.zeros_like(work[spare])
    else:
        work[...] = jnp.zeros_like(work)
    kinds = [classes[panel] for panel in range(len(panels))]
    count = chosen_products(packed, kinds, len(panels), todo, shape, layers, spare)
    for copy, when in copies:
        copy.wait() if when is None else pl.when(when)(copy.wait)
    add_chosen(todo, count, left, right, work)
    if not saved:
        outs[0][...] = work[:spare].astype(outs[0].dtype)
        return
    start, copies, targets = 0, [], list(outs)
    if mode == "split":
        kept[kept.shape[0] - 1] = jnp.zeros(kept.shape[1:], kept.dtype)
        targets.insert(0, kept.at[pl.ds(0, kept.shape[0] - 1)])
    for out in targets:
        size = out.shape[0]
        copies.append(pltpu.make_async_copy(work.at[pl.ds(start, size)], out, sems.at[len(copies)]))
        start += size
    for copy in copies:
        copy.start()
    for copy in copies:
        copy.wait()


def product_sums(packed, scalars, shape, layers, panels, rights, givens, result_slots, saved, mode="whole"):
    step_count, columns, slots = shape
    rows, width = rights[0][0].shape[1:]
    operands = []

    def number(value):
        for index, known in enumerate(operands):
            if known is value:
                return index
        operands.append(value)
        return len(operands) - 1

    def spans(pieces):
        return [
            (number(value), value.shape[0] // 2 if gathered else value.shape[0], gathered)
            for value, gathered in pieces
        ]

    right_spans = spans(rights)
    panel_spans = [spans(pieces) for pieces in panels]
    given_spans = [(number(value), value.shape[0]) for value in givens]
    right_slots = sum(size for _, size, _ in right_spans)
    left_slots = len(panels) * layers * slots
    assert right_slots <= 1024 and left_slots <= 1024 and result_slots < 1024 and slots % 8 == 0
    assert all(sum(size for _, size, _ in pieces) == layers * slots for pieces in panel_spans)
    anywhere = pl.BlockSpec(memory_space=pl.ANY)
    in_scalar, in_vector = pl.BlockSpec(memory_space=pltpu.SMEM), pl.BlockSpec(memory_space=pltpu.VMEM)
    copy_count = len(rights) + sum(len(pieces) for pieces in panels) + len(givens) + len(saved) + 1
    scratch = [
        pltpu.VMEM((result_slots + 1, rows, width), jnp.float32),
        pltpu.VMEM((left_slots, rows, width), jnp.bfloat16),
        pltpu.VMEM((right_slots, width, width), jnp.bfloat16),
    ]
    if saved:
        out_shape = [jax.ShapeDtypeStruct((size, rows, width), jnp.float32) for size in saved]
    else:
        out_shape = [jax.ShapeDtypeStruct((result_slots, rows, width), jnp.bfloat16)]
    out_specs = [anywhere if saved else in_vector] * len(out_shape)
    if mode == "split":
        out_shape += [scratch.pop(), pltpu.VMEM((result_slots - sum(saved) + 1, rows, width), jnp.float32)]
        out_specs += [in_vector] * 2
    return pl.pallas_call(
        functools.partial(
            sum_kernel,
            panel_spans,
            right_spans,
            given_spans,
            saved,
            mode,
            shape,
            layers,
            len(operands),
            len(panels),
        ),
        out_shape=out_shape,
        in_specs=[in_scalar, in_scalar] + [anywhere] * len(operands),
        out_specs=out_specs,
        scratch_shapes=scratch
        + [
            pltpu.SMEM((len(panels) * -(-step_count // columns) * layers * slots + UNROLL,), jnp.int32),
            pltpu.SemaphoreType.DMA((copy_count,)),
        ],
        compiler_params=pltpu.CompilerParams(vmem_limit_bytes=(34 if mode == "split" else 56) << 20),
        cost_estimate=pl.CostEstimate(flops=1, bytes_accessed=1, transcendentals=0),
    )(packed, scalars, *operands)


def received_kernel(given, *refs):
    del given
    work, start = refs[-1], 0
    for piece in refs[:-1]:
        span = pl.ds(start, piece.shape[0])
        work[span] += piece[...]
        start += piece.shape[0]


def add_received(given, pieces):
    in_vector = pl.BlockSpec(memory_space=pltpu.VMEM)
    return pl.pallas_call(
        received_kernel,
        out_shape=pltpu.VMEM(given.shape, given.dtype),
        in_specs=[in_vector] * (1 + len(pieces)),
        out_specs=in_vector,
        input_output_aliases={0: 0},
        compiler_params=pltpu.CompilerParams(vmem_limit_bytes=12 << 20),
        cost_estimate=pl.CostEstimate(flops=1, bytes_accessed=1, transcendentals=0),
    )(given, *pieces)


def panel_kernel(shape, layer, kind_at, finish, packed, scalars, right, given, left, *refs):
    del given
    step_count, columns, slots = shape
    work, todo = (refs[1], refs[2]) if finish else (refs[0], refs[1])
    spare, first = work.shape[0] - 1, layer * slots
    part = packed.at[pl.ds(layer * step_count * slots, step_count * slots)]
    count = chosen_products(part, [scalars[kind_at]], 1, todo, shape, 1, spare, first)
    add_chosen(todo, count, left, right, work, first)
    if finish:
        out, rounded, sems = refs[0], refs[3], refs[4]
        size = spare // PARTS
        copies = []
        for index in range(PARTS):
            span = pl.ds(index * size, size if index < PARTS - 1 else spare - index * size)
            rounded[span] = work[span].astype(rounded.dtype)
            copies.append(pltpu.make_async_copy(rounded.at[span], out.at[span], sems.at[index]))
            copies[-1].start()
        for copy in copies:
            copy.wait()


def add_panel(packed, scalars, kind_at, shape, layer, panel, right, given, finish):
    step_count, columns, slots = shape
    result_slots, rows, width = given.shape[0] - 1, *given.shape[1:]
    in_scalar, in_vector = pl.BlockSpec(memory_space=pltpu.SMEM), pl.BlockSpec(memory_space=pltpu.VMEM)
    out_shape, out_specs = [pltpu.VMEM(given.shape, given.dtype)], [in_vector]
    scratch = [pltpu.SMEM((-(-step_count // columns) * slots + UNROLL,), jnp.int32)]
    if finish:
        out_shape.insert(0, jax.ShapeDtypeStruct((result_slots, rows, width), jnp.bfloat16))
        out_specs.insert(0, pl.BlockSpec(memory_space=pl.ANY))
        scratch.append(pltpu.VMEM((result_slots, rows, width), jnp.bfloat16))
        scratch.append(pltpu.SemaphoreType.DMA((PARTS,)))
    return pl.pallas_call(
        functools.partial(panel_kernel, shape, layer, kind_at, finish),
        out_shape=out_shape,
        in_specs=[in_scalar] * 2 + [in_vector] * 3,
        out_specs=out_specs,
        scratch_shapes=scratch,
        input_output_aliases={3: len(out_shape) - 1},
        compiler_params=pltpu.CompilerParams(vmem_limit_bytes=12 << 20),
        cost_estimate=pl.CostEstimate(flops=1, bytes_accessed=1, transcendentals=0),
    )(packed, scalars, right, given, panel)[0]


def scalar_list(*values):
    return jnp.stack([jnp.asarray(value, jnp.int32) for value in values])


def swapped(value):
    return lax.ppermute(value, "dep", [(0, 1), (1, 0)])


def paired(value):
    return lax.all_gather(value, "dep", axis=0, tiled=True)


def kept_products(both, layer, half, right_slot):
    slots = both.shape[3]
    result = both[:, :, 2] - layer * half
    wanted = (result >= 0) & (result < half)
    layers = jnp.arange(2, dtype=jnp.int32)[:, None, None]
    packed = right_slot(both[:, :, 1], layers) << 20 | (layers * slots + both[:, :, 0]) << 10 | result
    return jnp.where(wanted, packed, -1).reshape(-1)


def layer_products(step_lists, layer, half, right_slot):
    result = step_lists[:, 2]
    turned = jnp.where(result < half, result + layer * half, result - layer * half)
    packed = right_slot(step_lists[:, 1], 0) << 20 | step_lists[:, 0] << 10 | turned
    return jnp.where(result < 2 * half, packed, -1).reshape(-1)


def ring(left_blocks, right_blocks, triples, half):
    own, right_own, step_lists = left_blocks[0, 0, 0], right_blocks[0, 0, 0], triples[0, 0, 0]
    columns, layer = lax.axis_size("col"), lax.axis_index("dep")
    gathered = lax.all_gather(right_own, "row", axis=0, tiled=True)
    right_slots = gathered.shape[0]
    both = jnp.stack([step_lists, swapped(step_lists)])
    packed = kept_products(both, layer, half, lambda slot, layers: layers * right_slots + slot)
    rights = [(gathered, False), (swapped(gathered), False)]
    shape = (step_lists.shape[0], columns, own.shape[0])
    rising, falling, total = own, own, []
    panels, classes = [[(own, False), (paired(own), True)]], [0]
    reach = step_lists.shape[0] // 2
    for distance in range(1, reach + 1):
        rising = lax.ppermute(rising, "col", [(i, (i + 1) % columns) for i in range(columns)])
        falling = lax.ppermute(falling, "col", [(i, (i - 1) % columns) for i in range(columns)])
        panels += [[(value, False), (paired(value), True)] for value in (rising, falling)]
        classes += [columns - distance, distance]
        saved = [] if distance == reach else [half]
        scalars = scalar_list(*classes, layer)
        total = product_sums(packed, scalars, shape, 2, panels, rights, total, half, saved)
        panels, classes = [], []
    return total[0][None, None, None]


def line(left_blocks, right_blocks, triples, half):
    own, right_own, step_lists = left_blocks[0, 0, 0], right_blocks[0, 0, 0], triples[0, 0, 0]
    slots, part = own.shape[0], right_own.shape[0]
    columns, layer, place = lax.axis_size("col"), lax.axis_index("dep"), lax.axis_index("col")
    shape = (step_lists.shape[0], columns, slots)
    inner = (place == 1) | (place == 2)
    low = place < 2
    outward, across, beside = [(2, 3), (1, 0)], [(1, 2), (2, 1)], [(0, 1), (1, 0), (2, 3), (3, 2)]
    fence = lax.optimization_barrier

    def hop(value, pairs):
        return lax.ppermute(value, "col", pairs)

    def right_slot(slot, layers):
        return (layers * 2 + ((slot // part) ^ lax.axis_index("row"))) * part + slot % part

    beside_one, across_one, across_two = hop(own, beside), hop(own, across), hop(own, [(0, 2), (3, 1)])
    met = lax.ppermute(right_own, "row", [(0, 1), (1, 0)])
    listed = layer_products(step_lists, layer, half, right_slot)
    classes = [0, jnp.where(place % 2 == 0, 1, 3), jnp.where(inner, jnp.where(low, 1, 3), -1)]
    classes += [jnp.where(inner, 2, -1), jnp.where(inner, -1, 2)]
    scalars = scalar_list(*classes, layer, jnp.where(inner, -1, jnp.where(low, 3, 1)))

    outer_two = hop(across_one, outward)
    beside_one, across_one, met, listed, scalars = fence((beside_one, across_one, met, listed, scalars))
    right_other, met_other = swapped(right_own), swapped(met)
    both = jnp.stack([step_lists, swapped(step_lists)])
    kept = kept_products(both, layer, half, right_slot)

    across_two, right_other, met_other, kept = fence((across_two, right_other, met_other, kept))
    outer_three = hop(across_two, outward)
    panels = [[(value, False)] for value in (own, beside_one, across_one, across_two, outer_two)]
    rights = [(value, False) for value in (right_own, met, right_other, met_other)]
    saved = [half // PARTS] * (PARTS - 1) + [half - half // PARTS * (PARTS - 1)]
    *parts, right, total = product_sums(
        listed, scalars, shape, 1, panels, rights, [], 2 * half, saved, "split"
    )
    total = add_received(total, [swapped(part) for part in parts])

    outer_three, total, right = fence((outer_three, total, right))
    kind_at = len(classes) + 1
    total = add_panel(kept, scalars, kind_at, shape, 0, outer_three, right, total, False)
    block = add_panel(kept, scalars, kind_at, shape, 1, swapped(outer_three), right, total, True)
    return block[None, None, None]


def local(left_blocks, right_blocks, triples):
    step_count = triples.shape[3]
    row_count, columns = lax.axis_size("row"), lax.axis_size("col")
    half = (2 * step_count - 2 + row_count) // row_count * NBQ // 2
    if columns >= step_count:
        return ring(left_blocks, right_blocks, triples, half)
    assert columns == 4 and row_count == 2
    return line(left_blocks, right_blocks, triples, half)


def solution(mesh):
    return jax.shard_map(
        local,
        mesh=mesh,
        in_specs=(
            P(("grp", "row"), "col", "dep", None, None, None),
            P(("grp", "row"), "col", "dep", None, None, None),
            P(("grp", "row"), "col", "dep", None, None, None),
        ),
        out_specs=P(("grp", "row"), "col", "dep", None, None, None),
        check_vma=False,
    )
```

```python
import functools

import jax
import jax.numpy as jnp
from jax import lax
from jax.experimental import pallas as pl
from jax.experimental.pallas import tpu as pltpu
from jax.sharding import PartitionSpec as P

NBQ = 32
UNROLL = 8
PARTS = 4


def chosen_products(packed, classes, panels, todo, shape, layers, spare, first_left=0):
    step_count, columns, slots = shape
    count = jnp.int32(0)
    for panel in range(panels):
        kind = classes[panel]
        for extra in range(-(-step_count // columns)):
            step = lax.rem(kind + step_count // 2, columns) + extra * columns
            groups = jnp.where((kind >= 0) & (step < step_count), slots // 8, 0)
            for layer in range(layers):
                base = (layer * step_count + step) * slots

                def keep(group, count):
                    for lane in range(8):
                        entry = packed[base + group * 8 + lane]
                        todo[count] = entry + (panel * layers * slots << 10)
                        count += (entry >= 0).astype(jnp.int32)
                    return count

                count = lax.fori_loop(0, groups, keep, count)
    for extra in range(UNROLL - 1):
        todo[count + extra] = jnp.int32(first_left << 10 | spare)
    return count


def add_chosen(todo, count, left, right, work, first_left=0):
    def several(group, carry):
        entries = [todo[group * UNROLL + lane] for lane in range(UNROLL)]
        products = [
            jnp.dot(
                left[((entry >> 10) & 1023) - first_left],
                right[entry >> 20],
                preferred_element_type=jnp.float32,
            )
            for entry in entries
        ]
        for entry, product in zip(entries, products):
            work[entry & 1023] += product
        return carry

    lax.fori_loop(0, (count + UNROLL - 1) // UNROLL, several, jnp.int32(0))


def sum_kernel(panels, rights, givens, saved, mode, shape, layers, operand_count, layer_at, *refs):
    packed, classes, refs = refs[0], refs[1], refs[2:]
    operands, refs = refs[:operand_count], refs[operand_count:]
    out_count = max(len(saved), 1)
    outs, refs = refs[:out_count], refs[out_count:]
    if mode == "split":
        (right, kept), (work, left, todo, sems) = refs[:2], refs[2:]
    else:
        work, left, right, todo, sems = refs
    spare = work.shape[0] - 1
    other = 1 - classes[layer_at]
    copies = []

    def plan(source, target, when=None):
        copies.append((pltpu.make_async_copy(source, target, sems.at[len(copies)]), when))

    start = 0
    for operand, size, gathered in rights:
        source = operands[operand]
        if gathered:
            source = source.at[pl.ds(other * size, size)]
        plan(source, right.at[pl.ds(start, size)])
        start += size
    start = 0
    for panel, pieces in enumerate(panels):
        for operand, size, gathered in pieces:
            source = operands[operand]
            if gathered:
                source = source.at[pl.ds(other * size, size)]
            plan(source, left.at[pl.ds(start, size)], classes[panel] >= 0)
            start += size
    start = 0
    for operand, size in givens:
        plan(operands[operand], work.at[pl.ds(start, size)])
        start += size
    for copy, when in copies:
        copy.start() if when is None else pl.when(when)(copy.start)
    if givens:
        work[spare] = jnp.zeros_like(work[spare])
    else:
        work[...] = jnp.zeros_like(work)
    kinds = [classes[panel] for panel in range(len(panels))]
    count = chosen_products(packed, kinds, len(panels), todo, shape, layers, spare)
    for copy, when in copies:
        copy.wait() if when is None else pl.when(when)(copy.wait)
    add_chosen(todo, count, left, right, work)
    if not saved:
        outs[0][...] = work[:spare].astype(outs[0].dtype)
        return
    start, copies, targets = 0, [], list(outs)
    if mode == "split":
        kept[kept.shape[0] - 1] = jnp.zeros(kept.shape[1:], kept.dtype)
        targets.insert(0, kept.at[pl.ds(0, kept.shape[0] - 1)])
    for out in targets:
        size = out.shape[0]
        copies.append(pltpu.make_async_copy(work.at[pl.ds(start, size)], out, sems.at[len(copies)]))
        start += size
    for copy in copies:
        copy.start()
    for copy in copies:
        copy.wait()


def product_sums(packed, scalars, shape, layers, panels, rights, givens, result_slots, saved, mode="whole"):
    step_count, columns, slots = shape
    rows, width = rights[0][0].shape[1:]
    operands = []

    def number(value):
        for index, known in enumerate(operands):
            if known is value:
                return index
        operands.append(value)
        return len(operands) - 1

    def spans(pieces):
        return [
            (number(value), value.shape[0] // 2 if gathered else value.shape[0], gathered)
            for value, gathered in pieces
        ]

    right_spans = spans(rights)
    panel_spans = [spans(pieces) for pieces in panels]
    given_spans = [(number(value), value.shape[0]) for value in givens]
    right_slots = sum(size for _, size, _ in right_spans)
    left_slots = len(panels) * layers * slots
    assert right_slots <= 1024 and left_slots <= 1024 and result_slots < 1024 and slots % 8 == 0
    assert all(sum(size for _, size, _ in pieces) == layers * slots for pieces in panel_spans)
    anywhere = pl.BlockSpec(memory_space=pl.ANY)
    in_scalar, in_vector = pl.BlockSpec(memory_space=pltpu.SMEM), pl.BlockSpec(memory_space=pltpu.VMEM)
    copy_count = len(rights) + sum(len(pieces) for pieces in panels) + len(givens) + len(saved) + 1
    scratch = [
        pltpu.VMEM((result_slots + 1, rows, width), jnp.float32),
        pltpu.VMEM((left_slots, rows, width), jnp.bfloat16),
        pltpu.VMEM((right_slots, width, width), jnp.bfloat16),
    ]
    if saved:
        out_shape = [jax.ShapeDtypeStruct((size, rows, width), jnp.float32) for size in saved]
    else:
        out_shape = [jax.ShapeDtypeStruct((result_slots, rows, width), jnp.bfloat16)]
    out_specs = [anywhere if saved else in_vector] * len(out_shape)
    if mode == "split":
        out_shape += [scratch.pop(), pltpu.VMEM((result_slots - sum(saved) + 1, rows, width), jnp.float32)]
        out_specs += [in_vector] * 2
    return pl.pallas_call(
        functools.partial(
            sum_kernel,
            panel_spans,
            right_spans,
            given_spans,
            saved,
            mode,
            shape,
            layers,
            len(operands),
            len(panels),
        ),
        out_shape=out_shape,
        in_specs=[in_scalar, in_scalar] + [anywhere] * len(operands),
        out_specs=out_specs,
        scratch_shapes=scratch
        + [
            pltpu.SMEM((len(panels) * -(-step_count // columns) * layers * slots + UNROLL,), jnp.int32),
            pltpu.SemaphoreType.DMA((copy_count,)),
        ],
        compiler_params=pltpu.CompilerParams(vmem_limit_bytes=(34 if mode == "split" else 56) << 20),
        cost_estimate=pl.CostEstimate(flops=1, bytes_accessed=1, transcendentals=0),
    )(packed, scalars, *operands)


def received_kernel(given, *refs):
    del given
    work, start = refs[-1], 0
    for piece in refs[:-1]:
        span = pl.ds(start, piece.shape[0])
        work[span] += piece[...]
        start += piece.shape[0]


def add_received(given, pieces):
    in_vector = pl.BlockSpec(memory_space=pltpu.VMEM)
    return pl.pallas_call(
        received_kernel,
        out_shape=pltpu.VMEM(given.shape, given.dtype),
        in_specs=[in_vector] * (1 + len(pieces)),
        out_specs=in_vector,
        input_output_aliases={0: 0},
        compiler_params=pltpu.CompilerParams(vmem_limit_bytes=12 << 20),
        cost_estimate=pl.CostEstimate(flops=1, bytes_accessed=1, transcendentals=0),
    )(given, *pieces)


def panel_kernel(shape, layer, kind_at, finish, packed, scalars, right, given, left, *refs):
    del given
    step_count, columns, slots = shape
    work, todo = (refs[1], refs[2]) if finish else (refs[0], refs[1])
    spare, first = work.shape[0] - 1, layer * slots
    part = packed.at[pl.ds(layer * step_count * slots, step_count * slots)]
    count = chosen_products(part, [scalars[kind_at]], 1, todo, shape, 1, spare, first)
    add_chosen(todo, count, left, right, work, first)
    if finish:
        out, rounded, sems = refs[0], refs[3], refs[4]
        size = spare // PARTS
        copies = []
        for index in range(PARTS):
            span = pl.ds(index * size, size if index < PARTS - 1 else spare - index * size)
            rounded[span] = work[span].astype(rounded.dtype)
            copies.append(pltpu.make_async_copy(rounded.at[span], out.at[span], sems.at[index]))
            copies[-1].start()
        for copy in copies:
            copy.wait()


def add_panel(packed, scalars, kind_at, shape, layer, panel, right, given, finish):
    step_count, columns, slots = shape
    result_slots, rows, width = given.shape[0] - 1, *given.shape[1:]
    in_scalar, in_vector = pl.BlockSpec(memory_space=pltpu.SMEM), pl.BlockSpec(memory_space=pltpu.VMEM)
    out_shape, out_specs = [pltpu.VMEM(given.shape, given.dtype)], [in_vector]
    scratch = [pltpu.SMEM((-(-step_count // columns) * slots + UNROLL,), jnp.int32)]
    if finish:
        out_shape.insert(0, jax.ShapeDtypeStruct((result_slots, rows, width), jnp.bfloat16))
        out_specs.insert(0, pl.BlockSpec(memory_space=pl.ANY))
        scratch.append(pltpu.VMEM((result_slots, rows, width), jnp.bfloat16))
        scratch.append(pltpu.SemaphoreType.DMA((PARTS,)))
    return pl.pallas_call(
        functools.partial(panel_kernel, shape, layer, kind_at, finish),
        out_shape=out_shape,
        in_specs=[in_scalar] * 2 + [in_vector] * 3,
        out_specs=out_specs,
        scratch_shapes=scratch,
        input_output_aliases={3: len(out_shape) - 1},
        compiler_params=pltpu.CompilerParams(vmem_limit_bytes=12 << 20),
        cost_estimate=pl.CostEstimate(flops=1, bytes_accessed=1, transcendentals=0),
    )(packed, scalars, right, given, panel)[0]


def scalar_list(*values):
    return jnp.stack([jnp.asarray(value, jnp.int32) for value in values])


def swapped(value):
    return lax.ppermute(value, "dep", [(0, 1), (1, 0)])


def paired(value):
    return lax.all_gather(value, "dep", axis=0, tiled=True)


def kept_products(both, layer, half, right_slot):
    slots = both.shape[3]
    result = both[:, :, 2] - layer * half
    wanted = (result >= 0) & (result < half)
    layers = jnp.arange(2, dtype=jnp.int32)[:, None, None]
    packed = right_slot(both[:, :, 1], layers) << 20 | (layers * slots + both[:, :, 0]) << 10 | result
    return jnp.where(wanted, packed, -1).reshape(-1)


def layer_products(step_lists, layer, half, right_slot):
    result = step_lists[:, 2]
    turned = jnp.where(result < half, result + layer * half, result - layer * half)
    packed = right_slot(step_lists[:, 1], 0) << 20 | step_lists[:, 0] << 10 | turned
    return jnp.where(result < 2 * half, packed, -1).reshape(-1)


def ring(left_blocks, right_blocks, triples, half):
    own, right_own, step_lists = left_blocks[0, 0, 0], right_blocks[0, 0, 0], triples[0, 0, 0]
    columns, layer = lax.axis_size("col"), lax.axis_index("dep")
    gathered = lax.all_gather(right_own, "row", axis=0, tiled=True)
    right_slots = gathered.shape[0]
    both = jnp.stack([step_lists, swapped(step_lists)])
    packed = kept_products(both, layer, half, lambda slot, layers: layers * right_slots + slot)
    rights = [(gathered, False), (swapped(gathered), False)]
    shape = (step_lists.shape[0], columns, own.shape[0])
    rising, falling, total = own, own, []
    panels, classes = [[(own, False), (paired(own), True)]], [0]
    reach = step_lists.shape[0] // 2
    for distance in range(1, reach + 1):
        rising = lax.ppermute(rising, "col", [(i, (i + 1) % columns) for i in range(columns)])
        falling = lax.ppermute(falling, "col", [(i, (i - 1) % columns) for i in range(columns)])
        panels += [[(value, False), (paired(value), True)] for value in (rising, falling)]
        classes += [columns - distance, distance]
        saved = [] if distance == reach else [half]
        scalars = scalar_list(*classes, layer)
        total = product_sums(packed, scalars, shape, 2, panels, rights, total, half, saved)
        panels, classes = [], []
    return total[0][None, None, None]


def line(left_blocks, right_blocks, triples, half):
    own, right_own, step_lists = left_blocks[0, 0, 0], right_blocks[0, 0, 0], triples[0, 0, 0]
    slots, part = own.shape[0], right_own.shape[0]
    columns, layer, place = lax.axis_size("col"), lax.axis_index("dep"), lax.axis_index("col")
    shape = (step_lists.shape[0], columns, slots)
    inner = (place == 1) | (place == 2)
    low = place < 2
    outward, across, beside = [(2, 3), (1, 0)], [(1, 2), (2, 1)], [(0, 1), (1, 0), (2, 3), (3, 2)]
    fence = lax.optimization_barrier

    def hop(value, pairs):
        return lax.ppermute(value, "col", pairs)

    def right_slot(slot, layers):
        return (layers * 2 + ((slot // part) ^ lax.axis_index("row"))) * part + slot % part

    beside_one, across_one = hop(own, beside), hop(own, across)
    met = lax.ppermute(right_own, "row", [(0, 1), (1, 0)])
    sent_late, met = fence((own, met))
    across_two = hop(sent_late, [(0, 2), (3, 1)])
    listed = layer_products(step_lists, layer, half, right_slot)
    classes = [0, jnp.where(place % 2 == 0, 1, 3), jnp.where(inner, jnp.where(low, 1, 3), -1)]
    classes += [jnp.where(inner, 2, -1), jnp.where(inner, -1, 2)]
    scalars = scalar_list(*classes, layer, jnp.where(inner, -1, jnp.where(low, 3, 1)))

    outer_two = hop(across_one, outward)
    beside_one, across_one, met, listed, scalars = fence((beside_one, across_one, met, listed, scalars))
    right_other, met_other = swapped(right_own), swapped(met)
    both = jnp.stack([step_lists, swapped(step_lists)])
    kept = kept_products(both, layer, half, right_slot)

    across_two, right_other, met_other, kept = fence((across_two, right_other, met_other, kept))
    outer_three = hop(across_two, outward)
    panels = [[(value, False)] for value in (own, beside_one, across_one, across_two, outer_two)]
    rights = [(value, False) for value in (right_own, met, right_other, met_other)]
    saved = [half // PARTS] * (PARTS - 1) + [half - half // PARTS * (PARTS - 1)]
    *parts, right, total = product_sums(
        listed, scalars, shape, 1, panels, rights, [], 2 * half, saved, "split"
    )
    total = add_received(total, [swapped(part) for part in parts])

    outer_three, total, right = fence((outer_three, total, right))
    kind_at = len(classes) + 1
    total = add_panel(kept, scalars, kind_at, shape, 0, outer_three, right, total, False)
    block = add_panel(kept, scalars, kind_at, shape, 1, swapped(outer_three), right, total, True)
    return block[None, None, None]


def local(left_blocks, right_blocks, triples):
    step_count = triples.shape[3]
    row_count, columns = lax.axis_size("row"), lax.axis_size("col")
    half = (2 * step_count - 2 + row_count) // row_count * NBQ // 2
    if columns >= step_count:
        return ring(left_blocks, right_blocks, triples, half)
    assert columns == 4 and row_count == 2
    return line(left_blocks, right_blocks, triples, half)


def solution(mesh):
    return jax.shard_map(
        local,
        mesh=mesh,
        in_specs=(
            P(("grp", "row"), "col", "dep", None, None, None),
            P(("grp", "row"), "col", "dep", None, None, None),
            P(("grp", "row"), "col", "dep", None, None, None),
        ),
        out_specs=P(("grp", "row"), "col", "dep", None, None, None),
        check_vma=False,
    )
```

```python
import functools

import jax
import jax.numpy as jnp
from jax import lax
from jax.experimental import pallas as pl
from jax.experimental.pallas import tpu as pltpu
from jax.sharding import PartitionSpec as P

NBQ = 32
UNROLL = 16
PARTS = 4
OUT_PARTS = 8


def chosen_products(packed, classes, panels, todo, shape, layers, spare, first_left=0):
    step_count, columns, slots = shape
    count = jnp.int32(0)
    for panel in range(panels):
        kind = classes[panel]
        for extra in range(-(-step_count // columns)):
            step = lax.rem(kind + step_count // 2, columns) + extra * columns
            groups = jnp.where((kind >= 0) & (step < step_count), slots // 8, 0)
            for layer in range(layers):
                base = (layer * step_count + step) * slots

                def keep(group, count):
                    for lane in range(8):
                        entry = packed[base + group * 8 + lane]
                        todo[count] = entry + (panel * layers * slots << 10)
                        count += (entry >= 0).astype(jnp.int32)
                    return count

                count = lax.fori_loop(0, groups, keep, count)
    for extra in range(UNROLL - 1):
        todo[count + extra] = jnp.int32(first_left << 10 | spare)
    return count


def add_chosen(todo, count, left, right, work, first_left=0):
    def several(group, carry):
        entries = [todo[group * UNROLL + lane] for lane in range(UNROLL)]
        products = [
            jnp.dot(
                left[((entry >> 10) & 1023) - first_left],
                right[entry >> 20],
                preferred_element_type=jnp.float32,
            )
            for entry in entries
        ]
        for entry, product in zip(entries, products):
            work[entry & 1023] += product
        return carry

    lax.fori_loop(0, (count + UNROLL - 1) // UNROLL, several, jnp.int32(0))


def sum_kernel(panels, rights, givens, saved, mode, shape, layers, operand_count, layer_at, *refs):
    packed, classes, refs = refs[0], refs[1], refs[2:]
    operands, refs = refs[:operand_count], refs[operand_count:]
    out_count = max(len(saved), 1)
    outs, refs = refs[:out_count], refs[out_count:]
    if mode == "split":
        (right, kept), (work, left, todo, sems) = refs[:2], refs[2:]
    else:
        work, left, right, todo, sems = refs
    spare = work.shape[0] - 1
    other = 1 - classes[layer_at]
    copies = []

    def plan(source, target, when=None):
        copies.append((pltpu.make_async_copy(source, target, sems.at[len(copies)]), when))

    start = 0
    for operand, size, gathered in rights:
        source = operands[operand]
        if gathered:
            source = source.at[pl.ds(other * size, size)]
        plan(source, right.at[pl.ds(start, size)])
        start += size
    start = 0
    for panel, pieces in enumerate(panels):
        for operand, size, gathered in pieces:
            source = operands[operand]
            if gathered:
                source = source.at[pl.ds(other * size, size)]
            plan(source, left.at[pl.ds(start, size)], classes[panel] >= 0)
            start += size
    start = 0
    for operand, size in givens:
        plan(operands[operand], work.at[pl.ds(start, size)])
        start += size
    for copy, when in copies:
        copy.start() if when is None else pl.when(when)(copy.start)
    if givens:
        work[spare] = jnp.zeros_like(work[spare])
    else:
        work[...] = jnp.zeros_like(work)
    kinds = [classes[panel] for panel in range(len(panels))]
    count = chosen_products(packed, kinds, len(panels), todo, shape, layers, spare)
    for copy, when in copies:
        copy.wait() if when is None else pl.when(when)(copy.wait)
    add_chosen(todo, count, left, right, work)
    if not saved:
        outs[0][...] = work[:spare].astype(outs[0].dtype)
        return
    start, copies, targets = 0, [], list(outs)
    if mode == "split":
        kept[kept.shape[0] - 1] = jnp.zeros(kept.shape[1:], kept.dtype)
        targets.insert(0, kept.at[pl.ds(0, kept.shape[0] - 1)])
    for out in targets:
        size = out.shape[0]
        copies.append(pltpu.make_async_copy(work.at[pl.ds(start, size)], out, sems.at[len(copies)]))
        start += size
    for copy in copies:
        copy.start()
    for copy in copies:
        copy.wait()


def product_sums(packed, scalars, shape, layers, panels, rights, givens, result_slots, saved, mode="whole"):
    step_count, columns, slots = shape
    rows, width = rights[0][0].shape[1:]
    operands = []

    def number(value):
        for index, known in enumerate(operands):
            if known is value:
                return index
        operands.append(value)
        return len(operands) - 1

    def spans(pieces):
        return [
            (number(value), value.shape[0] // 2 if gathered else value.shape[0], gathered)
            for value, gathered in pieces
        ]

    right_spans = spans(rights)
    panel_spans = [spans(pieces) for pieces in panels]
    given_spans = [(number(value), value.shape[0]) for value in givens]
    right_slots = sum(size for _, size, _ in right_spans)
    left_slots = len(panels) * layers * slots
    assert right_slots <= 1024 and left_slots <= 1024 and result_slots < 1024 and slots % 8 == 0
    assert all(sum(size for _, size, _ in pieces) == layers * slots for pieces in panel_spans)
    anywhere = pl.BlockSpec(memory_space=pl.ANY)
    in_scalar, in_vector = pl.BlockSpec(memory_space=pltpu.SMEM), pl.BlockSpec(memory_space=pltpu.VMEM)
    copy_count = len(rights) + sum(len(pieces) for pieces in panels) + len(givens) + len(saved) + 1
    scratch = [
        pltpu.VMEM((result_slots + 1, rows, width), jnp.float32),
        pltpu.VMEM((left_slots, rows, width), jnp.bfloat16),
        pltpu.VMEM((right_slots, width, width), jnp.bfloat16),
    ]
    if saved:
        out_shape = [jax.ShapeDtypeStruct((size, rows, width), jnp.float32) for size in saved]
    else:
        out_shape = [jax.ShapeDtypeStruct((result_slots, rows, width), jnp.bfloat16)]
    out_specs = [anywhere if saved else in_vector] * len(out_shape)
    if mode == "split":
        out_shape += [scratch.pop(), pltpu.VMEM((result_slots - sum(saved) + 1, rows, width), jnp.float32)]
        out_specs += [in_vector] * 2
    return pl.pallas_call(
        functools.partial(
            sum_kernel,
            panel_spans,
            right_spans,
            given_spans,
            saved,
            mode,
            shape,
            layers,
            len(operands),
            len(panels),
        ),
        out_shape=out_shape,
        in_specs=[in_scalar, in_scalar] + [anywhere] * len(operands),
        out_specs=out_specs,
        scratch_shapes=scratch
        + [
            pltpu.SMEM((len(panels) * -(-step_count // columns) * layers * slots + UNROLL,), jnp.int32),
            pltpu.SemaphoreType.DMA((copy_count,)),
        ],
        compiler_params=pltpu.CompilerParams(vmem_limit_bytes=(34 if mode == "split" else 56) << 20),
        cost_estimate=pl.CostEstimate(flops=1, bytes_accessed=1, transcendentals=0),
    )(packed, scalars, *operands)


def received_kernel(given, *refs):
    del given
    work, start = refs[-1], 0
    for piece in refs[:-1]:
        span = pl.ds(start, piece.shape[0])
        work[span] += piece[...]
        start += piece.shape[0]


def add_received(given, pieces):
    in_vector = pl.BlockSpec(memory_space=pltpu.VMEM)
    return pl.pallas_call(
        received_kernel,
        out_shape=pltpu.VMEM(given.shape, given.dtype),
        in_specs=[in_vector] * (1 + len(pieces)),
        out_specs=in_vector,
        input_output_aliases={0: 0},
        compiler_params=pltpu.CompilerParams(vmem_limit_bytes=12 << 20),
        cost_estimate=pl.CostEstimate(flops=1, bytes_accessed=1, transcendentals=0),
    )(given, *pieces)


def panel_kernel(shape, layer, kind_at, finish, packed, scalars, right, given, left, *refs):
    del given
    step_count, columns, slots = shape
    work, todo = (refs[1], refs[2]) if finish else (refs[0], refs[1])
    spare, first = work.shape[0] - 1, layer * slots
    part = packed.at[pl.ds(layer * step_count * slots, step_count * slots)]
    count = chosen_products(part, [scalars[kind_at]], 1, todo, shape, 1, spare, first)
    add_chosen(todo, count, left, right, work, first)
    if finish:
        out, rounded, sems = refs[0], refs[3], refs[4]
        size = spare // OUT_PARTS
        copies = []
        for index in range(OUT_PARTS):
            span = pl.ds(index * size, size if index < OUT_PARTS - 1 else spare - index * size)
            rounded[span] = work[span].astype(rounded.dtype)
            copies.append(pltpu.make_async_copy(rounded.at[span], out.at[span], sems.at[index]))
            copies[-1].start()
        for copy in copies:
            copy.wait()


def add_panel(packed, scalars, kind_at, shape, layer, panel, right, given, finish):
    step_count, columns, slots = shape
    result_slots, rows, width = given.shape[0] - 1, *given.shape[1:]
    in_scalar, in_vector = pl.BlockSpec(memory_space=pltpu.SMEM), pl.BlockSpec(memory_space=pltpu.VMEM)
    out_shape, out_specs = [pltpu.VMEM(given.shape, given.dtype)], [in_vector]
    scratch = [pltpu.SMEM((-(-step_count // columns) * slots + UNROLL,), jnp.int32)]
    if finish:
        out_shape.insert(0, jax.ShapeDtypeStruct((result_slots, rows, width), jnp.bfloat16))
        out_specs.insert(0, pl.BlockSpec(memory_space=pl.ANY))
        scratch.append(pltpu.VMEM((result_slots, rows, width), jnp.bfloat16))
        scratch.append(pltpu.SemaphoreType.DMA((OUT_PARTS,)))
    return pl.pallas_call(
        functools.partial(panel_kernel, shape, layer, kind_at, finish),
        out_shape=out_shape,
        in_specs=[in_scalar] * 2 + [in_vector] * 3,
        out_specs=out_specs,
        scratch_shapes=scratch,
        input_output_aliases={3: len(out_shape) - 1},
        compiler_params=pltpu.CompilerParams(vmem_limit_bytes=12 << 20),
        cost_estimate=pl.CostEstimate(flops=1, bytes_accessed=1, transcendentals=0),
    )(packed, scalars, right, given, panel)[0]


def scalar_list(*values):
    return jnp.stack([jnp.asarray(value, jnp.int32) for value in values])


def swapped(value):
    return lax.ppermute(value, "dep", [(0, 1), (1, 0)])


def paired(value):
    return lax.all_gather(value, "dep", axis=0, tiled=True)


def kept_products(both, layer, half, right_slot):
    slots = both.shape[3]
    result = both[:, :, 2] - layer * half
    wanted = (result >= 0) & (result < half)
    layers = jnp.arange(2, dtype=jnp.int32)[:, None, None]
    packed = right_slot(both[:, :, 1], layers) << 20 | (layers * slots + both[:, :, 0]) << 10 | result
    return jnp.where(wanted, packed, -1).reshape(-1)


def layer_products(step_lists, layer, half, right_slot):
    result = step_lists[:, 2]
    turned = jnp.where(result < half, result + layer * half, result - layer * half)
    packed = right_slot(step_lists[:, 1], 0) << 20 | step_lists[:, 0] << 10 | turned
    return jnp.where(result < 2 * half, packed, -1).reshape(-1)


def ring(left_blocks, right_blocks, triples, half):
    own, right_own, step_lists = left_blocks[0, 0, 0], right_blocks[0, 0, 0], triples[0, 0, 0]
    columns, layer = lax.axis_size("col"), lax.axis_index("dep")
    gathered = lax.all_gather(right_own, "row", axis=0, tiled=True)
    right_slots = gathered.shape[0]
    both = jnp.stack([step_lists, swapped(step_lists)])
    packed = kept_products(both, layer, half, lambda slot, layers: layers * right_slots + slot)
    rights = [(gathered, False), (swapped(gathered), False)]
    shape = (step_lists.shape[0], columns, own.shape[0])
    rising, falling, total = own, own, []
    panels, classes = [[(own, False), (paired(own), True)]], [0]
    reach = step_lists.shape[0] // 2
    for distance in range(1, reach + 1):
        rising = lax.ppermute(rising, "col", [(i, (i + 1) % columns) for i in range(columns)])
        falling = lax.ppermute(falling, "col", [(i, (i - 1) % columns) for i in range(columns)])
        panels += [[(value, False), (paired(value), True)] for value in (rising, falling)]
        classes += [columns - distance, distance]
        saved = [] if distance == reach else [half]
        scalars = scalar_list(*classes, layer)
        total = product_sums(packed, scalars, shape, 2, panels, rights, total, half, saved)
        panels, classes = [], []
    return total[0][None, None, None]


def line(left_blocks, right_blocks, triples, half):
    own, right_own, step_lists = left_blocks[0, 0, 0], right_blocks[0, 0, 0], triples[0, 0, 0]
    slots, part = own.shape[0], right_own.shape[0]
    columns, layer, place = lax.axis_size("col"), lax.axis_index("dep"), lax.axis_index("col")
    shape = (step_lists.shape[0], columns, slots)
    inner = (place == 1) | (place == 2)
    low = place < 2
    outward, across, beside = [(2, 3), (1, 0)], [(1, 2), (2, 1)], [(0, 1), (1, 0), (2, 3), (3, 2)]
    fence = lax.optimization_barrier

    def hop(value, pairs):
        return lax.ppermute(value, "col", pairs)

    def right_slot(slot, layers):
        return (layers * 2 + ((slot // part) ^ lax.axis_index("row"))) * part + slot % part

    beside_one, across_one, across_two = hop(own, beside), hop(own, across), hop(own, [(0, 2), (3, 1)])
    met = lax.ppermute(right_own, "row", [(0, 1), (1, 0)])
    listed = layer_products(step_lists, layer, half, right_slot)
    classes = [0, jnp.where(place % 2 == 0, 1, 3), jnp.where(inner, jnp.where(low, 1, 3), -1)]
    classes += [jnp.where(inner, 2, -1), jnp.where(inner, -1, 2)]
    scalars = scalar_list(*classes, layer, jnp.where(inner, -1, jnp.where(low, 3, 1)))

    outer_two = hop(across_one, outward)
    beside_one, across_one, met, listed, scalars = fence((beside_one, across_one, met, listed, scalars))
    right_other, met_other = swapped(right_own), swapped(met)
    both = jnp.stack([step_lists, swapped(step_lists)])
    kept = kept_products(both, layer, half, right_slot)

    across_two, right_other, met_other, kept = fence((across_two, right_other, met_other, kept))
    outer_three = hop(across_two, outward)
    panels = [[(value, False)] for value in (own, beside_one, across_one, across_two, outer_two)]
    rights = [(value, False) for value in (right_own, met, right_other, met_other)]
    saved = [half // PARTS] * (PARTS - 1) + [half - half // PARTS * (PARTS - 1)]
    *parts, right, total = product_sums(
        listed, scalars, shape, 1, panels, rights, [], 2 * half, saved, "split"
    )
    total = add_received(total, [swapped(part) for part in parts])

    outer_three, total, right = fence((outer_three, total, right))
    kind_at = len(classes) + 1
    total = add_panel(kept, scalars, kind_at, shape, 0, outer_three, right, total, False)
    block = add_panel(kept, scalars, kind_at, shape, 1, swapped(outer_three), right, total, True)
    return block[None, None, None]


def local(left_blocks, right_blocks, triples):
    step_count = triples.shape[3]
    row_count, columns = lax.axis_size("row"), lax.axis_size("col")
    half = (2 * step_count - 2 + row_count) // row_count * NBQ // 2
    if columns >= step_count:
        return ring(left_blocks, right_blocks, triples, half)
    assert columns == 4 and row_count == 2
    return line(left_blocks, right_blocks, triples, half)


def solution(mesh):
    return jax.shard_map(
        local,
        mesh=mesh,
        in_specs=(
            P(("grp", "row"), "col", "dep", None, None, None),
            P(("grp", "row"), "col", "dep", None, None, None),
            P(("grp", "row"), "col", "dep", None, None, None),
        ),
        out_specs=P(("grp", "row"), "col", "dep", None, None, None),
        check_vma=False,
    )
```

```python
import functools

import jax
import jax.numpy as jnp
from jax import lax
from jax.experimental import pallas as pl
from jax.experimental.pallas import tpu as pltpu
from jax.sharding import PartitionSpec as P

NBQ = 32
UNROLL = 16
PARTS = 4
OUT_PARTS = 8


def chosen_products(packed, classes, panels, todo, shape, layers, spare, first_left=0):
    step_count, columns, slots = shape
    count = jnp.int32(0)
    for panel in range(panels):
        kind = classes[panel]
        for extra in range(-(-step_count // columns)):
            step = lax.rem(kind + step_count // 2, columns) + extra * columns
            groups = jnp.where((kind >= 0) & (step < step_count), slots // 8, 0)
            for layer in range(layers):
                base = (layer * step_count + step) * slots

                def keep(group, count):
                    for lane in range(8):
                        entry = packed[base + group * 8 + lane]
                        todo[count] = entry + (panel * layers * slots << 10)
                        count += (entry >= 0).astype(jnp.int32)
                    return count

                count = lax.fori_loop(0, groups, keep, count)
    for extra in range(UNROLL - 1):
        todo[count + extra] = jnp.int32(first_left << 10 | spare)
    return count


def add_chosen(todo, count, left, right, work, first_left=0):
    def several(group, carry):
        entries = [todo[group * UNROLL + lane] for lane in range(UNROLL)]
        products = [
            jnp.dot(
                left[((entry >> 10) & 1023) - first_left],
                right[entry >> 20],
                preferred_element_type=jnp.float32,
            )
            for entry in entries
        ]
        for entry, product in zip(entries, products):
            work[entry & 1023] += product
        return carry

    lax.fori_loop(0, (count + UNROLL - 1) // UNROLL, several, jnp.int32(0))


def sum_kernel(panels, rights, givens, saved, mode, shape, layers, operand_count, layer_at, *refs):
    packed, classes, refs = refs[0], refs[1], refs[2:]
    operands, refs = refs[:operand_count], refs[operand_count:]
    out_count = max(len(saved), 1)
    outs, refs = refs[:out_count], refs[out_count:]
    if mode == "split":
        (right, kept), (work, left, todo, sems) = refs[:2], refs[2:]
    else:
        work, left, right, todo, sems = refs
    spare = work.shape[0] - 1
    other = 1 - classes[layer_at]
    copies = []

    def plan(source, target, when=None):
        copies.append((pltpu.make_async_copy(source, target, sems.at[len(copies)]), when))

    start = 0
    for operand, size, gathered in rights:
        source = operands[operand]
        if gathered:
            source = source.at[pl.ds(other * size, size)]
        plan(source, right.at[pl.ds(start, size)])
        start += size
    start = 0
    for panel, pieces in enumerate(panels):
        for operand, size, gathered in pieces:
            source = operands[operand]
            if gathered:
                source = source.at[pl.ds(other * size, size)]
            plan(source, left.at[pl.ds(start, size)], classes[panel] >= 0)
            start += size
    start = 0
    for operand, size in givens:
        plan(operands[operand], work.at[pl.ds(start, size)])
        start += size
    for copy, when in copies:
        copy.start() if when is None else pl.when(when)(copy.start)
    if givens:
        work[spare] = jnp.zeros_like(work[spare])
    else:
        work[...] = jnp.zeros_like(work)
    kinds = [classes[panel] for panel in range(len(panels))]
    count = chosen_products(packed, kinds, len(panels), todo, shape, layers, spare)
    for copy, when in copies:
        copy.wait() if when is None else pl.when(when)(copy.wait)
    add_chosen(todo, count, left, right, work)
    if not saved:
        outs[0][...] = work[:spare].astype(outs[0].dtype)
        return
    start, copies, targets = 0, [], list(outs)
    if mode == "split":
        kept[kept.shape[0] - 1] = jnp.zeros(kept.shape[1:], kept.dtype)
        targets.insert(0, kept.at[pl.ds(0, kept.shape[0] - 1)])
    for out in targets:
        size = out.shape[0]
        copies.append(pltpu.make_async_copy(work.at[pl.ds(start, size)], out, sems.at[len(copies)]))
        start += size
    for copy in copies:
        copy.start()
    for copy in copies:
        copy.wait()


def product_sums(packed, scalars, shape, layers, panels, rights, givens, result_slots, saved, mode="whole"):
    step_count, columns, slots = shape
    rows, width = rights[0][0].shape[1:]
    operands = []

    def number(value):
        for index, known in enumerate(operands):
            if known is value:
                return index
        operands.append(value)
        return len(operands) - 1

    def spans(pieces):
        return [
            (number(value), value.shape[0] // 2 if gathered else value.shape[0], gathered)
            for value, gathered in pieces
        ]

    right_spans = spans(rights)
    panel_spans = [spans(pieces) for pieces in panels]
    given_spans = [(number(value), value.shape[0]) for value in givens]
    right_slots = sum(size for _, size, _ in right_spans)
    left_slots = len(panels) * layers * slots
    assert right_slots <= 1024 and left_slots <= 1024 and result_slots < 1024 and slots % 8 == 0
    assert all(sum(size for _, size, _ in pieces) == layers * slots for pieces in panel_spans)
    anywhere = pl.BlockSpec(memory_space=pl.ANY)
    in_scalar, in_vector = pl.BlockSpec(memory_space=pltpu.SMEM), pl.BlockSpec(memory_space=pltpu.VMEM)
    copy_count = len(rights) + sum(len(pieces) for pieces in panels) + len(givens) + len(saved) + 1
    scratch = [
        pltpu.VMEM((result_slots + 1, rows, width), jnp.float32),
        pltpu.VMEM((left_slots, rows, width), jnp.bfloat16),
        pltpu.VMEM((right_slots, width, width), jnp.bfloat16),
    ]
    if saved:
        out_shape = [jax.ShapeDtypeStruct((size, rows, width), jnp.float32) for size in saved]
    else:
        out_shape = [jax.ShapeDtypeStruct((result_slots, rows, width), jnp.bfloat16)]
    out_specs = [anywhere if saved else in_vector] * len(out_shape)
    if mode == "split":
        out_shape += [scratch.pop(), pltpu.VMEM((result_slots - sum(saved) + 1, rows, width), jnp.float32)]
        out_specs += [in_vector] * 2
    return pl.pallas_call(
        functools.partial(
            sum_kernel,
            panel_spans,
            right_spans,
            given_spans,
            saved,
            mode,
            shape,
            layers,
            len(operands),
            len(panels),
        ),
        out_shape=out_shape,
        in_specs=[in_scalar, in_scalar] + [anywhere] * len(operands),
        out_specs=out_specs,
        scratch_shapes=scratch
        + [
            pltpu.SMEM((len(panels) * -(-step_count // columns) * layers * slots + UNROLL,), jnp.int32),
            pltpu.SemaphoreType.DMA((copy_count,)),
        ],
        compiler_params=pltpu.CompilerParams(vmem_limit_bytes=(34 if mode == "split" else 56) << 20),
        cost_estimate=pl.CostEstimate(flops=1, bytes_accessed=1, transcendentals=0),
    )(packed, scalars, *operands)


def received_kernel(given, *refs):
    del given
    work, start = refs[-1], 0
    for piece in refs[:-1]:
        span = pl.ds(start, piece.shape[0])
        work[span] += piece[...]
        start += piece.shape[0]


def add_received(given, pieces):
    in_vector = pl.BlockSpec(memory_space=pltpu.VMEM)
    return pl.pallas_call(
        received_kernel,
        out_shape=pltpu.VMEM(given.shape, given.dtype),
        in_specs=[in_vector] * (1 + len(pieces)),
        out_specs=in_vector,
        input_output_aliases={0: 0},
        compiler_params=pltpu.CompilerParams(vmem_limit_bytes=12 << 20),
        cost_estimate=pl.CostEstimate(flops=1, bytes_accessed=1, transcendentals=0),
    )(given, *pieces)


def panel_kernel(shape, layer, kind_at, finish, packed, scalars, right, given, left, *refs):
    del given
    step_count, columns, slots = shape
    work, todo = (refs[1], refs[2]) if finish else (refs[0], refs[1])
    spare, first = work.shape[0] - 1, layer * slots
    part = packed.at[pl.ds(layer * step_count * slots, step_count * slots)]
    count = chosen_products(part, [scalars[kind_at]], 1, todo, shape, 1, spare, first)
    add_chosen(todo, count, left, right, work, first)
    if finish:
        out, rounded, sems = refs[0], refs[3], refs[4]
        size = spare // OUT_PARTS
        copies = []
        for index in range(OUT_PARTS):
            span = pl.ds(index * size, size if index < OUT_PARTS - 1 else spare - index * size)
            rounded[span] = work[span].astype(rounded.dtype)
            copies.append(pltpu.make_async_copy(rounded.at[span], out.at[span], sems.at[index]))
            copies[-1].start()
        for copy in copies:
            copy.wait()


def add_panel(packed, scalars, kind_at, shape, layer, panel, right, given, finish):
    step_count, columns, slots = shape
    result_slots, rows, width = given.shape[0] - 1, *given.shape[1:]
    in_scalar, in_vector = pl.BlockSpec(memory_space=pltpu.SMEM), pl.BlockSpec(memory_space=pltpu.VMEM)
    out_shape, out_specs = [pltpu.VMEM(given.shape, given.dtype)], [in_vector]
    scratch = [pltpu.SMEM((-(-step_count // columns) * slots + UNROLL,), jnp.int32)]
    if finish:
        out_shape.insert(0, jax.ShapeDtypeStruct((result_slots, rows, width), jnp.bfloat16))
        out_specs.insert(0, pl.BlockSpec(memory_space=pl.ANY))
        scratch.append(pltpu.VMEM((result_slots, rows, width), jnp.bfloat16))
        scratch.append(pltpu.SemaphoreType.DMA((OUT_PARTS,)))
    return pl.pallas_call(
        functools.partial(panel_kernel, shape, layer, kind_at, finish),
        out_shape=out_shape,
        in_specs=[in_scalar] * 2 + [in_vector] * 3,
        out_specs=out_specs,
        scratch_shapes=scratch,
        input_output_aliases={3: len(out_shape) - 1},
        compiler_params=pltpu.CompilerParams(vmem_limit_bytes=12 << 20),
        cost_estimate=pl.CostEstimate(flops=1, bytes_accessed=1, transcendentals=0),
    )(packed, scalars, right, given, panel)[0]


def scalar_list(*values):
    return jnp.stack([jnp.asarray(value, jnp.int32) for value in values])


def swapped(value):
    return lax.ppermute(value, "dep", [(0, 1), (1, 0)])


def paired(value):
    return lax.all_gather(value, "dep", axis=0, tiled=True)


def kept_products(both, layer, half, right_slot):
    slots = both.shape[3]
    result = both[:, :, 2] - layer * half
    wanted = (result >= 0) & (result < half)
    layers = jnp.arange(2, dtype=jnp.int32)[:, None, None]
    packed = right_slot(both[:, :, 1], layers) << 20 | (layers * slots + both[:, :, 0]) << 10 | result
    return jnp.where(wanted, packed, -1).reshape(-1)


def layer_products(step_lists, layer, half, right_slot):
    result = step_lists[:, 2]
    turned = jnp.where(result < half, result + layer * half, result - layer * half)
    packed = right_slot(step_lists[:, 1], 0) << 20 | step_lists[:, 0] << 10 | turned
    return jnp.where(result < 2 * half, packed, -1).reshape(-1)


def ring(left_blocks, right_blocks, triples, half):
    own, right_own, step_lists = left_blocks[0, 0, 0], right_blocks[0, 0, 0], triples[0, 0, 0]
    columns, layer = lax.axis_size("col"), lax.axis_index("dep")
    gathered = lax.all_gather(right_own, "row", axis=0, tiled=True)
    right_slots = gathered.shape[0]
    both = jnp.stack([step_lists, swapped(step_lists)])
    packed = kept_products(both, layer, half, lambda slot, layers: layers * right_slots + slot)
    rights = [(gathered, False), (swapped(gathered), False)]
    shape = (step_lists.shape[0], columns, own.shape[0])
    rising, falling, total = own, own, []
    panels, classes = [[(own, False), (paired(own), True)]], [0]
    reach = step_lists.shape[0] // 2
    for distance in range(1, reach + 1):
        rising = lax.ppermute(rising, "col", [(i, (i + 1) % columns) for i in range(columns)])
        falling = lax.ppermute(falling, "col", [(i, (i - 1) % columns) for i in range(columns)])
        panels += [[(value, False), (paired(value), True)] for value in (rising, falling)]
        classes += [columns - distance, distance]
        saved = [] if distance == reach else [half]
        scalars = scalar_list(*classes, layer)
        total = product_sums(packed, scalars, shape, 2, panels, rights, total, half, saved)
        panels, classes = [], []
    return total[0][None, None, None]


def line(left_blocks, right_blocks, triples, half):
    own, right_own, step_lists = left_blocks[0, 0, 0], right_blocks[0, 0, 0], triples[0, 0, 0]
    slots, part = own.shape[0], right_own.shape[0]
    columns, layer, place = lax.axis_size("col"), lax.axis_index("dep"), lax.axis_index("col")
    shape = (step_lists.shape[0], columns, slots)
    inner = (place == 1) | (place == 2)
    low = place < 2
    outward, across, beside = [(2, 3), (1, 0)], [(1, 2), (2, 1)], [(0, 1), (1, 0), (2, 3), (3, 2)]
    fence = lax.optimization_barrier

    def hop(value, pairs):
        return lax.ppermute(value, "col", pairs)

    def right_slot(slot, layers):
        return (layers * 2 + ((slot // part) ^ lax.axis_index("row"))) * part + slot % part

    beside_one, across_one, across_two = hop(own, beside), hop(own, across), hop(own, [(0, 2), (3, 1)])
    middle = part // 2
    met = [lax.ppermute(right_own[:middle], "row", [(0, 1), (1, 0)])]
    across_one, sent_late = fence((across_one, right_own[middle:]))
    late_met = lax.ppermute(sent_late, "row", [(0, 1), (1, 0)])
    listed = layer_products(step_lists, layer, half, right_slot)
    classes = [0, jnp.where(place % 2 == 0, 1, 3), jnp.where(inner, jnp.where(low, 1, 3), -1)]
    classes += [jnp.where(inner, 2, -1), jnp.where(inner, -1, 2)]
    scalars = scalar_list(*classes, layer, jnp.where(inner, -1, jnp.where(low, 3, 1)))

    outer_two = hop(across_one, outward)
    beside_one, across_one, met, listed, scalars = fence((beside_one, across_one, met, listed, scalars))
    met.append(late_met)
    right_other, met_other = swapped(right_own), [swapped(value) for value in met]
    both = jnp.stack([step_lists, swapped(step_lists)])
    kept = kept_products(both, layer, half, right_slot)

    across_two, right_other, met_other, kept = fence((across_two, right_other, met_other, kept))
    outer_three = hop(across_two, outward)
    panels = [[(value, False)] for value in (own, beside_one, across_one, across_two, outer_two)]
    rights = [(value, False) for value in (right_own, *met, right_other, *met_other)]
    saved = [half // PARTS] * (PARTS - 1) + [half - half // PARTS * (PARTS - 1)]
    *parts, right, total = product_sums(
        listed, scalars, shape, 1, panels, rights, [], 2 * half, saved, "split"
    )
    total = add_received(total, [swapped(part) for part in parts])

    outer_three, total, right = fence((outer_three, total, right))
    kind_at = len(classes) + 1
    total = add_panel(kept, scalars, kind_at, shape, 0, outer_three, right, total, False)
    block = add_panel(kept, scalars, kind_at, shape, 1, swapped(outer_three), right, total, True)
    return block[None, None, None]


def local(left_blocks, right_blocks, triples):
    step_count = triples.shape[3]
    row_count, columns = lax.axis_size("row"), lax.axis_size("col")
    half = (2 * step_count - 2 + row_count) // row_count * NBQ // 2
    if columns >= step_count:
        return ring(left_blocks, right_blocks, triples, half)
    assert columns == 4 and row_count == 2
    return line(left_blocks, right_blocks, triples, half)


def solution(mesh):
    return jax.shard_map(
        local,
        mesh=mesh,
        in_specs=(
            P(("grp", "row"), "col", "dep", None, None, None),
            P(("grp", "row"), "col", "dep", None, None, None),
            P(("grp", "row"), "col", "dep", None, None, None),
        ),
        out_specs=P(("grp", "row"), "col", "dep", None, None, None),
        check_vma=False,
    )
```

```python
import functools

import jax
import jax.numpy as jnp
from jax import lax
from jax.experimental import pallas as pl
from jax.experimental.pallas import tpu as pltpu
from jax.sharding import PartitionSpec as P

NBQ = 32
UNROLL = 16
PARTS = 4
PART_UNROLL = 8


def chosen_products(packed, classes, panels, todo, shape, layers, spare, first_left=0):
    step_count, columns, slots = shape
    count = jnp.int32(0)
    for panel in range(panels):
        kind = classes[panel]
        for extra in range(-(-step_count // columns)):
            step = lax.rem(kind + step_count // 2, columns) + extra * columns
            groups = jnp.where((kind >= 0) & (step < step_count), slots // 8, 0)
            for layer in range(layers):
                base = (layer * step_count + step) * slots

                def keep(group, count):
                    for lane in range(8):
                        entry = packed[base + group * 8 + lane]
                        todo[count] = entry + (panel * layers * slots << 10)
                        count += (entry >= 0).astype(jnp.int32)
                    return count

                count = lax.fori_loop(0, groups, keep, count)
    for extra in range(UNROLL - 1):
        todo[count + extra] = jnp.int32(first_left << 10 | spare)
    return count


def add_chosen(todo, count, left, right, work, first_left=0, start=0, unroll=UNROLL):
    def several(group, carry):
        entries = [todo[start + group * unroll + lane] for lane in range(unroll)]
        products = [
            jnp.dot(
                left[((entry >> 10) & 1023) - first_left],
                right[entry >> 20],
                preferred_element_type=jnp.float32,
            )
            for entry in entries
        ]
        for entry, product in zip(entries, products):
            work[entry & 1023] += product
        return carry

    lax.fori_loop(0, (count + unroll - 1) // unroll, several, jnp.int32(0))


def sort_products(packed, base, kind, shape, sorted_out, spare, first_left):
    step_count, columns, slots = shape
    room, counts, size = part_room(shape), PARTS * part_room(shape), spare // PARTS
    for part in range(PARTS):
        sorted_out[counts + part] = jnp.int32(0)
    for extra in range(-(-step_count // columns)):
        step = lax.rem(kind + step_count // 2, columns) + extra * columns
        groups = jnp.where((kind >= 0) & (step < step_count), slots // 8, 0)
        first = base + step * slots

        def place(group, carry):
            for lane in range(8):
                entry = packed[first + group * 8 + lane]
                result, part = entry & 1023, jnp.int32(0)
                for bound in range(1, PARTS):
                    part += (result >= bound * size).astype(jnp.int32)
                count = sorted_out[counts + part]
                sorted_out[part * room + count] = entry
                sorted_out[counts + part] = count + (entry >= 0).astype(jnp.int32)
            return carry

        lax.fori_loop(0, groups, place, jnp.int32(0))
    for part in range(PARTS):
        count = sorted_out[counts + part]
        for extra in range(PART_UNROLL - 1):
            sorted_out[part * room + count + extra] = jnp.int32(first_left << 10 | spare)


def part_room(shape):
    step_count, columns, slots = shape
    return -(-step_count // columns) * slots + PART_UNROLL


def sum_kernel(panels, rights, givens, saved, mode, shape, layers, operand_count, layer_at, *refs):
    packed, classes, refs = refs[0], refs[1], refs[2:]
    operands, refs = refs[:operand_count], refs[operand_count:]
    out_count = max(len(saved), 1)
    outs, refs = refs[:out_count], refs[out_count:]
    if mode == "split":
        (right, kept), (work, left, todo, sems) = refs[:2], refs[2:]
    else:
        work, left, right, todo, sems = refs
    spare = work.shape[0] - 1
    other = 1 - classes[layer_at]
    copies = []

    def plan(source, target, when=None):
        copies.append((pltpu.make_async_copy(source, target, sems.at[len(copies)]), when))

    start = 0
    for operand, size, gathered in rights:
        source = operands[operand]
        if gathered:
            source = source.at[pl.ds(other * size, size)]
        plan(source, right.at[pl.ds(start, size)])
        start += size
    start = 0
    for panel, pieces in enumerate(panels):
        for operand, size, gathered in pieces:
            source = operands[operand]
            if gathered:
                source = source.at[pl.ds(other * size, size)]
            plan(source, left.at[pl.ds(start, size)], classes[panel] >= 0)
            start += size
    start = 0
    for operand, size in givens:
        plan(operands[operand], work.at[pl.ds(start, size)])
        start += size
    for copy, when in copies:
        copy.start() if when is None else pl.when(when)(copy.start)
    if givens:
        work[spare] = jnp.zeros_like(work[spare])
    else:
        work[...] = jnp.zeros_like(work)
    kinds = [classes[panel] for panel in range(len(panels))]
    count = chosen_products(packed, kinds, len(panels), todo, shape, layers, spare)
    for copy, when in copies:
        copy.wait() if when is None else pl.when(when)(copy.wait)
    add_chosen(todo, count, left, right, work)
    if not saved:
        outs[0][...] = work[:spare].astype(outs[0].dtype)
        return
    start, copies, targets = 0, [], list(outs)
    if mode == "split":
        kept[kept.shape[0] - 1] = jnp.zeros(kept.shape[1:], kept.dtype)
        targets.insert(0, kept.at[pl.ds(0, kept.shape[0] - 1)])
    for out in targets:
        size = out.shape[0]
        copies.append(pltpu.make_async_copy(work.at[pl.ds(start, size)], out, sems.at[len(copies)]))
        start += size
    for copy in copies:
        copy.start()
    for copy in copies:
        copy.wait()


def product_sums(packed, scalars, shape, layers, panels, rights, givens, result_slots, saved, mode="whole"):
    step_count, columns, slots = shape
    rows, width = rights[0][0].shape[1:]
    operands = []

    def number(value):
        for index, known in enumerate(operands):
            if known is value:
                return index
        operands.append(value)
        return len(operands) - 1

    def spans(pieces):
        return [
            (number(value), value.shape[0] // 2 if gathered else value.shape[0], gathered)
            for value, gathered in pieces
        ]

    right_spans = spans(rights)
    panel_spans = [spans(pieces) for pieces in panels]
    given_spans = [(number(value), value.shape[0]) for value in givens]
    right_slots = sum(size for _, size, _ in right_spans)
    left_slots = len(panels) * layers * slots
    assert right_slots <= 1024 and left_slots <= 1024 and result_slots < 1024 and slots % 8 == 0
    assert all(sum(size for _, size, _ in pieces) == layers * slots for pieces in panel_spans)
    anywhere = pl.BlockSpec(memory_space=pl.ANY)
    in_scalar, in_vector = pl.BlockSpec(memory_space=pltpu.SMEM), pl.BlockSpec(memory_space=pltpu.VMEM)
    copy_count = len(rights) + sum(len(pieces) for pieces in panels) + len(givens) + len(saved) + 1
    scratch = [
        pltpu.VMEM((result_slots + 1, rows, width), jnp.float32),
        pltpu.VMEM((left_slots, rows, width), jnp.bfloat16),
        pltpu.VMEM((right_slots, width, width), jnp.bfloat16),
    ]
    if saved:
        out_shape = [jax.ShapeDtypeStruct((size, rows, width), jnp.float32) for size in saved]
    else:
        out_shape = [jax.ShapeDtypeStruct((result_slots, rows, width), jnp.bfloat16)]
    out_specs = [anywhere if saved else in_vector] * len(out_shape)
    if mode == "split":
        out_shape += [scratch.pop(), pltpu.VMEM((result_slots - sum(saved) + 1, rows, width), jnp.float32)]
        out_specs += [in_vector] * 2
    return pl.pallas_call(
        functools.partial(
            sum_kernel,
            panel_spans,
            right_spans,
            given_spans,
            saved,
            mode,
            shape,
            layers,
            len(operands),
            len(panels),
        ),
        out_shape=out_shape,
        in_specs=[in_scalar, in_scalar] + [anywhere] * len(operands),
        out_specs=out_specs,
        scratch_shapes=scratch
        + [
            pltpu.SMEM((len(panels) * -(-step_count // columns) * layers * slots + UNROLL,), jnp.int32),
            pltpu.SemaphoreType.DMA((copy_count,)),
        ],
        compiler_params=pltpu.CompilerParams(vmem_limit_bytes=(34 if mode == "split" else 56) << 20),
        cost_estimate=pl.CostEstimate(flops=1, bytes_accessed=1, transcendentals=0),
    )(packed, scalars, *operands)


def received_kernel(given, *refs):
    del given
    work, start = refs[-1], 0
    for piece in refs[:-1]:
        span = pl.ds(start, piece.shape[0])
        work[span] += piece[...]
        start += piece.shape[0]


def add_received(given, pieces):
    in_vector = pl.BlockSpec(memory_space=pltpu.VMEM)
    return pl.pallas_call(
        received_kernel,
        out_shape=pltpu.VMEM(given.shape, given.dtype),
        in_specs=[in_vector] * (1 + len(pieces)),
        out_specs=in_vector,
        input_output_aliases={0: 0},
        compiler_params=pltpu.CompilerParams(vmem_limit_bytes=12 << 20),
        cost_estimate=pl.CostEstimate(flops=1, bytes_accessed=1, transcendentals=0),
    )(given, *pieces)


def own_kernel(shape, kind_at, packed, scalars, right, given, left, work, sorted_out, todo):
    del given
    step_count, _, slots = shape
    spare, kind = work.shape[0] - 1, scalars[kind_at]
    count = chosen_products(packed, [kind], 1, todo, shape, 1, spare)
    add_chosen(todo, count, left, right, work)
    sort_products(packed, step_count * slots, kind, shape, sorted_out, spare, slots)


def add_own(packed, scalars, kind_at, shape, panel, right, given):
    step_count, columns, slots = shape
    in_scalar, in_vector = pl.BlockSpec(memory_space=pltpu.SMEM), pl.BlockSpec(memory_space=pltpu.VMEM)
    return pl.pallas_call(
        functools.partial(own_kernel, shape, kind_at),
        out_shape=[
            pltpu.VMEM(given.shape, given.dtype),
            jax.ShapeDtypeStruct((PARTS * part_room(shape) + PARTS,), jnp.int32),
        ],
        in_specs=[in_scalar] * 2 + [in_vector] * 3,
        out_specs=[in_vector, in_scalar],
        scratch_shapes=[pltpu.SMEM((-(-step_count // columns) * slots + UNROLL,), jnp.int32)],
        input_output_aliases={3: 0},
        compiler_params=pltpu.CompilerParams(vmem_limit_bytes=12 << 20),
        cost_estimate=pl.CostEstimate(flops=1, bytes_accessed=1, transcendentals=0),
    )(packed, scalars, right, given, panel)


def other_kernel(shape, sorted_lists, right, given, left, out, work, rounded, sems):
    del given
    slots, room, spare = shape[2], part_room(shape), work.shape[0] - 1
    size, copies = spare // PARTS, []
    for part in range(PARTS):
        count = sorted_lists[PARTS * room + part]
        add_chosen(sorted_lists, count, left, right, work, slots, part * room, PART_UNROLL)
        span = pl.ds(part * size, size if part < PARTS - 1 else spare - part * size)
        rounded[span] = work[span].astype(rounded.dtype)
        copies.append(pltpu.make_async_copy(rounded.at[span], out.at[span], sems.at[part]))
        copies[-1].start()
    for copy in copies:
        copy.wait()


def add_other(sorted_lists, shape, panel, right, given):
    result_slots, rows, width = given.shape[0] - 1, *given.shape[1:]
    in_scalar, in_vector = pl.BlockSpec(memory_space=pltpu.SMEM), pl.BlockSpec(memory_space=pltpu.VMEM)
    return pl.pallas_call(
        functools.partial(other_kernel, shape),
        out_shape=[
            jax.ShapeDtypeStruct((result_slots, rows, width), jnp.bfloat16),
            pltpu.VMEM(given.shape, given.dtype),
        ],
        in_specs=[in_scalar] + [in_vector] * 3,
        out_specs=[pl.BlockSpec(memory_space=pl.ANY), in_vector],
        scratch_shapes=[
            pltpu.VMEM((result_slots, rows, width), jnp.bfloat16),
            pltpu.SemaphoreType.DMA((PARTS,)),
        ],
        input_output_aliases={2: 1},
        compiler_params=pltpu.CompilerParams(vmem_limit_bytes=12 << 20),
        cost_estimate=pl.CostEstimate(flops=1, bytes_accessed=1, transcendentals=0),
    )(sorted_lists, right, given, panel)[0]


def scalar_list(*values):
    return jnp.stack([jnp.asarray(value, jnp.int32) for value in values])


def swapped(value):
    return lax.ppermute(value, "dep", [(0, 1), (1, 0)])


def paired(value):
    return lax.all_gather(value, "dep", axis=0, tiled=True)


def kept_products(both, layer, half, right_slot):
    slots = both.shape[3]
    result = both[:, :, 2] - layer * half
    wanted = (result >= 0) & (result < half)
    layers = jnp.arange(2, dtype=jnp.int32)[:, None, None]
    packed = right_slot(both[:, :, 1], layers) << 20 | (layers * slots + both[:, :, 0]) << 10 | result
    return jnp.where(wanted, packed, -1).reshape(-1)


def layer_products(step_lists, layer, half, right_slot):
    result = step_lists[:, 2]
    turned = jnp.where(result < half, result + layer * half, result - layer * half)
    packed = right_slot(step_lists[:, 1], 0) << 20 | step_lists[:, 0] << 10 | turned
    return jnp.where(result < 2 * half, packed, -1).reshape(-1)


def ring(left_blocks, right_blocks, triples, half):
    own, right_own, step_lists = left_blocks[0, 0, 0], right_blocks[0, 0, 0], triples[0, 0, 0]
    columns, layer = lax.axis_size("col"), lax.axis_index("dep")
    gathered = lax.all_gather(right_own, "row", axis=0, tiled=True)
    right_slots = gathered.shape[0]
    both = jnp.stack([step_lists, swapped(step_lists)])
    packed = kept_products(both, layer, half, lambda slot, layers: layers * right_slots + slot)
    rights = [(gathered, False), (swapped(gathered), False)]
    shape = (step_lists.shape[0], columns, own.shape[0])
    rising, falling, total = own, own, []
    panels, classes = [[(own, False), (paired(own), True)]], [0]
    reach = step_lists.shape[0] // 2
    for distance in range(1, reach + 1):
        rising = lax.ppermute(rising, "col", [(i, (i + 1) % columns) for i in range(columns)])
        falling = lax.ppermute(falling, "col", [(i, (i - 1) % columns) for i in range(columns)])
        panels += [[(value, False), (paired(value), True)] for value in (rising, falling)]
        classes += [columns - distance, distance]
        saved = [] if distance == reach else [half]
        scalars = scalar_list(*classes, layer)
        total = product_sums(packed, scalars, shape, 2, panels, rights, total, half, saved)
        panels, classes = [], []
    return total[0][None, None, None]


def line(left_blocks, right_blocks, triples, half):
    own, right_own, step_lists = left_blocks[0, 0, 0], right_blocks[0, 0, 0], triples[0, 0, 0]
    slots, part = own.shape[0], right_own.shape[0]
    columns, layer, place = lax.axis_size("col"), lax.axis_index("dep"), lax.axis_index("col")
    shape = (step_lists.shape[0], columns, slots)
    inner = (place == 1) | (place == 2)
    low = place < 2
    outward, across, beside = [(2, 3), (1, 0)], [(1, 2), (2, 1)], [(0, 1), (1, 0), (2, 3), (3, 2)]
    fence = lax.optimization_barrier

    def hop(value, pairs):
        return lax.ppermute(value, "col", pairs)

    def right_slot(slot, layers):
        return (layers * 2 + ((slot // part) ^ lax.axis_index("row"))) * part + slot % part

    beside_one, across_one, across_two = hop(own, beside), hop(own, across), hop(own, [(0, 2), (3, 1)])
    met = lax.ppermute(right_own, "row", [(0, 1), (1, 0)])
    listed = layer_products(step_lists, layer, half, right_slot)
    classes = [0, jnp.where(place % 2 == 0, 1, 3), jnp.where(inner, jnp.where(low, 1, 3), -1)]
    classes += [jnp.where(inner, 2, -1), jnp.where(inner, -1, 2)]
    scalars = scalar_list(*classes, layer, jnp.where(inner, -1, jnp.where(low, 3, 1)))

    outer_two = hop(across_one, outward)
    beside_one, across_one, met, listed, scalars = fence((beside_one, across_one, met, listed, scalars))
    right_other, met_other = swapped(right_own), swapped(met)
    both = jnp.stack([step_lists, swapped(step_lists)])
    kept = kept_products(both, layer, half, right_slot)

    across_two, right_other, met_other, kept = fence((across_two, right_other, met_other, kept))
    outer_three = hop(across_two, outward)
    panels = [[(value, False)] for value in (own, beside_one, across_one, across_two, outer_two)]
    rights = [(value, False) for value in (right_own, met, right_other, met_other)]
    saved = [half // PARTS] * (PARTS - 1) + [half - half // PARTS * (PARTS - 1)]
    *parts, right, total = product_sums(
        listed, scalars, shape, 1, panels, rights, [], 2 * half, saved, "split"
    )
    total = add_received(total, [swapped(part) for part in parts])

    outer_three, total, right = fence((outer_three, total, right))
    kind_at = len(classes) + 1
    total, sorted_lists = add_own(kept, scalars, kind_at, shape, outer_three, right, total)
    block = add_other(sorted_lists, shape, swapped(outer_three), right, total)
    return block[None, None, None]


def local(left_blocks, right_blocks, triples):
    step_count = triples.shape[3]
    row_count, columns = lax.axis_size("row"), lax.axis_size("col")
    half = (2 * step_count - 2 + row_count) // row_count * NBQ // 2
    if columns >= step_count:
        return ring(left_blocks, right_blocks, triples, half)
    assert columns == 4 and row_count == 2
    return line(left_blocks, right_blocks, triples, half)


def solution(mesh):
    return jax.shard_map(
        local,
        mesh=mesh,
        in_specs=(
            P(("grp", "row"), "col", "dep", None, None, None),
            P(("grp", "row"), "col", "dep", None, None, None),
            P(("grp", "row"), "col", "dep", None, None, None),
        ),
        out_specs=P(("grp", "row"), "col", "dep", None, None, None),
        check_vma=False,
    )
```

```python
import functools

import jax
import jax.numpy as jnp
from jax import lax
from jax.experimental import pallas as pl
from jax.experimental.pallas import tpu as pltpu
from jax.sharding import PartitionSpec as P

NBQ = 32
UNROLL = 16
PARTS = 4
LAST_PARTS = 2
PART_UNROLL = 16
PIECES = 2


def chosen_products(packed, classes, panels, todo, shape, layers, spare, first_left=0):
    step_count, columns, slots = shape
    count = jnp.int32(0)
    for panel in range(panels):
        kind = classes[panel]
        for extra in range(-(-step_count // columns)):
            step = lax.rem(kind + step_count // 2, columns) + extra * columns
            groups = jnp.where((kind >= 0) & (step < step_count), slots // 8, 0)
            for layer in range(layers):
                base = (layer * step_count + step) * slots

                def keep(group, count):
                    for lane in range(8):
                        entry = packed[base + group * 8 + lane]
                        todo[count] = entry + (panel * layers * slots << 10)
                        count += (entry >= 0).astype(jnp.int32)
                    return count

                count = lax.fori_loop(0, groups, keep, count)
    for extra in range(UNROLL - 1):
        todo[count + extra] = jnp.int32(first_left << 10 | spare)
    return count


def add_chosen(todo, count, left, right, work, first_left=0, start=0, unroll=UNROLL):
    def several(group, carry):
        entries = [todo[start + group * unroll + lane] for lane in range(unroll)]
        products = [
            jnp.dot(
                left[((entry >> 10) & 1023) - first_left],
                right[entry >> 20],
                preferred_element_type=jnp.float32,
            )
            for entry in entries
        ]
        for entry, product in zip(entries, products):
            work[entry & 1023] += product
        return carry

    lax.fori_loop(0, (count + unroll - 1) // unroll, several, jnp.int32(0))


def sort_products(packed, base, kind, shape, sorted_out, spare, first_left):
    step_count, columns, slots = shape
    room, counts, size = part_room(shape), LAST_PARTS * part_room(shape), spare // LAST_PARTS
    for part in range(LAST_PARTS):
        sorted_out[counts + part] = jnp.int32(0)
    for extra in range(-(-step_count // columns)):
        step = lax.rem(kind + step_count // 2, columns) + extra * columns
        groups = jnp.where((kind >= 0) & (step < step_count), slots // 8, 0)
        first = base + step * slots

        def place(group, carry):
            for lane in range(8):
                entry = packed[first + group * 8 + lane]
                result, part = entry & 1023, jnp.int32(0)
                for bound in range(1, LAST_PARTS):
                    part += (result >= bound * size).astype(jnp.int32)
                count = sorted_out[counts + part]
                sorted_out[part * room + count] = entry
                sorted_out[counts + part] = count + (entry >= 0).astype(jnp.int32)
            return carry

        lax.fori_loop(0, groups, place, jnp.int32(0))
    for part in range(LAST_PARTS):
        count = sorted_out[counts + part]
        for extra in range(PART_UNROLL - 1):
            sorted_out[part * room + count + extra] = jnp.int32(first_left << 10 | spare)


def part_room(shape):
    step_count, columns, slots = shape
    return -(-step_count // columns) * slots + PART_UNROLL


def sum_kernel(panels, rights, givens, saved, mode, shape, layers, operand_count, layer_at, *refs):
    packed, classes, refs = refs[0], refs[1], refs[2:]
    operands, refs = refs[:operand_count], refs[operand_count:]
    out_count = max(len(saved), 1)
    outs, refs = refs[:out_count], refs[out_count:]
    if mode == "split":
        (right, kept), (work, left, todo, sems) = refs[:2], refs[2:]
    else:
        work, left, right, todo, sems = refs
    spare = work.shape[0] - 1
    other = 1 - classes[layer_at]
    copies = []

    def plan(source, target, when=None):
        copies.append((pltpu.make_async_copy(source, target, sems.at[len(copies)]), when))

    start = 0
    for operand, size, gathered in rights:
        source = operands[operand]
        if gathered:
            source = source.at[pl.ds(other * size, size)]
        plan(source, right.at[pl.ds(start, size)])
        start += size
    start = 0
    for panel, pieces in enumerate(panels):
        for operand, size, gathered in pieces:
            source = operands[operand]
            if gathered:
                source = source.at[pl.ds(other * size, size)]
            plan(source, left.at[pl.ds(start, size)], classes[panel] >= 0)
            start += size
    start = 0
    for operand, size in givens:
        plan(operands[operand], work.at[pl.ds(start, size)])
        start += size
    for copy, when in copies:
        copy.start() if when is None else pl.when(when)(copy.start)
    if givens:
        work[spare] = jnp.zeros_like(work[spare])
    else:
        work[...] = jnp.zeros_like(work)
    kinds = [classes[panel] for panel in range(len(panels))]
    count = chosen_products(packed, kinds, len(panels), todo, shape, layers, spare)
    for copy, when in copies:
        copy.wait() if when is None else pl.when(when)(copy.wait)
    add_chosen(todo, count, left, right, work)
    if not saved:
        outs[0][...] = work[:spare].astype(outs[0].dtype)
        return
    start, copies, targets = 0, [], list(outs)
    if mode == "split":
        kept[kept.shape[0] - 1] = jnp.zeros(kept.shape[1:], kept.dtype)
        targets.insert(0, kept.at[pl.ds(0, kept.shape[0] - 1)])
    for out in targets:
        size = out.shape[0]
        copies.append(pltpu.make_async_copy(work.at[pl.ds(start, size)], out, sems.at[len(copies)]))
        start += size
    for copy in copies:
        copy.start()
    for copy in copies:
        copy.wait()


def product_sums(packed, scalars, shape, layers, panels, rights, givens, result_slots, saved, mode="whole"):
    step_count, columns, slots = shape
    rows, width = rights[0][0].shape[1:]
    operands = []

    def number(value):
        for index, known in enumerate(operands):
            if known is value:
                return index
        operands.append(value)
        return len(operands) - 1

    def spans(pieces):
        return [
            (number(value), value.shape[0] // 2 if gathered else value.shape[0], gathered)
            for value, gathered in pieces
        ]

    right_spans = spans(rights)
    panel_spans = [spans(pieces) for pieces in panels]
    given_spans = [(number(value), value.shape[0]) for value in givens]
    right_slots = sum(size for _, size, _ in right_spans)
    left_slots = len(panels) * layers * slots
    assert right_slots <= 1024 and left_slots <= 1024 and result_slots < 1024 and slots % 8 == 0
    assert all(sum(size for _, size, _ in pieces) == layers * slots for pieces in panel_spans)
    anywhere = pl.BlockSpec(memory_space=pl.ANY)
    in_scalar, in_vector = pl.BlockSpec(memory_space=pltpu.SMEM), pl.BlockSpec(memory_space=pltpu.VMEM)
    copy_count = len(rights) + sum(len(pieces) for pieces in panels) + len(givens) + len(saved) + 1
    scratch = [
        pltpu.VMEM((result_slots + 1, rows, width), jnp.float32),
        pltpu.VMEM((left_slots, rows, width), jnp.bfloat16),
        pltpu.VMEM((right_slots, width, width), jnp.bfloat16),
    ]
    if saved:
        out_shape = [jax.ShapeDtypeStruct((size, rows, width), jnp.float32) for size in saved]
    else:
        out_shape = [jax.ShapeDtypeStruct((result_slots, rows, width), jnp.bfloat16)]
    out_specs = [anywhere if saved else in_vector] * len(out_shape)
    if mode == "split":
        out_shape += [scratch.pop(), pltpu.VMEM((result_slots - sum(saved) + 1, rows, width), jnp.float32)]
        out_specs += [in_vector] * 2
    return pl.pallas_call(
        functools.partial(
            sum_kernel,
            panel_spans,
            right_spans,
            given_spans,
            saved,
            mode,
            shape,
            layers,
            len(operands),
            len(panels),
        ),
        out_shape=out_shape,
        in_specs=[in_scalar, in_scalar] + [anywhere] * len(operands),
        out_specs=out_specs,
        scratch_shapes=scratch
        + [
            pltpu.SMEM((len(panels) * -(-step_count // columns) * layers * slots + UNROLL,), jnp.int32),
            pltpu.SemaphoreType.DMA((copy_count,)),
        ],
        compiler_params=pltpu.CompilerParams(vmem_limit_bytes=(34 if mode == "split" else 56) << 20),
        cost_estimate=pl.CostEstimate(flops=1, bytes_accessed=1, transcendentals=0),
    )(packed, scalars, *operands)


def received_kernel(given, *refs):
    del given
    work, start = refs[-1], 0
    for piece in refs[:-1]:
        span = pl.ds(start, piece.shape[0])
        work[span] += piece[...]
        start += piece.shape[0]


def add_received(given, pieces):
    in_vector = pl.BlockSpec(memory_space=pltpu.VMEM)
    return pl.pallas_call(
        received_kernel,
        out_shape=pltpu.VMEM(given.shape, given.dtype),
        in_specs=[in_vector] * (1 + len(pieces)),
        out_specs=in_vector,
        input_output_aliases={0: 0},
        compiler_params=pltpu.CompilerParams(vmem_limit_bytes=12 << 20),
        cost_estimate=pl.CostEstimate(flops=1, bytes_accessed=1, transcendentals=0),
    )(given, *pieces)


def own_kernel(shape, kind_at, packed, scalars, right, given, left, work, sorted_out, todo):
    del given
    step_count, _, slots = shape
    spare, kind = work.shape[0] - 1, scalars[kind_at]
    count = chosen_products(packed, [kind], 1, todo, shape, 1, spare)
    add_chosen(todo, count, left, right, work)
    sort_products(packed, step_count * slots, kind, shape, sorted_out, spare, slots)


def add_own(packed, scalars, kind_at, shape, panel, right, given):
    step_count, columns, slots = shape
    in_scalar, in_vector = pl.BlockSpec(memory_space=pltpu.SMEM), pl.BlockSpec(memory_space=pltpu.VMEM)
    return pl.pallas_call(
        functools.partial(own_kernel, shape, kind_at),
        out_shape=[
            pltpu.VMEM(given.shape, given.dtype),
            jax.ShapeDtypeStruct((LAST_PARTS * part_room(shape) + LAST_PARTS,), jnp.int32),
        ],
        in_specs=[in_scalar] * 2 + [in_vector] * 3,
        out_specs=[in_vector, in_scalar],
        scratch_shapes=[pltpu.SMEM((-(-step_count // columns) * slots + UNROLL,), jnp.int32)],
        input_output_aliases={3: 0},
        compiler_params=pltpu.CompilerParams(vmem_limit_bytes=12 << 20),
        cost_estimate=pl.CostEstimate(flops=1, bytes_accessed=1, transcendentals=0),
    )(packed, scalars, right, given, panel)


def other_kernel(shape, sorted_lists, right, given, left, out, work, rounded, sems):
    del given
    slots, room, spare = shape[2], part_room(shape), work.shape[0] - 1
    size, copies = spare // LAST_PARTS, []
    for part in range(LAST_PARTS):
        count = sorted_lists[LAST_PARTS * room + part]
        add_chosen(sorted_lists, count, left, right, work, slots, part * room, PART_UNROLL)
        last = (part + 1) * size if part < LAST_PARTS - 1 else spare
        cuts = [part * size + (last - part * size) * piece // PIECES for piece in range(PIECES + 1)]
        for first, after in zip(cuts, cuts[1:]):
            span = pl.ds(first, after - first)
            rounded[span] = work[span].astype(rounded.dtype)
            copies.append(pltpu.make_async_copy(rounded.at[span], out.at[span], sems.at[len(copies)]))
            copies[-1].start()
    for copy in copies:
        copy.wait()


def add_other(sorted_lists, shape, panel, right, given):
    result_slots, rows, width = given.shape[0] - 1, *given.shape[1:]
    in_scalar, in_vector = pl.BlockSpec(memory_space=pltpu.SMEM), pl.BlockSpec(memory_space=pltpu.VMEM)
    return pl.pallas_call(
        functools.partial(other_kernel, shape),
        out_shape=[
            jax.ShapeDtypeStruct((result_slots, rows, width), jnp.bfloat16),
            pltpu.VMEM(given.shape, given.dtype),
        ],
        in_specs=[in_scalar] + [in_vector] * 3,
        out_specs=[pl.BlockSpec(memory_space=pl.ANY), in_vector],
        scratch_shapes=[
            pltpu.VMEM((result_slots, rows, width), jnp.bfloat16),
            pltpu.SemaphoreType.DMA((LAST_PARTS * PIECES,)),
        ],
        input_output_aliases={2: 1},
        compiler_params=pltpu.CompilerParams(vmem_limit_bytes=12 << 20),
        cost_estimate=pl.CostEstimate(flops=1, bytes_accessed=1, transcendentals=0),
    )(sorted_lists, right, given, panel)[0]


def scalar_list(*values):
    return jnp.stack([jnp.asarray(value, jnp.int32) for value in values])


def swapped(value):
    return lax.ppermute(value, "dep", [(0, 1), (1, 0)])


def paired(value):
    return lax.all_gather(value, "dep", axis=0, tiled=True)


def kept_products(both, layer, half, right_slot):
    slots = both.shape[3]
    result = both[:, :, 2] - layer * half
    wanted = (result >= 0) & (result < half)
    layers = jnp.arange(2, dtype=jnp.int32)[:, None, None]
    packed = right_slot(both[:, :, 1], layers) << 20 | (layers * slots + both[:, :, 0]) << 10 | result
    return jnp.where(wanted, packed, -1).reshape(-1)


def layer_products(step_lists, layer, half, right_slot):
    result = step_lists[:, 2]
    turned = jnp.where(result < half, result + layer * half, result - layer * half)
    packed = right_slot(step_lists[:, 1], 0) << 20 | step_lists[:, 0] << 10 | turned
    return jnp.where(result < 2 * half, packed, -1).reshape(-1)


def ring(left_blocks, right_blocks, triples, half):
    own, right_own, step_lists = left_blocks[0, 0, 0], right_blocks[0, 0, 0], triples[0, 0, 0]
    columns, layer = lax.axis_size("col"), lax.axis_index("dep")
    gathered = lax.all_gather(right_own, "row", axis=0, tiled=True)
    right_slots = gathered.shape[0]
    both = jnp.stack([step_lists, swapped(step_lists)])
    packed = kept_products(both, layer, half, lambda slot, layers: layers * right_slots + slot)
    rights = [(gathered, False), (swapped(gathered), False)]
    shape = (step_lists.shape[0], columns, own.shape[0])
    rising, falling, total = own, own, []
    panels, classes = [[(own, False), (paired(own), True)]], [0]
    reach = step_lists.shape[0] // 2
    for distance in range(1, reach + 1):
        rising = lax.ppermute(rising, "col", [(i, (i + 1) % columns) for i in range(columns)])
        falling = lax.ppermute(falling, "col", [(i, (i - 1) % columns) for i in range(columns)])
        panels += [[(value, False), (paired(value), True)] for value in (rising, falling)]
        classes += [columns - distance, distance]
        saved = [] if distance == reach else [half]
        scalars = scalar_list(*classes, layer)
        total = product_sums(packed, scalars, shape, 2, panels, rights, total, half, saved)
        panels, classes = [], []
    return total[0][None, None, None]


def line(left_blocks, right_blocks, triples, half):
    own, right_own, step_lists = left_blocks[0, 0, 0], right_blocks[0, 0, 0], triples[0, 0, 0]
    slots, part = own.shape[0], right_own.shape[0]
    columns, layer, place = lax.axis_size("col"), lax.axis_index("dep"), lax.axis_index("col")
    shape = (step_lists.shape[0], columns, slots)
    inner = (place == 1) | (place == 2)
    low = place < 2
    outward, across, beside = [(2, 3), (1, 0)], [(1, 2), (2, 1)], [(0, 1), (1, 0), (2, 3), (3, 2)]
    fence = lax.optimization_barrier

    def hop(value, pairs):
        return lax.ppermute(value, "col", pairs)

    def right_slot(slot, layers):
        return (layers * 2 + ((slot // part) ^ lax.axis_index("row"))) * part + slot % part

    beside_one, across_one, across_two = hop(own, beside), hop(own, across), hop(own, [(0, 2), (3, 1)])
    met = lax.ppermute(right_own, "row", [(0, 1), (1, 0)])
    listed = layer_products(step_lists, layer, half, right_slot)
    classes = [0, jnp.where(place % 2 == 0, 1, 3), jnp.where(inner, jnp.where(low, 1, 3), -1)]
    classes += [jnp.where(inner, 2, -1), jnp.where(inner, -1, 2)]
    scalars = scalar_list(*classes, layer, jnp.where(inner, -1, jnp.where(low, 3, 1)))

    outer_two = hop(across_one, outward)
    beside_one, across_one, met, listed, scalars = fence((beside_one, across_one, met, listed, scalars))
    right_other, met_other = swapped(right_own), swapped(met)
    both = jnp.stack([step_lists, swapped(step_lists)])
    kept = kept_products(both, layer, half, right_slot)

    across_two, right_other, met_other, kept = fence((across_two, right_other, met_other, kept))
    outer_three = hop(across_two, outward)
    panels = [[(value, False)] for value in (own, beside_one, across_one, across_two, outer_two)]
    rights = [(value, False) for value in (right_own, met, right_other, met_other)]
    saved = [half // PARTS] * (PARTS - 1) + [half - half // PARTS * (PARTS - 1)]
    *parts, right, total = product_sums(
        listed, scalars, shape, 1, panels, rights, [], 2 * half, saved, "split"
    )
    total = add_received(total, [swapped(part) for part in parts])

    outer_three, total, right = fence((outer_three, total, right))
    kind_at = len(classes) + 1
    total, sorted_lists = add_own(kept, scalars, kind_at, shape, outer_three, right, total)
    block = add_other(sorted_lists, shape, swapped(outer_three), right, total)
    return block[None, None, None]


def local(left_blocks, right_blocks, triples):
    step_count = triples.shape[3]
    row_count, columns = lax.axis_size("row"), lax.axis_size("col")
    half = (2 * step_count - 2 + row_count) // row_count * NBQ // 2
    if columns >= step_count:
        return ring(left_blocks, right_blocks, triples, half)
    assert columns == 4 and row_count == 2
    return line(left_blocks, right_blocks, triples, half)


def solution(mesh):
    return jax.shard_map(
        local,
        mesh=mesh,
        in_specs=(
            P(("grp", "row"), "col", "dep", None, None, None),
            P(("grp", "row"), "col", "dep", None, None, None),
            P(("grp", "row"), "col", "dep", None, None, None),
        ),
        out_specs=P(("grp", "row"), "col", "dep", None, None, None),
        check_vma=False,
    )
```

```python
import functools

import jax
import jax.numpy as jnp
from jax import lax
from jax.experimental import pallas as pl
from jax.experimental.pallas import tpu as pltpu
from jax.sharding import PartitionSpec as P

NBQ = 32
UNROLL = 16
PARTS = 4
LAST_PARTS = 2
PART_UNROLL = 32
PIECES = 4


def chosen_products(packed, classes, panels, todo, shape, layers, spare, first_left=0):
    step_count, columns, slots = shape
    count = jnp.int32(0)
    for panel in range(panels):
        kind = classes[panel]
        for extra in range(-(-step_count // columns)):
            step = lax.rem(kind + step_count // 2, columns) + extra * columns
            groups = jnp.where((kind >= 0) & (step < step_count), slots // 8, 0)
            for layer in range(layers):
                base = (layer * step_count + step) * slots

                def keep(group, count):
                    for lane in range(8):
                        entry = packed[base + group * 8 + lane]
                        todo[count] = entry + (panel * layers * slots << 10)
                        count += (entry >= 0).astype(jnp.int32)
                    return count

                count = lax.fori_loop(0, groups, keep, count)
    for extra in range(UNROLL - 1):
        todo[count + extra] = jnp.int32(first_left << 10 | spare)
    return count


def add_chosen(todo, count, left, right, work, first_left=0, start=0, unroll=UNROLL):
    def several(group, carry):
        entries = [todo[start + group * unroll + lane] for lane in range(unroll)]
        products = [
            jnp.dot(
                left[((entry >> 10) & 1023) - first_left],
                right[entry >> 20],
                preferred_element_type=jnp.float32,
            )
            for entry in entries
        ]
        for entry, product in zip(entries, products):
            work[entry & 1023] += product
        return carry

    lax.fori_loop(0, (count + unroll - 1) // unroll, several, jnp.int32(0))


def sort_products(packed, base, kind, shape, sorted_out, spare, first_left):
    step_count, columns, slots = shape
    room, counts, size = part_room(shape), LAST_PARTS * part_room(shape), spare // LAST_PARTS
    for part in range(LAST_PARTS):
        sorted_out[counts + part] = jnp.int32(0)
    for extra in range(-(-step_count // columns)):
        step = lax.rem(kind + step_count // 2, columns) + extra * columns
        groups = jnp.where((kind >= 0) & (step < step_count), slots // 8, 0)
        first = base + step * slots

        def place(group, carry):
            for lane in range(8):
                entry = packed[first + group * 8 + lane]
                result, part = entry & 1023, jnp.int32(0)
                for bound in range(1, LAST_PARTS):
                    part += (result >= bound * size).astype(jnp.int32)
                count = sorted_out[counts + part]
                sorted_out[part * room + count] = entry
                sorted_out[counts + part] = count + (entry >= 0).astype(jnp.int32)
            return carry

        lax.fori_loop(0, groups, place, jnp.int32(0))
    for part in range(LAST_PARTS):
        count = sorted_out[counts + part]
        for extra in range(PART_UNROLL - 1):
            sorted_out[part * room + count + extra] = jnp.int32(first_left << 10 | spare)


def part_room(shape):
    step_count, columns, slots = shape
    return -(-step_count // columns) * slots + PART_UNROLL


def sum_kernel(panels, rights, givens, saved, mode, shape, layers, operand_count, layer_at, *refs):
    packed, classes, refs = refs[0], refs[1], refs[2:]
    operands, refs = refs[:operand_count], refs[operand_count:]
    out_count = max(len(saved), 1)
    outs, refs = refs[:out_count], refs[out_count:]
    if mode == "split":
        (right, kept), (work, left, todo, sems) = refs[:2], refs[2:]
    else:
        work, left, right, todo, sems = refs
    spare = work.shape[0] - 1
    other = 1 - classes[layer_at]
    copies = []

    def plan(source, target, when=None):
        copies.append((pltpu.make_async_copy(source, target, sems.at[len(copies)]), when))

    start = 0
    for operand, size, gathered in rights:
        source = operands[operand]
        if gathered:
            source = source.at[pl.ds(other * size, size)]
        plan(source, right.at[pl.ds(start, size)])
        start += size
    start = 0
    for panel, pieces in enumerate(panels):
        for operand, size, gathered in pieces:
            source = operands[operand]
            if gathered:
                source = source.at[pl.ds(other * size, size)]
            plan(source, left.at[pl.ds(start, size)], classes[panel] >= 0)
            start += size
    start = 0
    for operand, size in givens:
        plan(operands[operand], work.at[pl.ds(start, size)])
        start += size
    for copy, when in copies:
        copy.start() if when is None else pl.when(when)(copy.start)
    if givens:
        work[spare] = jnp.zeros_like(work[spare])
    else:
        work[...] = jnp.zeros_like(work)
    kinds = [classes[panel] for panel in range(len(panels))]
    count = chosen_products(packed, kinds, len(panels), todo, shape, layers, spare)
    for copy, when in copies:
        copy.wait() if when is None else pl.when(when)(copy.wait)
    add_chosen(todo, count, left, right, work)
    if not saved:
        outs[0][...] = work[:spare].astype(outs[0].dtype)
        return
    start, copies, targets = 0, [], list(outs)
    if mode == "split":
        kept[kept.shape[0] - 1] = jnp.zeros(kept.shape[1:], kept.dtype)
        targets.insert(0, kept.at[pl.ds(0, kept.shape[0] - 1)])
    for out in targets:
        size = out.shape[0]
        copies.append(pltpu.make_async_copy(work.at[pl.ds(start, size)], out, sems.at[len(copies)]))
        start += size
    for copy in copies:
        copy.start()
    for copy in copies:
        copy.wait()


def product_sums(packed, scalars, shape, layers, panels, rights, givens, result_slots, saved, mode="whole"):
    step_count, columns, slots = shape
    rows, width = rights[0][0].shape[1:]
    operands = []

    def number(value):
        for index, known in enumerate(operands):
            if known is value:
                return index
        operands.append(value)
        return len(operands) - 1

    def spans(pieces):
        return [
            (number(value), value.shape[0] // 2 if gathered else value.shape[0], gathered)
            for value, gathered in pieces
        ]

    right_spans = spans(rights)
    panel_spans = [spans(pieces) for pieces in panels]
    given_spans = [(number(value), value.shape[0]) for value in givens]
    right_slots = sum(size for _, size, _ in right_spans)
    left_slots = len(panels) * layers * slots
    assert right_slots <= 1024 and left_slots <= 1024 and result_slots < 1024 and slots % 8 == 0
    assert all(sum(size for _, size, _ in pieces) == layers * slots for pieces in panel_spans)
    anywhere = pl.BlockSpec(memory_space=pl.ANY)
    in_scalar, in_vector = pl.BlockSpec(memory_space=pltpu.SMEM), pl.BlockSpec(memory_space=pltpu.VMEM)
    copy_count = len(rights) + sum(len(pieces) for pieces in panels) + len(givens) + len(saved) + 1
    scratch = [
        pltpu.VMEM((result_slots + 1, rows, width), jnp.float32),
        pltpu.VMEM((left_slots, rows, width), jnp.bfloat16),
        pltpu.VMEM((right_slots, width, width), jnp.bfloat16),
    ]
    if saved:
        out_shape = [jax.ShapeDtypeStruct((size, rows, width), jnp.float32) for size in saved]
    else:
        out_shape = [jax.ShapeDtypeStruct((result_slots, rows, width), jnp.bfloat16)]
    out_specs = [anywhere if saved else in_vector] * len(out_shape)
    if mode == "split":
        out_shape += [scratch.pop(), pltpu.VMEM((result_slots - sum(saved) + 1, rows, width), jnp.float32)]
        out_specs += [in_vector] * 2
    return pl.pallas_call(
        functools.partial(
            sum_kernel,
            panel_spans,
            right_spans,
            given_spans,
            saved,
            mode,
            shape,
            layers,
            len(operands),
            len(panels),
        ),
        out_shape=out_shape,
        in_specs=[in_scalar, in_scalar] + [anywhere] * len(operands),
        out_specs=out_specs,
        scratch_shapes=scratch
        + [
            pltpu.SMEM((len(panels) * -(-step_count // columns) * layers * slots + UNROLL,), jnp.int32),
            pltpu.SemaphoreType.DMA((copy_count,)),
        ],
        compiler_params=pltpu.CompilerParams(vmem_limit_bytes=(34 if mode == "split" else 56) << 20),
        cost_estimate=pl.CostEstimate(flops=1, bytes_accessed=1, transcendentals=0),
    )(packed, scalars, *operands)


def received_kernel(given, *refs):
    del given
    work, start = refs[-1], 0
    for piece in refs[:-1]:
        span = pl.ds(start, piece.shape[0])
        work[span] += piece[...]
        start += piece.shape[0]


def add_received(given, pieces):
    in_vector = pl.BlockSpec(memory_space=pltpu.VMEM)
    return pl.pallas_call(
        received_kernel,
        out_shape=pltpu.VMEM(given.shape, given.dtype),
        in_specs=[in_vector] * (1 + len(pieces)),
        out_specs=in_vector,
        input_output_aliases={0: 0},
        compiler_params=pltpu.CompilerParams(vmem_limit_bytes=12 << 20),
        cost_estimate=pl.CostEstimate(flops=1, bytes_accessed=1, transcendentals=0),
    )(given, *pieces)


def own_kernel(shape, kind_at, packed, scalars, right, given, left, work, sorted_out, todo):
    del given
    step_count, _, slots = shape
    spare, kind = work.shape[0] - 1, scalars[kind_at]
    count = chosen_products(packed, [kind], 1, todo, shape, 1, spare)
    add_chosen(todo, count, left, right, work)
    sort_products(packed, step_count * slots, kind, shape, sorted_out, spare, slots)


def add_own(packed, scalars, kind_at, shape, panel, right, given):
    step_count, columns, slots = shape
    in_scalar, in_vector = pl.BlockSpec(memory_space=pltpu.SMEM), pl.BlockSpec(memory_space=pltpu.VMEM)
    return pl.pallas_call(
        functools.partial(own_kernel, shape, kind_at),
        out_shape=[
            pltpu.VMEM(given.shape, given.dtype),
            jax.ShapeDtypeStruct((LAST_PARTS * part_room(shape) + LAST_PARTS,), jnp.int32),
        ],
        in_specs=[in_scalar] * 2 + [in_vector] * 3,
        out_specs=[in_vector, in_scalar],
        scratch_shapes=[pltpu.SMEM((-(-step_count // columns) * slots + UNROLL,), jnp.int32)],
        input_output_aliases={3: 0},
        compiler_params=pltpu.CompilerParams(vmem_limit_bytes=12 << 20),
        cost_estimate=pl.CostEstimate(flops=1, bytes_accessed=1, transcendentals=0),
    )(packed, scalars, right, given, panel)


def other_kernel(shape, sorted_lists, right, given, left, out, work, rounded, sems):
    del given
    slots, room, spare = shape[2], part_room(shape), work.shape[0] - 1
    size, copies = spare // LAST_PARTS, []
    for part in range(LAST_PARTS):
        count = sorted_lists[LAST_PARTS * room + part]
        add_chosen(sorted_lists, count, left, right, work, slots, part * room, PART_UNROLL)
        last = (part + 1) * size if part < LAST_PARTS - 1 else spare
        cuts = [part * size + (last - part * size) * piece // PIECES for piece in range(PIECES + 1)]
        for first, after in zip(cuts, cuts[1:]):
            span = pl.ds(first, after - first)
            rounded[span] = work[span].astype(rounded.dtype)
            copies.append(pltpu.make_async_copy(rounded.at[span], out.at[span], sems.at[len(copies)]))
            copies[-1].start()
    for copy in copies:
        copy.wait()


def add_other(sorted_lists, shape, panel, right, given):
    result_slots, rows, width = given.shape[0] - 1, *given.shape[1:]
    in_scalar, in_vector = pl.BlockSpec(memory_space=pltpu.SMEM), pl.BlockSpec(memory_space=pltpu.VMEM)
    return pl.pallas_call(
        functools.partial(other_kernel, shape),
        out_shape=[
            jax.ShapeDtypeStruct((result_slots, rows, width), jnp.bfloat16),
            pltpu.VMEM(given.shape, given.dtype),
        ],
        in_specs=[in_scalar] + [in_vector] * 3,
        out_specs=[pl.BlockSpec(memory_space=pl.ANY), in_vector],
        scratch_shapes=[
            pltpu.VMEM((result_slots, rows, width), jnp.bfloat16),
            pltpu.SemaphoreType.DMA((LAST_PARTS * PIECES,)),
        ],
        input_output_aliases={2: 1},
        compiler_params=pltpu.CompilerParams(vmem_limit_bytes=12 << 20),
        cost_estimate=pl.CostEstimate(flops=1, bytes_accessed=1, transcendentals=0),
    )(sorted_lists, right, given, panel)[0]


def scalar_list(*values):
    return jnp.stack([jnp.asarray(value, jnp.int32) for value in values])


def swapped(value):
    return lax.ppermute(value, "dep", [(0, 1), (1, 0)])


def paired(value):
    return lax.all_gather(value, "dep", axis=0, tiled=True)


def kept_products(both, layer, half, right_slot):
    slots = both.shape[3]
    result = both[:, :, 2] - layer * half
    wanted = (result >= 0) & (result < half)
    layers = jnp.arange(2, dtype=jnp.int32)[:, None, None]
    packed = right_slot(both[:, :, 1], layers) << 20 | (layers * slots + both[:, :, 0]) << 10 | result
    return jnp.where(wanted, packed, -1).reshape(-1)


def layer_products(step_lists, layer, half, right_slot):
    result = step_lists[:, 2]
    turned = jnp.where(result < half, result + layer * half, result - layer * half)
    packed = right_slot(step_lists[:, 1], 0) << 20 | step_lists[:, 0] << 10 | turned
    return jnp.where(result < 2 * half, packed, -1).reshape(-1)


def ring(left_blocks, right_blocks, triples, half):
    own, right_own, step_lists = left_blocks[0, 0, 0], right_blocks[0, 0, 0], triples[0, 0, 0]
    columns, layer = lax.axis_size("col"), lax.axis_index("dep")
    gathered = lax.all_gather(right_own, "row", axis=0, tiled=True)
    right_slots = gathered.shape[0]
    both = jnp.stack([step_lists, swapped(step_lists)])
    packed = kept_products(both, layer, half, lambda slot, layers: layers * right_slots + slot)
    rights = [(gathered, False), (swapped(gathered), False)]
    shape = (step_lists.shape[0], columns, own.shape[0])
    rising, falling, total = own, own, []
    panels, classes = [[(own, False), (paired(own), True)]], [0]
    reach = step_lists.shape[0] // 2
    for distance in range(1, reach + 1):
        rising = lax.ppermute(rising, "col", [(i, (i + 1) % columns) for i in range(columns)])
        falling = lax.ppermute(falling, "col", [(i, (i - 1) % columns) for i in range(columns)])
        panels += [[(value, False), (paired(value), True)] for value in (rising, falling)]
        classes += [columns - distance, distance]
        saved = [] if distance == reach else [half]
        scalars = scalar_list(*classes, layer)
        total = product_sums(packed, scalars, shape, 2, panels, rights, total, half, saved)
        panels, classes = [], []
    return total[0][None, None, None]


def line(left_blocks, right_blocks, triples, half):
    own, right_own, step_lists = left_blocks[0, 0, 0], right_blocks[0, 0, 0], triples[0, 0, 0]
    slots, part = own.shape[0], right_own.shape[0]
    columns, layer, place = lax.axis_size("col"), lax.axis_index("dep"), lax.axis_index("col")
    shape = (step_lists.shape[0], columns, slots)
    inner = (place == 1) | (place == 2)
    low = place < 2
    outward, across, beside = [(2, 3), (1, 0)], [(1, 2), (2, 1)], [(0, 1), (1, 0), (2, 3), (3, 2)]
    fence = lax.optimization_barrier

    def hop(value, pairs):
        return lax.ppermute(value, "col", pairs)

    def right_slot(slot, layers):
        return (layers * 2 + ((slot // part) ^ lax.axis_index("row"))) * part + slot % part

    beside_one, across_one, across_two = hop(own, beside), hop(own, across), hop(own, [(0, 2), (3, 1)])
    met = lax.ppermute(right_own, "row", [(0, 1), (1, 0)])
    listed = layer_products(step_lists, layer, half, right_slot)
    classes = [0, jnp.where(place % 2 == 0, 1, 3), jnp.where(inner, jnp.where(low, 1, 3), -1)]
    classes += [jnp.where(inner, 2, -1), jnp.where(inner, -1, 2)]
    scalars = scalar_list(*classes, layer, jnp.where(inner, -1, jnp.where(low, 3, 1)))

    outer_two = hop(across_one, outward)
    beside_one, across_one, met, listed, scalars = fence((beside_one, across_one, met, listed, scalars))
    right_other, met_other = swapped(right_own), swapped(met)
    both = jnp.stack([step_lists, swapped(step_lists)])
    kept = kept_products(both, layer, half, right_slot)

    across_two, right_other, met_other, kept = fence((across_two, right_other, met_other, kept))
    outer_three = hop(across_two, outward)
    panels = [[(value, False)] for value in (own, beside_one, across_one, across_two, outer_two)]
    rights = [(value, False) for value in (right_own, met, right_other, met_other)]
    saved = [half // PARTS] * (PARTS - 1) + [half - half // PARTS * (PARTS - 1)]
    *parts, right, total = product_sums(
        listed, scalars, shape, 1, panels, rights, [], 2 * half, saved, "split"
    )
    total = add_received(total, [swapped(part) for part in parts])

    outer_three, total, right = fence((outer_three, total, right))
    kind_at = len(classes) + 1
    total, sorted_lists = add_own(kept, scalars, kind_at, shape, outer_three, right, total)
    block = add_other(sorted_lists, shape, swapped(outer_three), right, total)
    return block[None, None, None]


def local(left_blocks, right_blocks, triples):
    step_count = triples.shape[3]
    row_count, columns = lax.axis_size("row"), lax.axis_size("col")
    half = (2 * step_count - 2 + row_count) // row_count * NBQ // 2
    if columns >= step_count:
        return ring(left_blocks, right_blocks, triples, half)
    assert columns == 4 and row_count == 2
    return line(left_blocks, right_blocks, triples, half)


def solution(mesh):
    return jax.shard_map(
        local,
        mesh=mesh,
        in_specs=(
            P(("grp", "row"), "col", "dep", None, None, None),
            P(("grp", "row"), "col", "dep", None, None, None),
            P(("grp", "row"), "col", "dep", None, None, None),
        ),
        out_specs=P(("grp", "row"), "col", "dep", None, None, None),
        check_vma=False,
    )
```

```python
import functools

import jax
import jax.numpy as jnp
from jax import lax
from jax.experimental import pallas as pl
from jax.experimental.pallas import tpu as pltpu
from jax.sharding import PartitionSpec as P

NBQ = 32
UNROLL = 16
PARTS = 4
LAST_PARTS = 4
PART_UNROLL = 16
PIECES = 1


def chosen_products(packed, classes, panels, todo, shape, layers, spare, first_left=0):
    step_count, columns, slots = shape
    count = jnp.int32(0)
    for panel in range(panels):
        kind = classes[panel]
        for extra in range(-(-step_count // columns)):
            step = lax.rem(kind + step_count // 2, columns) + extra * columns
            groups = jnp.where((kind >= 0) & (step < step_count), slots // 8, 0)
            for layer in range(layers):
                base = (layer * step_count + step) * slots

                def keep(group, count):
                    for lane in range(8):
                        entry = packed[base + group * 8 + lane]
                        todo[count] = entry + (panel * layers * slots << 10)
                        count += (entry >= 0).astype(jnp.int32)
                    return count

                count = lax.fori_loop(0, groups, keep, count)
    for extra in range(UNROLL - 1):
        todo[count + extra] = jnp.int32(first_left << 10 | spare)
    return count


def add_chosen(todo, count, left, right, work, first_left=0, start=0, unroll=UNROLL):
    def several(group, carry):
        entries = [todo[start + group * unroll + lane] for lane in range(unroll)]
        products = [
            jnp.dot(
                left[((entry >> 10) & 1023) - first_left],
                right[entry >> 20],
                preferred_element_type=jnp.float32,
            )
            for entry in entries
        ]
        for entry, product in zip(entries, products):
            work[entry & 1023] += product
        return carry

    lax.fori_loop(0, (count + unroll - 1) // unroll, several, jnp.int32(0))


def sort_products(packed, base, kind, shape, sorted_out, spare, first_left):
    step_count, columns, slots = shape
    room, counts, size = part_room(shape), LAST_PARTS * part_room(shape), spare // LAST_PARTS
    for part in range(LAST_PARTS):
        sorted_out[counts + part] = jnp.int32(0)
    for extra in range(-(-step_count // columns)):
        step = lax.rem(kind + step_count // 2, columns) + extra * columns
        groups = jnp.where((kind >= 0) & (step < step_count), slots // 8, 0)
        first = base + step * slots

        def place(group, carry):
            for lane in range(8):
                entry = packed[first + group * 8 + lane]
                result, part = entry & 1023, jnp.int32(0)
                for bound in range(1, LAST_PARTS):
                    part += (result >= bound * size).astype(jnp.int32)
                count = sorted_out[counts + part]
                sorted_out[part * room + count] = entry
                sorted_out[counts + part] = count + (entry >= 0).astype(jnp.int32)
            return carry

        lax.fori_loop(0, groups, place, jnp.int32(0))
    for part in range(LAST_PARTS):
        count = sorted_out[counts + part]
        for extra in range(PART_UNROLL - 1):
            sorted_out[part * room + count + extra] = jnp.int32(first_left << 10 | spare)


def part_room(shape):
    step_count, columns, slots = shape
    return -(-step_count // columns) * slots + PART_UNROLL


def sum_kernel(panels, rights, givens, saved, mode, shape, layers, operand_count, layer_at, *refs):
    packed, classes, refs = refs[0], refs[1], refs[2:]
    operands, refs = refs[:operand_count], refs[operand_count:]
    out_count = max(len(saved), 1)
    outs, refs = refs[:out_count], refs[out_count:]
    if mode == "split":
        (right, kept), (work, left, todo, sems) = refs[:2], refs[2:]
    else:
        work, left, right, todo, sems = refs
    spare = work.shape[0] - 1
    other = 1 - classes[layer_at]
    copies = []

    def plan(source, target, when=None):
        copies.append((pltpu.make_async_copy(source, target, sems.at[len(copies)]), when))

    start = 0
    for operand, size, gathered in rights:
        source = operands[operand]
        if gathered:
            source = source.at[pl.ds(other * size, size)]
        plan(source, right.at[pl.ds(start, size)])
        start += size
    start = 0
    for panel, pieces in enumerate(panels):
        for operand, size, gathered in pieces:
            source = operands[operand]
            if gathered:
                source = source.at[pl.ds(other * size, size)]
            plan(source, left.at[pl.ds(start, size)], classes[panel] >= 0)
            start += size
    start = 0
    for operand, size in givens:
        plan(operands[operand], work.at[pl.ds(start, size)])
        start += size
    for copy, when in copies:
        copy.start() if when is None else pl.when(when)(copy.start)
    if givens:
        work[spare] = jnp.zeros_like(work[spare])
    else:
        work[...] = jnp.zeros_like(work)
    kinds = [classes[panel] for panel in range(len(panels))]
    count = chosen_products(packed, kinds, len(panels), todo, shape, layers, spare)
    for copy, when in copies:
        copy.wait() if when is None else pl.when(when)(copy.wait)
    add_chosen(todo, count, left, right, work)
    if not saved:
        outs[0][...] = work[:spare].astype(outs[0].dtype)
        return
    start, copies, targets = 0, [], list(outs)
    if mode == "split":
        kept[kept.shape[0] - 1] = jnp.zeros(kept.shape[1:], kept.dtype)
        targets.insert(0, kept.at[pl.ds(0, kept.shape[0] - 1)])
    for out in targets:
        size = out.shape[0]
        copies.append(pltpu.make_async_copy(work.at[pl.ds(start, size)], out, sems.at[len(copies)]))
        start += size
    for copy in copies:
        copy.start()
    for copy in copies:
        copy.wait()


def product_sums(packed, scalars, shape, layers, panels, rights, givens, result_slots, saved, mode="whole"):
    step_count, columns, slots = shape
    rows, width = rights[0][0].shape[1:]
    operands = []

    def number(value):
        for index, known in enumerate(operands):
            if known is value:
                return index
        operands.append(value)
        return len(operands) - 1

    def spans(pieces):
        return [
            (number(value), value.shape[0] // 2 if gathered else value.shape[0], gathered)
            for value, gathered in pieces
        ]

    right_spans = spans(rights)
    panel_spans = [spans(pieces) for pieces in panels]
    given_spans = [(number(value), value.shape[0]) for value in givens]
    right_slots = sum(size for _, size, _ in right_spans)
    left_slots = len(panels) * layers * slots
    assert right_slots <= 1024 and left_slots <= 1024 and result_slots < 1024 and slots % 8 == 0
    assert all(sum(size for _, size, _ in pieces) == layers * slots for pieces in panel_spans)
    anywhere = pl.BlockSpec(memory_space=pl.ANY)
    in_scalar, in_vector = pl.BlockSpec(memory_space=pltpu.SMEM), pl.BlockSpec(memory_space=pltpu.VMEM)
    copy_count = len(rights) + sum(len(pieces) for pieces in panels) + len(givens) + len(saved) + 1
    scratch = [
        pltpu.VMEM((result_slots + 1, rows, width), jnp.float32),
        pltpu.VMEM((left_slots, rows, width), jnp.bfloat16),
        pltpu.VMEM((right_slots, width, width), jnp.bfloat16),
    ]
    if saved:
        out_shape = [jax.ShapeDtypeStruct((size, rows, width), jnp.float32) for size in saved]
    else:
        out_shape = [jax.ShapeDtypeStruct((result_slots, rows, width), jnp.bfloat16)]
    out_specs = [anywhere if saved else in_vector] * len(out_shape)
    if mode == "split":
        out_shape += [scratch.pop(), pltpu.VMEM((result_slots - sum(saved) + 1, rows, width), jnp.float32)]
        out_specs += [in_vector] * 2
    return pl.pallas_call(
        functools.partial(
            sum_kernel,
            panel_spans,
            right_spans,
            given_spans,
            saved,
            mode,
            shape,
            layers,
            len(operands),
            len(panels),
        ),
        out_shape=out_shape,
        in_specs=[in_scalar, in_scalar] + [anywhere] * len(operands),
        out_specs=out_specs,
        scratch_shapes=scratch
        + [
            pltpu.SMEM((len(panels) * -(-step_count // columns) * layers * slots + UNROLL,), jnp.int32),
            pltpu.SemaphoreType.DMA((copy_count,)),
        ],
        compiler_params=pltpu.CompilerParams(vmem_limit_bytes=(34 if mode == "split" else 56) << 20),
        cost_estimate=pl.CostEstimate(flops=1, bytes_accessed=1, transcendentals=0),
    )(packed, scalars, *operands)


def received_kernel(given, *refs):
    del given
    work, start = refs[-1], 0
    for piece in refs[:-1]:
        span = pl.ds(start, piece.shape[0])
        work[span] += piece[...]
        start += piece.shape[0]


def add_received(given, pieces):
    in_vector = pl.BlockSpec(memory_space=pltpu.VMEM)
    return pl.pallas_call(
        received_kernel,
        out_shape=pltpu.VMEM(given.shape, given.dtype),
        in_specs=[in_vector] * (1 + len(pieces)),
        out_specs=in_vector,
        input_output_aliases={0: 0},
        compiler_params=pltpu.CompilerParams(vmem_limit_bytes=12 << 20),
        cost_estimate=pl.CostEstimate(flops=1, bytes_accessed=1, transcendentals=0),
    )(given, *pieces)


def own_kernel(shape, kind_at, packed, scalars, right, given, left, work, sorted_out, todo):
    del given
    step_count, _, slots = shape
    spare, kind = work.shape[0] - 1, scalars[kind_at]
    count = chosen_products(packed, [kind], 1, todo, shape, 1, spare)
    add_chosen(todo, count, left, right, work)
    sort_products(packed, step_count * slots, kind, shape, sorted_out, spare, slots)


def add_own(packed, scalars, kind_at, shape, panel, right, given):
    step_count, columns, slots = shape
    in_scalar, in_vector = pl.BlockSpec(memory_space=pltpu.SMEM), pl.BlockSpec(memory_space=pltpu.VMEM)
    return pl.pallas_call(
        functools.partial(own_kernel, shape, kind_at),
        out_shape=[
            pltpu.VMEM(given.shape, given.dtype),
            jax.ShapeDtypeStruct((LAST_PARTS * part_room(shape) + LAST_PARTS,), jnp.int32),
        ],
        in_specs=[in_scalar] * 2 + [in_vector] * 3,
        out_specs=[in_vector, in_scalar],
        scratch_shapes=[pltpu.SMEM((-(-step_count // columns) * slots + UNROLL,), jnp.int32)],
        input_output_aliases={3: 0},
        compiler_params=pltpu.CompilerParams(vmem_limit_bytes=12 << 20),
        cost_estimate=pl.CostEstimate(flops=1, bytes_accessed=1, transcendentals=0),
    )(packed, scalars, right, given, panel)


def other_kernel(shape, sorted_lists, right, given, left, out, work, rounded, sems):
    del given
    slots, room, spare = shape[2], part_room(shape), work.shape[0] - 1
    size, copies = spare // LAST_PARTS, []
    for part in range(LAST_PARTS):
        count = sorted_lists[LAST_PARTS * room + part]
        add_chosen(sorted_lists, count, left, right, work, slots, part * room, PART_UNROLL)
        last = (part + 1) * size if part < LAST_PARTS - 1 else spare
        cuts = [part * size + (last - part * size) * piece // PIECES for piece in range(PIECES + 1)]
        for first, after in zip(cuts, cuts[1:]):
            span = pl.ds(first, after - first)
            rounded[span] = work[span].astype(rounded.dtype)
            copies.append(pltpu.make_async_copy(rounded.at[span], out.at[span], sems.at[len(copies)]))
            copies[-1].start()
    for copy in copies:
        copy.wait()


def add_other(sorted_lists, shape, panel, right, given):
    result_slots, rows, width = given.shape[0] - 1, *given.shape[1:]
    in_scalar, in_vector = pl.BlockSpec(memory_space=pltpu.SMEM), pl.BlockSpec(memory_space=pltpu.VMEM)
    return pl.pallas_call(
        functools.partial(other_kernel, shape),
        out_shape=[
            jax.ShapeDtypeStruct((result_slots, rows, width), jnp.bfloat16),
            pltpu.VMEM(given.shape, given.dtype),
        ],
        in_specs=[in_scalar] + [in_vector] * 3,
        out_specs=[pl.BlockSpec(memory_space=pl.ANY), in_vector],
        scratch_shapes=[
            pltpu.VMEM((result_slots, rows, width), jnp.bfloat16),
            pltpu.SemaphoreType.DMA((LAST_PARTS * PIECES,)),
        ],
        input_output_aliases={2: 1},
        compiler_params=pltpu.CompilerParams(vmem_limit_bytes=12 << 20),
        cost_estimate=pl.CostEstimate(flops=1, bytes_accessed=1, transcendentals=0),
    )(sorted_lists, right, given, panel)[0]


def scalar_list(*values):
    return jnp.stack([jnp.asarray(value, jnp.int32) for value in values])


def swapped(value):
    return lax.ppermute(value, "dep", [(0, 1), (1, 0)])


def paired(value):
    return lax.all_gather(value, "dep", axis=0, tiled=True)


def kept_products(both, layer, half, right_slot):
    slots = both.shape[3]
    result = both[:, :, 2] - layer * half
    wanted = (result >= 0) & (result < half)
    layers = jnp.arange(2, dtype=jnp.int32)[:, None, None]
    packed = right_slot(both[:, :, 1], layers) << 20 | (layers * slots + both[:, :, 0]) << 10 | result
    return jnp.where(wanted, packed, -1).reshape(-1)


def layer_products(step_lists, layer, half, right_slot):
    result = step_lists[:, 2]
    turned = jnp.where(result < half, result + layer * half, result - layer * half)
    packed = right_slot(step_lists[:, 1], 0) << 20 | step_lists[:, 0] << 10 | turned
    return jnp.where(result < 2 * half, packed, -1).reshape(-1)


def ring(left_blocks, right_blocks, triples, half):
    own, right_own, step_lists = left_blocks[0, 0, 0], right_blocks[0, 0, 0], triples[0, 0, 0]
    columns, layer = lax.axis_size("col"), lax.axis_index("dep")
    gathered = lax.all_gather(right_own, "row", axis=0, tiled=True)
    right_slots = gathered.shape[0]
    both = jnp.stack([step_lists, swapped(step_lists)])
    packed = kept_products(both, layer, half, lambda slot, layers: layers * right_slots + slot)
    rights = [(gathered, False), (swapped(gathered), False)]
    shape = (step_lists.shape[0], columns, own.shape[0])
    rising, falling, total = own, own, []
    panels, classes = [[(own, False), (paired(own), True)]], [0]
    reach = step_lists.shape[0] // 2
    for distance in range(1, reach + 1):
        rising = lax.ppermute(rising, "col", [(i, (i + 1) % columns) for i in range(columns)])
        falling = lax.ppermute(falling, "col", [(i, (i - 1) % columns) for i in range(columns)])
        panels += [[(value, False), (paired(value), True)] for value in (rising, falling)]
        classes += [columns - distance, distance]
        saved = [] if distance == reach else [half]
        scalars = scalar_list(*classes, layer)
        total = product_sums(packed, scalars, shape, 2, panels, rights, total, half, saved)
        panels, classes = [], []
    return total[0][None, None, None]


def line(left_blocks, right_blocks, triples, half):
    own, right_own, step_lists = left_blocks[0, 0, 0], right_blocks[0, 0, 0], triples[0, 0, 0]
    slots, part = own.shape[0], right_own.shape[0]
    columns, layer, place = lax.axis_size("col"), lax.axis_index("dep"), lax.axis_index("col")
    shape = (step_lists.shape[0], columns, slots)
    inner = (place == 1) | (place == 2)
    low = place < 2
    outward, across, beside = [(2, 3), (1, 0)], [(1, 2), (2, 1)], [(0, 1), (1, 0), (2, 3), (3, 2)]
    fence = lax.optimization_barrier

    def hop(value, pairs):
        return lax.ppermute(value, "col", pairs)

    def right_slot(slot, layers):
        return (layers * 2 + ((slot // part) ^ lax.axis_index("row"))) * part + slot % part

    beside_one, across_one, across_two = hop(own, beside), hop(own, across), hop(own, [(0, 2), (3, 1)])
    met = lax.ppermute(right_own, "row", [(0, 1), (1, 0)])
    listed = layer_products(step_lists, layer, half, right_slot)
    classes = [0, jnp.where(place % 2 == 0, 1, 3), jnp.where(inner, jnp.where(low, 1, 3), -1)]
    classes += [jnp.where(inner, 2, -1), jnp.where(inner, -1, 2)]
    scalars = scalar_list(*classes, layer, jnp.where(inner, -1, jnp.where(low, 3, 1)))

    outer_two = hop(across_one, outward)
    beside_one, across_one, met, listed, scalars = fence((beside_one, across_one, met, listed, scalars))
    right_other, met_other = swapped(right_own), swapped(met)
    both = jnp.stack([step_lists, swapped(step_lists)])
    kept = kept_products(both, layer, half, right_slot)

    across_two, right_other, met_other, kept = fence((across_two, right_other, met_other, kept))
    outer_three = hop(across_two, outward)
    panels = [[(value, False)] for value in (own, beside_one, across_one, across_two, outer_two)]
    rights = [(value, False) for value in (right_own, met, right_other, met_other)]
    saved = [half // PARTS] * (PARTS - 1) + [half - half // PARTS * (PARTS - 1)]
    *parts, right, total = product_sums(
        listed, scalars, shape, 1, panels, rights, [], 2 * half, saved, "split"
    )
    total = add_received(total, [swapped(part) for part in parts])

    outer_three, total, right = fence((outer_three, total, right))
    kind_at = len(classes) + 1
    total, sorted_lists = add_own(kept, scalars, kind_at, shape, outer_three, right, total)
    block = add_other(sorted_lists, shape, swapped(outer_three), right, total)
    return block[None, None, None]


def local(left_blocks, right_blocks, triples):
    step_count = triples.shape[3]
    row_count, columns = lax.axis_size("row"), lax.axis_size("col")
    half = (2 * step_count - 2 + row_count) // row_count * NBQ // 2
    if columns >= step_count:
        return ring(left_blocks, right_blocks, triples, half)
    assert columns == 4 and row_count == 2
    return line(left_blocks, right_blocks, triples, half)


def solution(mesh):
    return jax.shard_map(
        local,
        mesh=mesh,
        in_specs=(
            P(("grp", "row"), "col", "dep", None, None, None),
            P(("grp", "row"), "col", "dep", None, None, None),
            P(("grp", "row"), "col", "dep", None, None, None),
        ),
        out_specs=P(("grp", "row"), "col", "dep", None, None, None),
        check_vma=False,
    )
```

```python
import functools

import jax
import jax.numpy as jnp
from jax import lax
from jax.experimental import pallas as pl
from jax.experimental.pallas import tpu as pltpu
from jax.sharding import PartitionSpec as P

NBQ = 32
UNROLL = 16
PARTS = 4
LAST_PARTS = 3
PART_UNROLL = 24
PIECES = 2


def chosen_products(packed, classes, panels, todo, shape, layers, spare, first_left=0):
    step_count, columns, slots = shape
    count = jnp.int32(0)
    for panel in range(panels):
        kind = classes[panel]
        for extra in range(-(-step_count // columns)):
            step = lax.rem(kind + step_count // 2, columns) + extra * columns
            groups = jnp.where((kind >= 0) & (step < step_count), slots // 8, 0)
            for layer in range(layers):
                base = (layer * step_count + step) * slots

                def keep(group, count):
                    for lane in range(8):
                        entry = packed[base + group * 8 + lane]
                        todo[count] = entry + (panel * layers * slots << 10)
                        count += (entry >= 0).astype(jnp.int32)
                    return count

                count = lax.fori_loop(0, groups, keep, count)
    for extra in range(UNROLL - 1):
        todo[count + extra] = jnp.int32(first_left << 10 | spare)
    return count


def add_chosen(todo, count, left, right, work, first_left=0, start=0, unroll=UNROLL):
    def several(group, carry):
        entries = [todo[start + group * unroll + lane] for lane in range(unroll)]
        products = [
            jnp.dot(
                left[((entry >> 10) & 1023) - first_left],
                right[entry >> 20],
                preferred_element_type=jnp.float32,
            )
            for entry in entries
        ]
        for entry, product in zip(entries, products):
            work[entry & 1023] += product
        return carry

    lax.fori_loop(0, (count + unroll - 1) // unroll, several, jnp.int32(0))


def sort_products(packed, base, kind, shape, sorted_out, spare, first_left):
    step_count, columns, slots = shape
    room, counts, size = part_room(shape), LAST_PARTS * part_room(shape), spare // LAST_PARTS
    for part in range(LAST_PARTS):
        sorted_out[counts + part] = jnp.int32(0)
    for extra in range(-(-step_count // columns)):
        step = lax.rem(kind + step_count // 2, columns) + extra * columns
        groups = jnp.where((kind >= 0) & (step < step_count), slots // 8, 0)
        first = base + step * slots

        def place(group, carry):
            for lane in range(8):
                entry = packed[first + group * 8 + lane]
                result, part = entry & 1023, jnp.int32(0)
                for bound in range(1, LAST_PARTS):
                    part += (result >= bound * size).astype(jnp.int32)
                count = sorted_out[counts + part]
                sorted_out[part * room + count] = entry
                sorted_out[counts + part] = count + (entry >= 0).astype(jnp.int32)
            return carry

        lax.fori_loop(0, groups, place, jnp.int32(0))
    for part in range(LAST_PARTS):
        count = sorted_out[counts + part]
        for extra in range(PART_UNROLL - 1):
            sorted_out[part * room + count + extra] = jnp.int32(first_left << 10 | spare)


def part_room(shape):
    step_count, columns, slots = shape
    return -(-step_count // columns) * slots + PART_UNROLL


def sum_kernel(panels, rights, givens, saved, mode, shape, layers, operand_count, layer_at, *refs):
    packed, classes, refs = refs[0], refs[1], refs[2:]
    operands, refs = refs[:operand_count], refs[operand_count:]
    out_count = max(len(saved), 1)
    outs, refs = refs[:out_count], refs[out_count:]
    if mode == "split":
        (right, kept), (work, left, todo, sems) = refs[:2], refs[2:]
    else:
        work, left, right, todo, sems = refs
    spare = work.shape[0] - 1
    other = 1 - classes[layer_at]
    copies = []

    def plan(source, target, when=None):
        copies.append((pltpu.make_async_copy(source, target, sems.at[len(copies)]), when))

    start = 0
    for operand, size, gathered in rights:
        source = operands[operand]
        if gathered:
            source = source.at[pl.ds(other * size, size)]
        plan(source, right.at[pl.ds(start, size)])
        start += size
    start = 0
    for panel, pieces in enumerate(panels):
        for operand, size, gathered in pieces:
            source = operands[operand]
            if gathered:
                source = source.at[pl.ds(other * size, size)]
            plan(source, left.at[pl.ds(start, size)], classes[panel] >= 0)
            start += size
    start = 0
    for operand, size in givens:
        plan(operands[operand], work.at[pl.ds(start, size)])
        start += size
    for copy, when in copies:
        copy.start() if when is None else pl.when(when)(copy.start)
    if givens:
        work[spare] = jnp.zeros_like(work[spare])
    else:
        work[...] = jnp.zeros_like(work)
    kinds = [classes[panel] for panel in range(len(panels))]
    count = chosen_products(packed, kinds, len(panels), todo, shape, layers, spare)
    for copy, when in copies:
        copy.wait() if when is None else pl.when(when)(copy.wait)
    add_chosen(todo, count, left, right, work)
    if not saved:
        outs[0][...] = work[:spare].astype(outs[0].dtype)
        return
    start, copies, targets = 0, [], list(outs)
    if mode == "split":
        kept[kept.shape[0] - 1] = jnp.zeros(kept.shape[1:], kept.dtype)
        targets.insert(0, kept.at[pl.ds(0, kept.shape[0] - 1)])
    for out in targets:
        size = out.shape[0]
        copies.append(pltpu.make_async_copy(work.at[pl.ds(start, size)], out, sems.at[len(copies)]))
        start += size
    for copy in copies:
        copy.start()
    for copy in copies:
        copy.wait()


def product_sums(packed, scalars, shape, layers, panels, rights, givens, result_slots, saved, mode="whole"):
    step_count, columns, slots = shape
    rows, width = rights[0][0].shape[1:]
    operands = []

    def number(value):
        for index, known in enumerate(operands):
            if known is value:
                return index
        operands.append(value)
        return len(operands) - 1

    def spans(pieces):
        return [
            (number(value), value.shape[0] // 2 if gathered else value.shape[0], gathered)
            for value, gathered in pieces
        ]

    right_spans = spans(rights)
    panel_spans = [spans(pieces) for pieces in panels]
    given_spans = [(number(value), value.shape[0]) for value in givens]
    right_slots = sum(size for _, size, _ in right_spans)
    left_slots = len(panels) * layers * slots
    assert right_slots <= 1024 and left_slots <= 1024 and result_slots < 1024 and slots % 8 == 0
    assert all(sum(size for _, size, _ in pieces) == layers * slots for pieces in panel_spans)
    anywhere = pl.BlockSpec(memory_space=pl.ANY)
    in_scalar, in_vector = pl.BlockSpec(memory_space=pltpu.SMEM), pl.BlockSpec(memory_space=pltpu.VMEM)
    copy_count = len(rights) + sum(len(pieces) for pieces in panels) + len(givens) + len(saved) + 1
    scratch = [
        pltpu.VMEM((result_slots + 1, rows, width), jnp.float32),
        pltpu.VMEM((left_slots, rows, width), jnp.bfloat16),
        pltpu.VMEM((right_slots, width, width), jnp.bfloat16),
    ]
    if saved:
        out_shape = [jax.ShapeDtypeStruct((size, rows, width), jnp.float32) for size in saved]
    else:
        out_shape = [jax.ShapeDtypeStruct((result_slots, rows, width), jnp.bfloat16)]
    out_specs = [anywhere if saved else in_vector] * len(out_shape)
    if mode == "split":
        out_shape += [scratch.pop(), pltpu.VMEM((result_slots - sum(saved) + 1, rows, width), jnp.float32)]
        out_specs += [in_vector] * 2
    return pl.pallas_call(
        functools.partial(
            sum_kernel,
            panel_spans,
            right_spans,
            given_spans,
            saved,
            mode,
            shape,
            layers,
            len(operands),
            len(panels),
        ),
        out_shape=out_shape,
        in_specs=[in_scalar, in_scalar] + [anywhere] * len(operands),
        out_specs=out_specs,
        scratch_shapes=scratch
        + [
            pltpu.SMEM((len(panels) * -(-step_count // columns) * layers * slots + UNROLL,), jnp.int32),
            pltpu.SemaphoreType.DMA((copy_count,)),
        ],
        compiler_params=pltpu.CompilerParams(vmem_limit_bytes=(34 if mode == "split" else 56) << 20),
        cost_estimate=pl.CostEstimate(flops=1, bytes_accessed=1, transcendentals=0),
    )(packed, scalars, *operands)


def received_kernel(given, *refs):
    del given
    work, start = refs[-1], 0
    for piece in refs[:-1]:
        span = pl.ds(start, piece.shape[0])
        work[span] += piece[...]
        start += piece.shape[0]


def add_received(given, pieces):
    in_vector = pl.BlockSpec(memory_space=pltpu.VMEM)
    return pl.pallas_call(
        received_kernel,
        out_shape=pltpu.VMEM(given.shape, given.dtype),
        in_specs=[in_vector] * (1 + len(pieces)),
        out_specs=in_vector,
        input_output_aliases={0: 0},
        compiler_params=pltpu.CompilerParams(vmem_limit_bytes=12 << 20),
        cost_estimate=pl.CostEstimate(flops=1, bytes_accessed=1, transcendentals=0),
    )(given, *pieces)


def own_kernel(shape, kind_at, packed, scalars, right, given, left, work, sorted_out, todo):
    del given
    step_count, _, slots = shape
    spare, kind = work.shape[0] - 1, scalars[kind_at]
    count = chosen_products(packed, [kind], 1, todo, shape, 1, spare)
    add_chosen(todo, count, left, right, work)
    sort_products(packed, step_count * slots, kind, shape, sorted_out, spare, slots)


def add_own(packed, scalars, kind_at, shape, panel, right, given):
    step_count, columns, slots = shape
    in_scalar, in_vector = pl.BlockSpec(memory_space=pltpu.SMEM), pl.BlockSpec(memory_space=pltpu.VMEM)
    return pl.pallas_call(
        functools.partial(own_kernel, shape, kind_at),
        out_shape=[
            pltpu.VMEM(given.shape, given.dtype),
            jax.ShapeDtypeStruct((LAST_PARTS * part_room(shape) + LAST_PARTS,), jnp.int32),
        ],
        in_specs=[in_scalar] * 2 + [in_vector] * 3,
        out_specs=[in_vector, in_scalar],
        scratch_shapes=[pltpu.SMEM((-(-step_count // columns) * slots + UNROLL,), jnp.int32)],
        input_output_aliases={3: 0},
        compiler_params=pltpu.CompilerParams(vmem_limit_bytes=12 << 20),
        cost_estimate=pl.CostEstimate(flops=1, bytes_accessed=1, transcendentals=0),
    )(packed, scalars, right, given, panel)


def other_kernel(shape, sorted_lists, right, given, left, out, work, rounded, sems):
    del given
    slots, room, spare = shape[2], part_room(shape), work.shape[0] - 1
    size, copies = spare // LAST_PARTS, []
    for part in range(LAST_PARTS):
        count = sorted_lists[LAST_PARTS * room + part]
        add_chosen(sorted_lists, count, left, right, work, slots, part * room, PART_UNROLL)
        last = (part + 1) * size if part < LAST_PARTS - 1 else spare
        cuts = [part * size + (last - part * size) * piece // PIECES for piece in range(PIECES + 1)]
        for first, after in zip(cuts, cuts[1:]):
            span = pl.ds(first, after - first)
            rounded[span] = work[span].astype(rounded.dtype)
            copies.append(pltpu.make_async_copy(rounded.at[span], out.at[span], sems.at[len(copies)]))
            copies[-1].start()
    for copy in copies:
        copy.wait()


def add_other(sorted_lists, shape, panel, right, given):
    result_slots, rows, width = given.shape[0] - 1, *given.shape[1:]
    in_scalar, in_vector = pl.BlockSpec(memory_space=pltpu.SMEM), pl.BlockSpec(memory_space=pltpu.VMEM)
    return pl.pallas_call(
        functools.partial(other_kernel, shape),
        out_shape=[
            jax.ShapeDtypeStruct((result_slots, rows, width), jnp.bfloat16),
            pltpu.VMEM(given.shape, given.dtype),
        ],
        in_specs=[in_scalar] + [in_vector] * 3,
        out_specs=[pl.BlockSpec(memory_space=pl.ANY), in_vector],
        scratch_shapes=[
            pltpu.VMEM((result_slots, rows, width), jnp.bfloat16),
            pltpu.SemaphoreType.DMA((LAST_PARTS * PIECES,)),
        ],
        input_output_aliases={2: 1},
        compiler_params=pltpu.CompilerParams(vmem_limit_bytes=12 << 20),
        cost_estimate=pl.CostEstimate(flops=1, bytes_accessed=1, transcendentals=0),
    )(sorted_lists, right, given, panel)[0]


def scalar_list(*values):
    return jnp.stack([jnp.asarray(value, jnp.int32) for value in values])


def swapped(value):
    return lax.ppermute(value, "dep", [(0, 1), (1, 0)])


def paired(value):
    return lax.all_gather(value, "dep", axis=0, tiled=True)


def kept_products(both, layer, half, right_slot):
    slots = both.shape[3]
    result = both[:, :, 2] - layer * half
    wanted = (result >= 0) & (result < half)
    layers = jnp.arange(2, dtype=jnp.int32)[:, None, None]
    packed = right_slot(both[:, :, 1], layers) << 20 | (layers * slots + both[:, :, 0]) << 10 | result
    return jnp.where(wanted, packed, -1).reshape(-1)


def layer_products(step_lists, layer, half, right_slot):
    result = step_lists[:, 2]
    turned = jnp.where(result < half, result + layer * half, result - layer * half)
    packed = right_slot(step_lists[:, 1], 0) << 20 | step_lists[:, 0] << 10 | turned
    return jnp.where(result < 2 * half, packed, -1).reshape(-1)


def ring(left_blocks, right_blocks, triples, half):
    own, right_own, step_lists = left_blocks[0, 0, 0], right_blocks[0, 0, 0], triples[0, 0, 0]
    columns, layer = lax.axis_size("col"), lax.axis_index("dep")
    gathered = lax.all_gather(right_own, "row", axis=0, tiled=True)
    right_slots = gathered.shape[0]
    both = jnp.stack([step_lists, swapped(step_lists)])
    packed = kept_products(both, layer, half, lambda slot, layers: layers * right_slots + slot)
    rights = [(gathered, False), (swapped(gathered), False)]
    shape = (step_lists.shape[0], columns, own.shape[0])
    rising, falling, total = own, own, []
    panels, classes = [[(own, False), (paired(own), True)]], [0]
    reach = step_lists.shape[0] // 2
    for distance in range(1, reach + 1):
        rising = lax.ppermute(rising, "col", [(i, (i + 1) % columns) for i in range(columns)])
        falling = lax.ppermute(falling, "col", [(i, (i - 1) % columns) for i in range(columns)])
        panels += [[(value, False), (paired(value), True)] for value in (rising, falling)]
        classes += [columns - distance, distance]
        saved = [] if distance == reach else [half]
        scalars = scalar_list(*classes, layer)
        total = product_sums(packed, scalars, shape, 2, panels, rights, total, half, saved)
        panels, classes = [], []
    return total[0][None, None, None]


def line(left_blocks, right_blocks, triples, half):
    own, right_own, step_lists = left_blocks[0, 0, 0], right_blocks[0, 0, 0], triples[0, 0, 0]
    slots, part = own.shape[0], right_own.shape[0]
    columns, layer, place = lax.axis_size("col"), lax.axis_index("dep"), lax.axis_index("col")
    shape = (step_lists.shape[0], columns, slots)
    inner = (place == 1) | (place == 2)
    low = place < 2
    outward, across, beside = [(2, 3), (1, 0)], [(1, 2), (2, 1)], [(0, 1), (1, 0), (2, 3), (3, 2)]
    fence = lax.optimization_barrier

    def hop(value, pairs):
        return lax.ppermute(value, "col", pairs)

    def right_slot(slot, layers):
        return (layers * 2 + ((slot // part) ^ lax.axis_index("row"))) * part + slot % part

    beside_one, across_one, across_two = hop(own, beside), hop(own, across), hop(own, [(0, 2), (3, 1)])
    met = lax.ppermute(right_own, "row", [(0, 1), (1, 0)])
    listed = layer_products(step_lists, layer, half, right_slot)
    classes = [0, jnp.where(place % 2 == 0, 1, 3), jnp.where(inner, jnp.where(low, 1, 3), -1)]
    classes += [jnp.where(inner, 2, -1), jnp.where(inner, -1, 2)]
    scalars = scalar_list(*classes, layer, jnp.where(inner, -1, jnp.where(low, 3, 1)))

    outer_two = hop(across_one, outward)
    beside_one, across_one, met, listed, scalars = fence((beside_one, across_one, met, listed, scalars))
    right_other, met_other = swapped(right_own), swapped(met)
    both = jnp.stack([step_lists, swapped(step_lists)])
    kept = kept_products(both, layer, half, right_slot)

    across_two, right_other, met_other, kept = fence((across_two, right_other, met_other, kept))
    outer_three = hop(across_two, outward)
    panels = [[(value, False)] for value in (own, beside_one, across_one, across_two, outer_two)]
    rights = [(value, False) for value in (right_own, met, right_other, met_other)]
    saved = [half // PARTS] * (PARTS - 1) + [half - half // PARTS * (PARTS - 1)]
    *parts, right, total = product_sums(
        listed, scalars, shape, 1, panels, rights, [], 2 * half, saved, "split"
    )
    total = add_received(total, [swapped(part) for part in parts])

    outer_three, total, right = fence((outer_three, total, right))
    kind_at = len(classes) + 1
    total, sorted_lists = add_own(kept, scalars, kind_at, shape, outer_three, right, total)
    block = add_other(sorted_lists, shape, swapped(outer_three), right, total)
    return block[None, None, None]


def local(left_blocks, right_blocks, triples):
    step_count = triples.shape[3]
    row_count, columns = lax.axis_size("row"), lax.axis_size("col")
    half = (2 * step_count - 2 + row_count) // row_count * NBQ // 2
    if columns >= step_count:
        return ring(left_blocks, right_blocks, triples, half)
    assert columns == 4 and row_count == 2
    return line(left_blocks, right_blocks, triples, half)


def solution(mesh):
    return jax.shard_map(
        local,
        mesh=mesh,
        in_specs=(
            P(("grp", "row"), "col", "dep", None, None, None),
            P(("grp", "row"), "col", "dep", None, None, None),
            P(("grp", "row"), "col", "dep", None, None, None),
        ),
        out_specs=P(("grp", "row"), "col", "dep", None, None, None),
        check_vma=False,
    )
```
